256 devices in a mesh: row: 8 (over z), col: 16 (over x, y), tm: 2 (over core).
Axes of the slice: x: 4, y: 4, z: 8, core: 2. Of those that a mesh axis runs over, the one named last changes fastest.
Arguments:
- records: bfloat16 [2, 32768, 7680], P('tm', ('row', 'col')), may hold values from -6 to 6
- taper: float32 [1200], replicated, may hold values from 0.25 to 1
- pairs: int32 [128, 4], P(('row', 'col')), may hold values from -1 to 127, as said below
Outputs:
- correlations: float32 [128, 4, 256, 256], P(('row', 'col'), None, 'tm')
The draws below stay inside these ranges and needn't reach their ends.
Inputs may be any that keep to these rules, and one draw needn't show every extreme that they name: `pairs`: each entry of row a is a + o with 1 <= o <= 7, or -1 exactly where a + o would pass the last block; the entries of a row are distinct offsets.
All inputs are finite; a program needn't handle non-finite values.
Results may differ from the reference program's by a relative error of at most 0.0053.
Values may be sent and summed in bfloat16 or wider, within the bound.
No kernel may reach another device: no remote copies, remote signals or barrier semaphores. Data moves between devices by JAX's collectives and lax.ppermute only.
A program may use at most 128 MiB of HBM per device.

```python
import math
import jax
import jax.numpy as jnp
from jax import lax

BLOCK = 256
SAMPLES = 7680
FREQS = 1200
FIRST_BIN = 32
LAGS = 256
SMOOTH = 4
PARTNERS = 4
REACH = 7
WINDOWS = 2
BLOCKS = 128
CHANNELS = 32768


def draw_pairs(key, part):
    key = jax.random.fold_in(key, 11)
    row_keys = jax.random.split(key, BLOCKS)

    def choose(row_key):
        return jax.random.permutation(row_key, REACH)[:PARTNERS]
    offsets = jax.vmap(choose)(row_keys).astype(jnp.int32) + 1
    partner = jnp.arange(BLOCKS, dtype=jnp.int32)[:, None] + offsets
    return jnp.where(partner < BLOCKS, partner, -1).astype(jnp.int32)


def shard_levels(rng, extent, pieces, low, high):
    level = 1.0
    for position, shards_of in pieces:
        draws = jax.random.uniform(jax.random.fold_in(jax.random.fold_in(rng, 6), position), (shards_of,), jnp.float32, low / len(pieces), high / len(pieces))
        level = level * jnp.repeat(jnp.exp(draws), extent[position] // shards_of).reshape((-1,) + (1,) * (len(extent) - 1 - position))
    return level


def bell_draw(own_key, dims, deviation, reach, shards=(), held_as=jnp.bfloat16):
    array = deviation * jax.random.normal(own_key, dims, jnp.float32)
    if shards:
        array = array * shard_levels(own_key, dims, shards, -0.22, 0.18)
    return jnp.clip(array, -reach, reach).astype(held_as)


def setup_inputs(seed: int = 0) -> dict:
    streams_of = jax.random.split(jax.random.key(seed), 4)
    records = bell_draw(streams_of[0], (WINDOWS, CHANNELS, SAMPLES), 1.0, 6.0, ((0, 2), (1, 128)))
    taper = jnp.clip(jnp.exp(jax.random.uniform(streams_of[1], (FREQS,), jnp.float32, math.log(0.25), math.log(1.0))), 0.25, 1.0)
    pairs = draw_pairs(jax.random.fold_in(streams_of[3], 71), 0)
    return {"records": records, "taper": taper, "pairs": pairs}


WATER = 0.3
RESCALE = 2.0

def dft_table(start, block_len, freqs):
    samples = start + jnp.arange(block_len, dtype=jnp.int32)
    phase = samples[:, None] * freqs[None, :] % SAMPLES
    angle = phase.astype(jnp.float32) * (2.0 * math.pi / SAMPLES)
    return jnp.concatenate([jnp.cos(angle), -jnp.sin(angle)], axis=1).astype(jnp.bfloat16)

def spectra(series):
    block_len = math.gcd(SAMPLES, 512)
    freqs = FIRST_BIN + jnp.arange(FREQS, dtype=jnp.int32)

    def advance(total, start):
        piece = lax.dynamic_slice_in_dim(series, start, block_len, 1)
        return (total + jnp.dot(piece, dft_table(start, block_len, freqs), preferred_element_type=jnp.float32), None)
    starts = jnp.arange(SAMPLES // block_len, dtype=jnp.int32) * block_len
    total, unused = lax.scan(advance, jnp.zeros((series.shape[0], 2 * FREQS), jnp.float32), starts)
    return total

def whiten(spectrum, taper):
    real_part = spectrum[:, :FREQS]
    imag_part = spectrum[:, FREQS:]
    amplitude = jnp.sqrt(real_part * real_part + imag_part * imag_part)
    padded = jnp.pad(amplitude, ((0, 0), (SMOOTH, SMOOTH)))
    smoothed = padded[:, 0:FREQS]
    for offset in range(1, 2 * SMOOTH + 1):
        smoothed = smoothed + padded[:, offset:offset + FREQS]
    smoothed = smoothed / (2 * SMOOTH + 1)
    water_level = lax.optimization_barrier(jnp.mean(amplitude, axis=1, keepdims=True))
    scaling = taper[None, :] / (smoothed + WATER * water_level + 1e-05)
    return jnp.concatenate([real_part * scaling, imag_part * scaling], axis=1).astype(jnp.bfloat16)

def lag_table():
    freqs = FIRST_BIN + jnp.arange(FREQS, dtype=jnp.int32)
    lag_steps = jnp.arange(LAGS, dtype=jnp.int32) - LAGS // 2 + SAMPLES
    phase = freqs[:, None] * lag_steps[None, :] % SAMPLES
    angle = phase.astype(jnp.float32) * (2.0 * math.pi / SAMPLES)
    return jnp.concatenate([jnp.cos(angle), -jnp.sin(angle)], axis=0)

def cross_spectrum(first, second):
    first = first.astype(jnp.float32)
    second = second.astype(jnp.float32)
    first_re = first[..., :FREQS]
    first_im = first[..., FREQS:]
    second_re = second[..., :FREQS]
    second_im = second[..., FREQS:]
    return jnp.concatenate([first_re * second_re + first_im * second_im, first_im * second_re - first_re * second_im], axis=-1)

def reference(records, taper, pairs):
    spectrum = spectra(records.reshape(-1, SAMPLES))
    white = whiten(spectrum, taper).reshape(WINDOWS, BLOCKS, BLOCK, 2 * FREQS)
    table = lag_table()
    factor = RESCALE / math.sqrt(FREQS * WINDOWS)

    def one_block(inputs):
        first_block, partner_list = inputs
        first = white[:, first_block]
        safe_list = jnp.maximum(partner_list, 0)
        second = white[:, safe_list]
        spec_sum = lax.optimization_barrier(jnp.sum(cross_spectrum(first[:, None], second), axis=0))
        lagged = jnp.dot(spec_sum.reshape(-1, 2 * FREQS), table, precision=lax.Precision.HIGHEST, preferred_element_type=jnp.float32)
        lagged = lagged.reshape(PARTNERS, BLOCK, LAGS) * factor
        return jnp.where(partner_list[:, None, None] >= 0, lagged, jnp.zeros_like(lagged))
    return lax.map(one_block, (jnp.arange(BLOCKS, dtype=jnp.int32), pairs))
```

```python
import math

import jax
import jax.numpy as jnp
import ml_dtypes
import numpy as np
from jax import lax
from jax.experimental import pallas as pl
from jax.experimental.pallas import tpu as pltpu
from jax.sharding import PartitionSpec as P

SAMPLES = 7680
FREQS = 1200
FIRST_BIN = 32
LAGS = 256
SMOOTH = 4
PARTNERS = 4
REACH = 7
BLOCK = 256
WINDOWS = 2
WATER = 0.3
RESCALE = 2.0

QUARTER = SAMPLES // 4
HALF = BLOCK // 2
PER = FREQS // 4
BODY = 256
TAIL = PER - BODY
COLS = 2 * BODY + 128
WIDE = 4 * COLS
RESIDUES = (0, 2, 1, 3)
PLANE = 16
MINE = BLOCK // (2 * PLANE)
VMEM = 56 * 1024 * 1024


def spread(cos, sin):
    out = np.zeros(cos.shape[:-1] + (COLS,), np.float64)
    out[..., :BODY] = cos[..., :BODY]
    out[..., BODY : 2 * BODY] = sin[..., :BODY]
    out[..., 2 * BODY : 2 * BODY + TAIL] = cos[..., BODY:]
    out[..., 2 * BODY + 64 : 2 * BODY + 64 + TAIL] = sin[..., BODY:]
    return out


def residue_bins(residue):
    return FIRST_BIN + 4 * np.arange(PER) + residue


def dft_table():
    samples = np.arange(QUARTER)
    blocks = []
    for residue in RESIDUES:
        angle = (samples[:, None] * residue_bins(residue)[None, :] % SAMPLES) * (
            2.0 * math.pi / SAMPLES
        )
        blocks.append(spread(np.cos(angle), -np.sin(angle)))
    return np.stack(blocks).astype(np.float32).astype(ml_dtypes.bfloat16)


def lag_tables():
    lag_steps = np.arange(LAGS) - LAGS // 2 + SAMPLES
    factor = RESCALE / math.sqrt(FREQS * WINDOWS)
    blocks = []
    for residue in RESIDUES:
        angle = (lag_steps[:, None] * residue_bins(residue)[None, :] % SAMPLES) * (
            2.0 * math.pi / SAMPLES
        )
        blocks.append(spread(np.cos(angle), -np.sin(angle)).T)
    table = (np.concatenate(blocks) * factor).astype(np.float32)
    high = table.astype(ml_dtypes.bfloat16)
    low = (table - high.astype(np.float32)).astype(ml_dtypes.bfloat16)
    return high, low


def spread_taper(taper):
    parts = taper.reshape(PER, 4).T
    tail = jnp.pad(parts[:, BODY:], ((0, 0), (0, 64 - TAIL)))
    parts = jnp.concatenate([parts[:, :BODY], tail, tail], axis=1)
    return jnp.stack([parts[residue] for residue in RESIDUES])


def dft_kernel(x_ref, taper_ref, table_ref, mine_ref, theirs_ref, y_ref, s_ref):
    step = pl.program_id(0)
    core = lax.axis_index("tm")

    @pl.when(step == 0)
    def split():
        def rows(i, carry):
            at = pl.ds(pl.multiple_of(i * 16, 16), 16)
            x = [
                x_ref[at, n * QUARTER : (n + 1) * QUARTER].astype(jnp.float32) for n in range(4)
            ]
            even, odd = x[0] + x[2], x[1] + x[3]
            parts = (even + odd, even - odd, x[0] - x[2], x[1] - x[3])
            for n, part in enumerate(parts):
                y_ref[pl.ds(pl.multiple_of(n * BLOCK + i * 16, 16), 16), :] = part.astype(
                    jnp.bfloat16
                )
            return carry

        lax.fori_loop(0, BLOCK // 16, rows, 0)

    @pl.when(step < 2)
    def real_sums():
        at = pl.ds(pl.multiple_of(step * BLOCK, BLOCK), BLOCK)
        s_ref[at, :] = jnp.dot(y_ref[at, :], table_ref[0], preferred_element_type=jnp.float32)

    @pl.when(step >= 2)
    def complex_sums():
        at = pl.ds(pl.multiple_of((step - 1) * 2 * BLOCK, BLOCK), 2 * BLOCK)
        s_ref[at, :] = jnp.dot(
            y_ref[2 * BLOCK :, :], table_ref[0], preferred_element_type=jnp.float32
        )

    @pl.when(step == 3)
    def whiten():
        lane = lax.broadcasted_iota(jnp.int32, (16, 128), 1)
        low = lane < 64
        sign = jnp.where(low, 1.0, -1.0)

        def rows(i, first, out_ref):
            row = first + i * 16

            def load(base):
                block = s_ref[pl.ds(pl.multiple_of(base * BLOCK + row, 16), 16), :]
                return block[:, :BODY], block[:, BODY : 2 * BODY], block[:, 2 * BODY :]

            spectrum = [load(0), load(1)]
            for base, way in ((2, 1.0), (4, -1.0)):
                u_cos, u_sin, u_tail = load(base)
                v_cos, v_sin, v_tail = load(base + 1)
                spectrum.append(
                    (
                        u_cos + way * v_sin,
                        u_sin - way * v_cos,
                        u_tail + way * sign * pltpu.roll(v_tail, 64, 1),
                    )
                )
            amplitude = [None] * 4
            for residue, (re, im, tail) in zip(RESIDUES, spectrum):
                square = tail * tail
                square = jnp.where(low, square + pltpu.roll(square, 64, 1), 0.0)
                amplitude[residue] = jnp.concatenate(
                    [jnp.sqrt(re * re + im * im), jnp.sqrt(square)], axis=1
                )
            total = (amplitude[0] + amplitude[1]) + (amplitude[2] + amplitude[3])
            floor = WATER * jnp.sum(total, axis=1, keepdims=True) / FREQS + 1e-05
            before = [pltpu.roll(a, 1, 1) for a in amplitude]
            after = [pltpu.roll(a, BODY + 128 - 1, 1) for a in amplitude]
            for place, (residue, (re, im, tail)) in enumerate(zip(RESIDUES, spectrum)):
                smoothed = total + before[residue] + after[residue]
                for other in range(4):
                    if other > residue:
                        smoothed = smoothed + before[other]
                    if other < residue:
                        smoothed = smoothed + after[other]
                scale = taper_ref[place : place + 1, :] / (smoothed / (2 * SMOOTH + 1) + floor)
                last = scale[:, BODY:]
                last = jnp.where(low, last, pltpu.roll(last, 64, 1))
                white = jnp.concatenate([re * scale[:, :BODY], im * scale[:, :BODY], tail * last], 1)
                out_ref[
                    pl.ds(pl.multiple_of(i * 16, 16), 16), place * COLS : (place + 1) * COLS
                ] = white.astype(jnp.bfloat16)

        def theirs(i, carry):
            rows(i, (1 - core) * HALF, theirs_ref)
            return carry

        def mine(i, carry):
            rows(i, core * HALF, mine_ref)
            return carry

        lax.fori_loop(0, HALF // 16, theirs, 0)
        lax.fori_loop(0, HALF // 16, mine, 0)


def whitened(series, taper):
    half = jax.ShapeDtypeStruct((HALF, WIDE), jnp.bfloat16)
    table = jnp.asarray(dft_table())
    return pl.pallas_call(
        dft_kernel,
        grid=(4,),
        in_specs=[
            pl.BlockSpec((BLOCK, SAMPLES), lambda i: (0, 0)),
            pl.BlockSpec((4, BODY + 128), lambda i: (0, 0)),
            pl.BlockSpec((1, QUARTER, COLS), lambda i: (i, 0, 0)),
        ],
        out_specs=[pl.BlockSpec((HALF, WIDE), lambda i: (0, 0))] * 2,
        out_shape=[half, half],
        scratch_shapes=[
            pltpu.VMEM((4 * BLOCK, QUARTER), jnp.bfloat16),
            pltpu.VMEM((6 * BLOCK, COLS), jnp.float32),
        ],
        compiler_params=pltpu.CompilerParams(vmem_limit_bytes=VMEM),
        name="dft_whiten",
    )(series, spread_taper(taper), table)


def corr_kernel(pairs_ref, plane_ref, halo_ref, high_ref, low_ref, out_ref, w_ref, xh_ref, xl_ref, sems):
    base = lax.axis_index("row") * PLANE
    copies = [
        pltpu.make_async_copy(plane_ref, w_ref.at[:PLANE], sems.at[0]),
        pltpu.make_async_copy(halo_ref, w_ref.at[PLANE:], sems.at[1]),
    ]
    for copy in copies:
        copy.start()
    for copy in copies:
        copy.wait()
    lane = lax.broadcasted_iota(jnp.int32, (MINE, 128), 1)
    low = lane < 64

    def one_block(a, carry):
        first = w_ref[a].astype(jnp.float32)
        for slot in range(0, PARTNERS, 2):
            at = pl.ds(pl.multiple_of((a * PARTNERS + slot) * MINE, 16), 2 * MINE)
            seconds = []
            for k in (slot, slot + 1):
                index = jnp.clip(pairs_ref[a * PARTNERS + k] - base, 0, PLANE + REACH - 1)
                seconds.append(w_ref[index].astype(jnp.float32))
            for place in range(4):
                here = place * COLS
                pieces = []
                for second in seconds:
                    re, im = 0.0, 0.0
                    straight, crossed = 0.0, 0.0
                    for w in range(WINDOWS):
                        rows = slice(w * MINE, (w + 1) * MINE)
                        a_re = first[rows, here : here + BODY]
                        a_im = first[rows, here + BODY : here + 2 * BODY]
                        a_tail = first[rows, here + 2 * BODY : here + COLS]
                        b_re = second[rows, here : here + BODY]
                        b_im = second[rows, here + BODY : here + 2 * BODY]
                        b_tail = second[rows, here + 2 * BODY : here + COLS]
                        re = re + a_re * b_re + a_im * b_im
                        im = im + a_im * b_re - a_re * b_im
                        straight = straight + a_tail * b_tail
                        crossed = crossed + a_tail * pltpu.roll(b_tail, 64, 1)
                    tail = jnp.where(
                        low,
                        straight + pltpu.roll(straight, 64, 1),
                        crossed - pltpu.roll(crossed, 64, 1),
                    )
                    pieces.append(jnp.concatenate([re, im, tail], axis=1))
                cross = jnp.concatenate(pieces, axis=0)
                high = cross.astype(jnp.bfloat16)
                xh_ref[at, here : here + COLS] = high
                xl_ref[at, here : here + COLS] = (cross - high.astype(jnp.float32)).astype(
                    jnp.bfloat16
                )
        return carry

    lax.fori_loop(0, PLANE, one_block, 0)
    lagged = jnp.dot(xh_ref[...], high_ref[...], preferred_element_type=jnp.float32)
    lagged += jnp.dot(xh_ref[...], low_ref[...], preferred_element_type=jnp.float32)
    lagged += jnp.dot(xl_ref[...], high_ref[...], preferred_element_type=jnp.float32)
    out_ref[...] = lagged.reshape(out_ref.shape)

    def mask(i, carry):
        @pl.when(pairs_ref[i] < 0)
        def clear():
            out_ref[i] = jnp.zeros((MINE, LAGS), jnp.float32)

        return carry

    lax.fori_loop(0, PLANE * PARTNERS, mask, 0)


def correlated(pairs, plane, halo):
    high, low = lag_tables()
    rows = PLANE * PARTNERS * MINE
    vmem = pl.BlockSpec(memory_space=pltpu.VMEM)
    return pl.pallas_call(
        corr_kernel,
        in_specs=[
            pl.BlockSpec(memory_space=pltpu.SMEM),
            pl.BlockSpec(memory_space=pl.ANY),
            pl.BlockSpec(memory_space=pl.ANY),
            vmem,
            vmem,
        ],
        out_specs=vmem,
        out_shape=jax.ShapeDtypeStruct((PLANE * PARTNERS, MINE, LAGS), jnp.float32),
        scratch_shapes=[
            pltpu.VMEM((PLANE + REACH, 2 * MINE, WIDE), jnp.bfloat16),
            pltpu.VMEM((rows, WIDE), jnp.bfloat16),
            pltpu.VMEM((rows, WIDE), jnp.bfloat16),
            pltpu.SemaphoreType.DMA((2,)),
        ],
        compiler_params=pltpu.CompilerParams(vmem_limit_bytes=VMEM),
        name="correlate",
    )(pairs, plane, halo, jnp.asarray(high), jnp.asarray(low))


def per_device(records, taper, pairs):
    plane_pairs = lax.all_gather(pairs.reshape(-1), "col", axis=0, tiled=True)
    mine, theirs = whitened(records[0], taper)
    got = lax.ppermute(theirs, "tm", [(0, 1), (1, 0)])
    send = jnp.concatenate(
        [mine.reshape(PLANE, MINE, WIDE), got.reshape(PLANE, MINE, WIDE)], axis=1
    )
    plane = lax.all_to_all(send, "col", 0, 0, tiled=True)
    count = lax.axis_size("row")
    halo = lax.ppermute(plane[:REACH], "row", [(z, z - 1) for z in range(1, count)])
    lagged = correlated(plane_pairs, plane, halo)
    lagged = lagged.reshape(PLANE, PARTNERS, MINE, LAGS)
    back = lax.all_to_all(lagged, "col", 0, 0, tiled=True)
    return back.transpose(1, 0, 2, 3).reshape(1, PARTNERS, HALF, LAGS)


def solution(mesh):
    return jax.shard_map(
        per_device,
        mesh=mesh,
        in_specs=(P("tm", ("row", "col"), None), P(), P(("row", "col"), None)),
        out_specs=P(("row", "col"), None, "tm", None),
        check_vma=False,
    )
```

```python
import math

import jax
import jax.numpy as jnp
import ml_dtypes
import numpy as np
from jax import lax
from jax.experimental import pallas as pl
from jax.experimental.pallas import tpu as pltpu
from jax.sharding import PartitionSpec as P

SAMPLES = 7680
FREQS = 1200
FIRST_BIN = 32
LAGS = 256
SMOOTH = 4
PARTNERS = 4
REACH = 7
BLOCK = 256
WINDOWS = 2
WATER = 0.3
RESCALE = 2.0

RADIX = 10
PART = SAMPLES // RADIX
HALF = BLOCK // 2
PER = FREQS // RADIX
LANES = 128
WIDE = RADIX * 2 * LANES
ORDER = (0, 5, 2, 8, 4, 6, 3, 7, 1, 9)
PAIRS = len(ORDER) // 2 - 1
PLANE = 16
INNER = PLANE - REACH
MINE = HALF // PLANE
CHUNKS = 4
VMEM = 56 * 1024 * 1024


def residue_bins(residue):
    first = (residue - FIRST_BIN) % RADIX
    return FIRST_BIN + first + RADIX * np.arange(PER)


def place_in_band(residue):
    return (residue - FIRST_BIN) % RADIX


def angles(steps, residue):
    phase = steps[:, None] * residue_bins(residue)[None, :] % SAMPLES
    angle = phase * (2.0 * math.pi / SAMPLES)
    fill = ((0, 0), (0, LANES - PER))
    return np.concatenate([np.pad(np.cos(angle), fill), np.pad(-np.sin(angle), fill)], axis=1)


def dft_table():
    columns = [angles(np.arange(PART), residue) for residue in ORDER]
    chunks = [np.concatenate(columns[i : i + 2], axis=1) for i in range(0, RADIX, 2)]
    return np.stack(chunks).astype(np.float32).astype(ml_dtypes.bfloat16)


def lag_tables():
    lag_steps = np.arange(LAGS) - LAGS // 2 + SAMPLES
    factor = RESCALE / math.sqrt(FREQS * WINDOWS)
    table = np.concatenate([angles(lag_steps, residue).T for residue in ORDER]) * factor
    table = table.astype(np.float32)
    high = table.astype(ml_dtypes.bfloat16)
    low = (table - high.astype(np.float32)).astype(ml_dtypes.bfloat16)
    return high, low


def taper_columns(taper):
    parts = jnp.pad((taper * taper).reshape(PER, RADIX).T, ((0, 0), (0, LANES - PER)))
    return jnp.stack([parts[place_in_band(residue)] for residue in ORDER])


def five_point(x):
    cos = [math.cos(2.0 * math.pi * k / 5) for k in (1, 2)]
    sin = [math.sin(2.0 * math.pi * k / 5) for k in (1, 2)]
    near, far = x[1] + x[4], x[2] + x[3]
    near_gap, far_gap = x[1] - x[4], x[2] - x[3]
    return (
        x[0] + near + far,
        x[0] + cos[0] * near + cos[1] * far,
        sin[0] * near_gap + sin[1] * far_gap,
        x[0] + cos[1] * near + cos[0] * far,
        sin[1] * near_gap - sin[0] * far_gap,
    )


def dft_kernel(
    pairs_ref, x_hbm, table_hbm, mine_ref, theirs_ref, x_ref, table_ref, y_ref, real_ref, pair_ref, x_sems, t_sems
):
    core = lax.axis_index("tm")
    block = lax.axis_index("row") * PLANE + lax.axis_index("col")
    size = BLOCK // CHUNKS
    x_copies = [
        pltpu.make_async_copy(
            x_hbm.at[pl.ds(c * size, size)], x_ref.at[pl.ds(c * size, size)], x_sems.at[c]
        )
        for c in range(CHUNKS)
    ]
    t_copies = [
        pltpu.make_async_copy(table_hbm.at[c], table_ref.at[c], t_sems.at[c])
        for c in range(PAIRS + 1)
    ]
    for copy in x_copies + t_copies:
        copy.start()

    def split(i, carry):
        at = pl.ds(pl.multiple_of(i * 16, 16), 16)
        for lane in range(0, PART, LANES):
            x = [
                x_ref[at, n * PART + lane : n * PART + lane + LANES].astype(jnp.float32)
                for n in range(RADIX)
            ]
            even = five_point([x[n] + x[n + 5] for n in range(5)])
            odd = five_point([x[n] - x[n + 5] if n % 2 == 0 else x[n + 5] - x[n] for n in range(5)])
            parts = (even[0], odd[0]) + even[1:] + odd[1:3] + odd[3:]
            for n, part in enumerate(parts):
                y_ref[
                    pl.ds(pl.multiple_of(n * BLOCK + i * 16, 16), 16), lane : lane + LANES
                ] = part.astype(jnp.bfloat16)
        return carry

    for c in range(CHUNKS):
        x_copies[c].wait()
        lax.fori_loop(c * size // 16, (c + 1) * size // 16, split, 0)

    t_copies[0].wait()
    for n in range(2):
        real_ref[n] = jnp.dot(
            y_ref[n * BLOCK : (n + 1) * BLOCK, :],
            table_ref[0, :, n * 2 * LANES : (n + 1) * 2 * LANES],
            preferred_element_type=jnp.float32,
        )
    for n in range(PAIRS):
        t_copies[n + 1].wait()
        pair_ref[n] = jnp.dot(
            y_ref[(n + 1) * 2 * BLOCK : (n + 2) * 2 * BLOCK, :],
            table_ref[n + 1],
            preferred_element_type=jnp.float32,
        )

    lane = lax.broadcasted_iota(jnp.int32, (16, LANES), 1)
    offsets = jnp.zeros((16, LANES), jnp.float32)
    for k in range(PARTNERS):
        partner = pairs_ref[0, k]
        offset = jnp.where(partner < 0, 0, partner - block).astype(jnp.float32)
        offsets = jnp.where(lane == PER + k, offset, offsets)

    def white_rows(row):
        at = pl.ds(pl.multiple_of(row, 16), 16)
        under = pl.ds(pl.multiple_of(row + BLOCK, 16), 16)
        spectrum = [(real_ref[n, at, :LANES], real_ref[n, at, LANES:]) for n in range(2)]
        for n in range(PAIRS):
            for side, way in ((0, 1.0), (1, -1.0)):
                if n >= PAIRS // 2:
                    way = -way
                first = slice(2 * side * LANES, (2 * side + 1) * LANES)
                second = slice((2 * side + 1) * LANES, (2 * side + 2) * LANES)
                u_cos, u_sin = pair_ref[n, at, first], pair_ref[n, at, second]
                v_cos, v_sin = pair_ref[n, under, first], pair_ref[n, under, second]
                spectrum.append((u_cos + way * v_sin, u_sin - way * v_cos))
        band = [None] * RADIX
        for residue, (re, im) in zip(ORDER, spectrum):
            square = re * re + im * im
            band[place_in_band(residue)] = square * lax.rsqrt(jnp.maximum(square, 1e-30))
        total = band[0]
        for amplitude in band[1:]:
            total = total + amplitude
        floor = WATER / FREQS * jnp.sum(total, axis=1, keepdims=True) + 1e-05
        line = [pltpu.roll(a, 1, 1) for a in band[RADIX - SMOOTH :]]
        line = line + band + [pltpu.roll(a, LANES - 1, 1) for a in band[:SMOOTH]]
        two = [line[i] + line[i + 1] for i in range(len(line) - 1)]
        four = [two[i] + two[i + 2] for i in range(len(two) - 2)]
        out = []
        for residue, (re, im) in zip(ORDER, spectrum):
            i = place_in_band(residue)
            smoothed = (four[i] + four[i + 4] + line[i + 8]) * (1.0 / (2 * SMOOTH + 1))
            level = smoothed + floor
            scale = pl.reciprocal(level, approx=True)
            scale = scale * (2.0 - level * scale)
            out.append((re * scale, im * scale))
        first = jnp.where(lane >= PER, offsets, out[0][0])
        out[0] = (first, out[0][1])
        return out

    def theirs(i, carry):
        for n, parts in enumerate(white_rows((1 - core) * HALF + i * 16)):
            for side, part in enumerate(parts):
                here = (2 * n + side) * LANES
                theirs_ref[pl.ds(pl.multiple_of(i * 16, 16), 16), here : here + LANES] = (
                    part.astype(jnp.bfloat16)
                )
        return carry

    def mine(i, carry):
        for n, parts in enumerate(white_rows(core * HALF + i * 16)):
            for side, part in enumerate(parts):
                here = (2 * n + side) * LANES
                for j in range(2):
                    rows = part[j * MINE : (j + 1) * MINE]
                    mine_ref[i * 2 + j, :, here : here + LANES] = jnp.concatenate(
                        [rows, rows], axis=0
                    ).astype(jnp.bfloat16)
        return carry

    lax.fori_loop(0, HALF // 16, theirs, 0)
    lax.fori_loop(0, HALF // 16, mine, 0)


def whitened(series, pairs):
    hbm = pl.BlockSpec(memory_space=pl.ANY)
    vmem = pl.BlockSpec(memory_space=pltpu.VMEM)
    return pl.pallas_call(
        dft_kernel,
        in_specs=[pl.BlockSpec(memory_space=pltpu.SMEM), hbm, hbm],
        out_specs=[vmem, vmem],
        out_shape=[
            jax.ShapeDtypeStruct((PLANE, 2 * MINE, WIDE), jnp.bfloat16),
            jax.ShapeDtypeStruct((HALF, WIDE), jnp.bfloat16),
        ],
        scratch_shapes=[
            pltpu.VMEM((BLOCK, SAMPLES), jnp.bfloat16),
            pltpu.VMEM((PAIRS + 1, PART, 4 * LANES), jnp.bfloat16),
            pltpu.VMEM((RADIX * BLOCK, PART), jnp.bfloat16),
            pltpu.VMEM((2, BLOCK, 2 * LANES), jnp.float32),
            pltpu.VMEM((PAIRS, 2 * BLOCK, 4 * LANES), jnp.float32),
            pltpu.SemaphoreType.DMA((CHUNKS,)),
            pltpu.SemaphoreType.DMA((PAIRS + 1,)),
        ],
        compiler_params=pltpu.CompilerParams(vmem_limit_bytes=VMEM),
        name="dft_whiten",
    )(pairs, series, jnp.asarray(dft_table()))


def corr_kernel(
    first_block,
    count,
    with_halo,
    taper_ref,
    plane_ref,
    *refs,
):
    if with_halo:
        halo_ref, high_ref, low_ref, done_ref, out_ref = refs[:5]
        refs = refs[5:]
    else:
        high_ref, low_ref, out_ref = refs[:3]
        refs = refs[3:]
    w_ref, xh_ref, xl_ref, lag_ref, number_ref, scalar_ref, sems = refs
    inside = PLANE - first_block
    copies = [
        pltpu.make_async_copy(
            plane_ref.at[pl.ds(first_block, inside)], w_ref.at[pl.ds(0, inside)], sems.at[0]
        )
    ]
    if with_halo:
        copies.append(
            pltpu.make_async_copy(halo_ref, w_ref.at[pl.ds(inside, REACH)], sems.at[1])
        )
    for copy in copies:
        copy.start()
    for copy in copies:
        copy.wait()
    for a in range(count):
        number_ref[a : a + 1, :] = (
            w_ref[a, :, :LANES].astype(jnp.float32)[:1].astype(jnp.int32)
        )
    numbers = pltpu.make_async_copy(number_ref, scalar_ref, sems.at[2])
    numbers.start()
    numbers.wait()

    def one_block(a, carry):
        seconds = [a + scalar_ref[a, PER + k] for k in range(PARTNERS)]
        for n in range(RADIX):
            here = 2 * n * LANES

            def load(index):
                both = w_ref[index, :, here : here + 2 * LANES].astype(jnp.float32)
                return [
                    (both[w * MINE : (w + 1) * MINE, :LANES], both[w * MINE : (w + 1) * MINE, LANES:])
                    for w in range(WINDOWS)
                ]

            taper = taper_ref[n : n + 1, :]
            first = [(re * taper, im * taper) for re, im in load(a)]
            for slot in range(0, PARTNERS, 2):
                at = pl.ds(pl.multiple_of((a * PARTNERS + slot) * MINE, 16), 2 * MINE)
                re, im = [], []
                for k in (slot, slot + 1):
                    (a_re, a_im), (c_re, c_im) = first
                    (b_re, b_im), (d_re, d_im) = load(seconds[k])
                    re.append((a_re * b_re + a_im * b_im) + (c_re * d_re + c_im * d_im))
                    im.append((a_im * b_re - a_re * b_im) + (c_im * d_re - c_re * d_im))
                for side, both in enumerate((re, im)):
                    cross = jnp.concatenate(both, axis=0)
                    high = cross.astype(jnp.bfloat16)
                    columns = slice(here + side * LANES, here + (side + 1) * LANES)
                    xh_ref[at, columns] = high
                    xl_ref[at, columns] = (cross - high.astype(jnp.float32)).astype(jnp.bfloat16)
        return carry

    lax.fori_loop(0, count, one_block, 0)
    lagged = jnp.dot(xh_ref[...], high_ref[...], preferred_element_type=jnp.float32)
    lagged += jnp.dot(xh_ref[...], low_ref[...], preferred_element_type=jnp.float32)
    lagged += jnp.dot(xl_ref[...], high_ref[...], preferred_element_type=jnp.float32)
    lag_ref[...] = lagged.reshape(lag_ref.shape)

    def mask(a, carry):
        for k in range(PARTNERS):

            @pl.when(scalar_ref[a, PER + k] == 0)
            def clear():
                lag_ref[a * PARTNERS + k] = jnp.zeros((MINE, LAGS), jnp.float32)

        return carry

    lax.fori_loop(0, count, mask, 0)
    write = pltpu.make_async_copy(
        lag_ref, out_ref.at[pl.ds(first_block * PARTNERS, count * PARTNERS)], sems.at[0]
    )
    write.start()
    write.wait()


def correlated(taper, plane, halo=None, done=None):
    high, low = lag_tables()
    with_halo = halo is not None
    first_block, count = (INNER, REACH) if with_halo else (0, INNER)
    held = PLANE + REACH - first_block if with_halo else PLANE
    rows = count * PARTNERS * MINE
    vmem = pl.BlockSpec(memory_space=pltpu.VMEM)
    hbm = pl.BlockSpec(memory_space=pl.ANY)
    operands = [taper, plane] + ([halo] if with_halo else []) + [jnp.asarray(high), jnp.asarray(low)]
    specs = [vmem, hbm] + ([hbm] if with_halo else []) + [vmem, vmem]
    aliases = {}
    if with_halo:
        aliases = {len(operands): 0}
        operands.append(done)
        specs.append(hbm)

    def body(*refs):
        corr_kernel(first_block, count, with_halo, *refs)

    return pl.pallas_call(
        body,
        in_specs=specs,
        out_specs=hbm,
        out_shape=jax.ShapeDtypeStruct((PLANE * PARTNERS, MINE, LAGS), jnp.float32),
        scratch_shapes=[
            pltpu.VMEM((held, 2 * MINE, WIDE), jnp.bfloat16),
            pltpu.VMEM((rows, WIDE), jnp.bfloat16),
            pltpu.VMEM((rows, WIDE), jnp.bfloat16),
            pltpu.VMEM((count * PARTNERS, MINE, LAGS), jnp.float32),
            pltpu.VMEM((PLANE, LANES), jnp.int32),
            pltpu.SMEM((PLANE, LANES), jnp.int32),
            pltpu.SemaphoreType.DMA((3,)),
        ],
        input_output_aliases=aliases,
        compiler_params=pltpu.CompilerParams(vmem_limit_bytes=VMEM),
        cost_estimate=pl.CostEstimate(
            flops=6 * rows * WIDE * LAGS, bytes_accessed=4 << 20, transcendentals=0
        ),
        name="correlate_halo" if with_halo else "correlate_inner",
    )(*operands)


def per_device(records, taper, pairs):
    mine, theirs = whitened(records[0], pairs)
    got = lax.ppermute(theirs, "tm", [(0, 1), (1, 0)])
    send = mine.at[:, MINE:].set(got.reshape(PLANE, MINE, WIDE))
    plane = lax.all_to_all(send, "col", 0, 0, tiled=True)
    count = lax.axis_size("row")
    halo = lax.ppermute(plane[:REACH], "row", [(z, z - 1) for z in range(1, count)])
    plane, taper = lax.optimization_barrier((plane, taper))
    squared = taper_columns(taper)
    lagged = correlated(squared, plane)
    lagged = correlated(squared, plane, halo, lagged)
    lagged = lagged.reshape(PLANE, PARTNERS, MINE, LAGS)
    back = lax.all_to_all(lagged, "col", 0, 0, tiled=True)
    return back.transpose(1, 0, 2, 3).reshape(1, PARTNERS, HALF, LAGS)


def solution(mesh):
    return jax.shard_map(
        per_device,
        mesh=mesh,
        in_specs=(P("tm", ("row", "col"), None), P(), P(("row", "col"), None)),
        out_specs=P(("row", "col"), None, "tm", None),
        check_vma=False,
    )
```

```python
import math

import jax
import jax.numpy as jnp
import ml_dtypes
import numpy as np
from jax import lax
from jax.experimental import pallas as pl
from jax.experimental.pallas import tpu as pltpu
from jax.sharding import PartitionSpec as P

SAMPLES = 7680
FREQS = 1200
FIRST_BIN = 32
LAGS = 256
SMOOTH = 4
PARTNERS = 4
REACH = 7
BLOCK = 256
WINDOWS = 2
WATER = 0.3
RESCALE = 2.0

RADIX = 10
PART = SAMPLES // RADIX
HALF = BLOCK // 2
PER = FREQS // RADIX
LANES = 128
WIDE = RADIX * 2 * LANES
ORDER = (0, 5, 2, 8, 4, 6, 3, 7, 1, 9)
PAIRS = len(ORDER) // 2 - 1
PLANE = 16
INNER = PLANE - REACH
MINE = HALF // PLANE
CHUNKS = 4


def residue_bins(residue):
    first = (residue - FIRST_BIN) % RADIX
    return FIRST_BIN + first + RADIX * np.arange(PER)


def place_in_band(residue):
    return (residue - FIRST_BIN) % RADIX


def angles(steps, residue):
    phase = steps[:, None] * residue_bins(residue)[None, :] % SAMPLES
    angle = phase * (2.0 * math.pi / SAMPLES)
    fill = ((0, 0), (0, LANES - PER))
    return np.concatenate([np.pad(np.cos(angle), fill), np.pad(-np.sin(angle), fill)], axis=1)


def dft_table():
    columns = [angles(np.arange(PART), residue) for residue in ORDER]
    chunks = [np.concatenate(columns[i : i + 2], axis=1) for i in range(0, RADIX, 2)]
    return np.stack(chunks).astype(np.float32).astype(ml_dtypes.bfloat16)


def lag_tables():
    lag_steps = np.arange(LAGS) - LAGS // 2 + SAMPLES
    factor = RESCALE / math.sqrt(FREQS * WINDOWS)
    table = np.concatenate([angles(lag_steps, residue).T for residue in ORDER]) * factor
    table = table.astype(np.float32)
    high = table.astype(ml_dtypes.bfloat16)
    low = (table - high.astype(np.float32)).astype(ml_dtypes.bfloat16)
    return high, low


def taper_columns(taper):
    parts = jnp.pad((taper * taper).reshape(PER, RADIX).T, ((0, 0), (0, LANES - PER)))
    return jnp.stack([parts[place_in_band(residue)] for residue in ORDER])


def five_point(x):
    cos = [math.cos(2.0 * math.pi * k / 5) for k in (1, 2)]
    sin = [math.sin(2.0 * math.pi * k / 5) for k in (1, 2)]
    near, far = x[1] + x[4], x[2] + x[3]
    near_gap, far_gap = x[1] - x[4], x[2] - x[3]
    return (
        x[0] + near + far,
        x[0] + cos[0] * near + cos[1] * far,
        sin[0] * near_gap + sin[1] * far_gap,
        x[0] + cos[1] * near + cos[0] * far,
        sin[1] * near_gap - sin[0] * far_gap,
    )


def dft_kernel(
    x_hbm, table_hbm, theirs_ref, real_ref, pair_ref, x_ref, table_ref, y_ref, x_sems, t_sems
):
    core = lax.axis_index("tm")
    size = BLOCK // CHUNKS
    x_copies = [
        pltpu.make_async_copy(
            x_hbm.at[pl.ds(c * size, size)], x_ref.at[pl.ds(c * size, size)], x_sems.at[c]
        )
        for c in range(CHUNKS)
    ]
    t_copies = [
        pltpu.make_async_copy(table_hbm.at[c], table_ref.at[c], t_sems.at[c])
        for c in range(PAIRS + 1)
    ]
    for copy in x_copies:
        copy.start()

    def split(i, carry):
        at = pl.ds(pl.multiple_of(i * 16, 16), 16)
        for lane in range(0, PART, LANES):
            x = [
                x_ref[at, n * PART + lane : n * PART + lane + LANES].astype(jnp.float32)
                for n in range(RADIX)
            ]
            even = five_point([x[n] + x[n + 5] for n in range(5)])
            odd = five_point([x[n] - x[n + 5] if n % 2 == 0 else x[n + 5] - x[n] for n in range(5)])
            parts = (even[0], odd[0]) + even[1:] + odd[1:]
            for n, part in enumerate(parts):
                y_ref[
                    pl.ds(pl.multiple_of(n * BLOCK + i * 16, 16), 16), lane : lane + LANES
                ] = part.astype(jnp.bfloat16)
        return carry

    for c in range(CHUNKS):
        x_copies[c].wait()
        if c == CHUNKS - 2:
            for copy in t_copies:
                copy.start()
        lax.fori_loop(c * size // 16, (c + 1) * size // 16, split, 0)

    t_copies[0].wait()
    for n in range(2):
        real_ref[n] = jnp.dot(
            y_ref[n * BLOCK : (n + 1) * BLOCK, :],
            table_ref[0, :, n * 2 * LANES : (n + 1) * 2 * LANES],
            preferred_element_type=jnp.float32,
        )
    for n in range(PAIRS):
        t_copies[n + 1].wait()
        pair_ref[n] = jnp.dot(
            y_ref[(n + 1) * 2 * BLOCK : (n + 2) * 2 * BLOCK, :],
            table_ref[n + 1],
            preferred_element_type=jnp.float32,
        )

    def rows(i, carry):
        row = (1 - core) * HALF + i * 16
        parts = [white_rows(real_ref, pair_ref, row + j * MINE) for j in range(2)]
        for n in range(2 * RADIX):
            theirs_ref[pl.ds(pl.multiple_of(i * 16, 16), 16), n * LANES : (n + 1) * LANES] = (
                jnp.concatenate([parts[0][n], parts[1][n]], axis=0).astype(jnp.bfloat16)
            )
        return carry

    lax.fori_loop(0, HALF // 16, rows, 0)


def spectrum_part(real_ref, pair_ref, row, place):
    at = pl.ds(pl.multiple_of(row, MINE), MINE)
    if place < 2:
        return real_ref[place, at, :LANES], real_ref[place, at, LANES:]
    n, side = (place - 2) // 2, place % 2
    plain = (side == 0) == (n < PAIRS // 2)
    under = pl.ds(pl.multiple_of(row + BLOCK, MINE), MINE)
    first = slice(2 * side * LANES, (2 * side + 1) * LANES)
    second = slice((2 * side + 1) * LANES, (2 * side + 2) * LANES)
    u_cos, u_sin = pair_ref[n, at, first], pair_ref[n, at, second]
    v_cos, v_sin = pair_ref[n, under, first], pair_ref[n, under, second]
    if plain:
        return u_cos + v_sin, u_sin - v_cos
    return u_cos - v_sin, u_sin + v_cos


def white_rows(real_ref, pair_ref, row):
    band = [None] * RADIX
    for place, residue in enumerate(ORDER):
        re, im = spectrum_part(real_ref, pair_ref, row, place)
        square = re * re + im * im
        band[place_in_band(residue)] = square * lax.rsqrt(jnp.maximum(square, 1e-30))
    total = band[0]
    for amplitude in band[1:]:
        total = total + amplitude
    floor = WATER / FREQS * jnp.sum(total, axis=1, keepdims=True) + 1e-05
    line = [pltpu.roll(a, 1, 1) for a in band[RADIX - SMOOTH :]]
    line = line + band + [pltpu.roll(a, LANES - 1, 1) for a in band[:SMOOTH]]
    two = [line[i] + line[i + 1] for i in range(len(line) - 1)]
    four = [two[i] + two[i + 2] for i in range(len(two) - 2)]
    out = []
    for place, residue in enumerate(ORDER):
        i = place_in_band(residue)
        smoothed = (four[i] + four[i + 4] + line[i + 8]) * (1.0 / (2 * SMOOTH + 1))
        level = smoothed + floor
        scale = pl.reciprocal(level, approx=True)
        scale = scale * (2.0 - level * scale)
        re, im = spectrum_part(real_ref, pair_ref, row, place)
        out += [re * scale, im * scale]
    return out


def own_kernel(pairs_ref, real_ref, pair_ref, mine_ref):
    core = lax.axis_index("tm")
    block = lax.axis_index("row") * PLANE + lax.axis_index("col")
    lane = lax.broadcasted_iota(jnp.int32, (MINE, LANES), 1)
    offsets = jnp.zeros((MINE, LANES), jnp.float32)
    for k in range(PARTNERS):
        partner = pairs_ref[0, k]
        offset = jnp.where(partner < 0, 0, partner - block).astype(jnp.float32)
        offsets = jnp.where(lane == PER + k, offset, offsets)

    def rows(j, carry):
        parts = white_rows(real_ref, pair_ref, core * HALF + j * MINE)
        parts[0] = jnp.where(lane >= PER, offsets, parts[0])
        for n, part in enumerate(parts):
            mine_ref[j, :, n * LANES : (n + 1) * LANES] = jnp.concatenate(
                [part, part], axis=0
            ).astype(jnp.bfloat16)
        return carry

    lax.fori_loop(0, PLANE, rows, 0)


def in_vmem(array):
    return pltpu.with_memory_space_constraint(array, pltpu.VMEM)


def spectra(series):
    hbm = pl.BlockSpec(memory_space=pltpu.HBM)
    vmem = pl.BlockSpec(memory_space=pltpu.VMEM)
    return pl.pallas_call(
        dft_kernel,
        in_specs=[hbm, hbm],
        out_specs=[vmem, vmem, vmem],
        out_shape=[
            pltpu.VMEM((HALF, WIDE), jnp.bfloat16),
            pltpu.VMEM((2, BLOCK, 2 * LANES), jnp.float32),
            pltpu.VMEM((PAIRS, 2 * BLOCK, 4 * LANES), jnp.float32),
        ],
        scratch_shapes=[
            pltpu.VMEM((BLOCK, SAMPLES), jnp.bfloat16),
            pltpu.VMEM((PAIRS + 1, PART, 4 * LANES), jnp.bfloat16),
            pltpu.VMEM((RADIX * BLOCK, PART), jnp.bfloat16),
            pltpu.SemaphoreType.DMA((CHUNKS,)),
            pltpu.SemaphoreType.DMA((PAIRS + 1,)),
        ],
        compiler_params=pltpu.CompilerParams(vmem_limit_bytes=20 << 20),
        name="dft_whiten",
    )(*[pltpu.with_memory_space_constraint(a, pltpu.HBM) for a in (series, jnp.asarray(dft_table()))])


def own_half(pairs, real, pair):
    vmem = pl.BlockSpec(memory_space=pltpu.VMEM)
    return pl.pallas_call(
        own_kernel,
        in_specs=[pl.BlockSpec(memory_space=pltpu.SMEM), vmem, vmem],
        out_specs=vmem,
        out_shape=pltpu.VMEM((PLANE, 2 * MINE, WIDE), jnp.bfloat16),
        compiler_params=pltpu.CompilerParams(vmem_limit_bytes=4 << 20),
        cost_estimate=pl.CostEstimate(
            flops=40 * HALF * WIDE, bytes_accessed=5 << 20, transcendentals=0
        ),
        name="whiten_own",
    )(pairs, in_vmem(real), in_vmem(pair))


def corr_kernel(first_block, count, taper_ref, plane_ref, *refs):
    with_halo = first_block > 0
    if with_halo:
        halo_ref, high_ref, low_ref, _, out_ref, xh_ref, xl_ref, number_ref, scalar_ref, sem, w_ref = refs
    else:
        high_ref, low_ref, out_ref, xh_ref, xl_ref, number_ref, scalar_ref, sem = refs
        w_ref = plane_ref
    for a in range(count):
        number_ref[a : a + 1, :] = (
            plane_ref[first_block + a, :, :LANES].astype(jnp.float32)[:1].astype(jnp.int32)
        )
    numbers = pltpu.make_async_copy(number_ref, scalar_ref, sem)
    numbers.start()
    if with_halo:

        def own(i, carry):
            w_ref[i] = plane_ref[first_block + i]
            w_ref[count + i] = halo_ref[i]
            return carry

        lax.fori_loop(0, REACH, own, 0)
    numbers.wait()

    def one_block(a, carry):
        seconds = [a + scalar_ref[a, PER + k] for k in range(PARTNERS)]
        for n in range(RADIX):
            here = 2 * n * LANES

            def load(index):
                both = w_ref[index, :, here : here + 2 * LANES].astype(jnp.float32)
                return [
                    (both[w * MINE : (w + 1) * MINE, :LANES], both[w * MINE : (w + 1) * MINE, LANES:])
                    for w in range(WINDOWS)
                ]

            taper = taper_ref[n : n + 1, :]
            first = [(re * taper, im * taper) for re, im in load(a)]
            for slot in range(0, PARTNERS, 2):
                at = pl.ds(pl.multiple_of((a * PARTNERS + slot) * MINE, 16), 2 * MINE)
                re, im = [], []
                for k in (slot, slot + 1):
                    (a_re, a_im), (c_re, c_im) = first
                    (b_re, b_im), (d_re, d_im) = load(seconds[k])
                    re.append((a_re * b_re + a_im * b_im) + (c_re * d_re + c_im * d_im))
                    im.append((a_im * b_re - a_re * b_im) + (c_im * d_re - c_re * d_im))
                for side, both in enumerate((re, im)):
                    cross = jnp.concatenate(both, axis=0)
                    high = cross.astype(jnp.bfloat16)
                    columns = slice(here + side * LANES, here + (side + 1) * LANES)
                    xh_ref[at, columns] = high
                    xl_ref[at, columns] = (cross - high.astype(jnp.float32)).astype(jnp.bfloat16)
        return carry

    lax.fori_loop(0, count, one_block, 0)
    lagged = jnp.dot(xh_ref[...], high_ref[...], preferred_element_type=jnp.float32)
    lagged += jnp.dot(xh_ref[...], low_ref[...], preferred_element_type=jnp.float32)
    lagged += jnp.dot(xl_ref[...], high_ref[...], preferred_element_type=jnp.float32)
    start = first_block * PARTNERS
    out_ref[start : start + count * PARTNERS] = lagged.reshape(count * PARTNERS, MINE, LAGS)

    def mask(a, carry):
        for k in range(PARTNERS):

            @pl.when(scalar_ref[a, PER + k] == 0)
            def clear():
                out_ref[start + a * PARTNERS + k] = jnp.zeros((MINE, LAGS), jnp.float32)

        return carry

    lax.fori_loop(0, count, mask, 0)


def correlated(taper, plane, high, low, halo=None, done=None):
    with_halo = halo is not None
    first_block, count = (INNER, REACH) if with_halo else (0, INNER)
    rows = count * PARTNERS * MINE
    vmem = pl.BlockSpec(memory_space=pltpu.VMEM)
    operands = [taper, plane] + ([halo] if with_halo else []) + [high, low]
    aliases = {}
    scratch = [
        pltpu.VMEM((rows, WIDE), jnp.bfloat16),
        pltpu.VMEM((rows, WIDE), jnp.bfloat16),
        pltpu.VMEM((PLANE, LANES), jnp.int32),
        pltpu.SMEM((PLANE, LANES), jnp.int32),
        pltpu.SemaphoreType.DMA(()),
    ]
    if with_halo:
        aliases = {len(operands): 0}
        operands.append(done)
        scratch.append(pltpu.VMEM((2 * REACH, 2 * MINE, WIDE), jnp.bfloat16))

    def body(*refs):
        corr_kernel(first_block, count, *refs)

    return pl.pallas_call(
        body,
        in_specs=[vmem] * len(operands),
        out_specs=vmem,
        out_shape=pltpu.VMEM((PLANE * PARTNERS, MINE, LAGS), jnp.float32),
        scratch_shapes=scratch,
        input_output_aliases=aliases,
        compiler_params=pltpu.CompilerParams(vmem_limit_bytes=10 << 20),
        cost_estimate=pl.CostEstimate(
            flops=6 * rows * WIDE * LAGS, bytes_accessed=4 << 20, transcendentals=0
        ),
        name="correlate_halo" if with_halo else "correlate_inner",
    )(*[in_vmem(operand) for operand in operands])


def per_device(records, taper, pairs):
    theirs, real, pair = spectra(records[0])
    got = lax.ppermute(theirs, "tm", [(0, 1), (1, 0)])
    mine = own_half(pairs, real, pair)
    send = mine.at[:, MINE:].set(got.reshape(PLANE, MINE, WIDE))
    plane = lax.all_to_all(send, "col", 0, 0, tiled=True)
    count = lax.axis_size("row")
    halo = lax.ppermute(plane[:REACH], "row", [(z, z - 1) for z in range(1, count)])
    plane, taper = lax.optimization_barrier((plane, taper))
    squared = taper_columns(taper)
    high, low = (jnp.asarray(table) for table in lag_tables())
    lagged = correlated(squared, plane, high, low)
    lagged = correlated(squared, plane, high, low, halo, lagged)
    lagged = lagged.reshape(PLANE, PARTNERS, MINE, LAGS)
    back = lax.all_to_all(lagged, "col", 0, 0, tiled=True)
    return back.transpose(1, 0, 2, 3).reshape(1, PARTNERS, HALF, LAGS)


def solution(mesh):
    return jax.shard_map(
        per_device,
        mesh=mesh,
        in_specs=(P("tm", ("row", "col"), None), P(), P(("row", "col"), None)),
        out_specs=P(("row", "col"), None, "tm", None),
        check_vma=False,
    )
```

```python
import math

import jax
import jax.numpy as jnp
import ml_dtypes
import numpy as np
from jax import lax
from jax.experimental import pallas as pl
from jax.experimental.pallas import tpu as pltpu
from jax.sharding import PartitionSpec as P

SAMPLES = 7680
FREQS = 1200
FIRST_BIN = 32
LAGS = 256
SMOOTH = 4
PARTNERS = 4
REACH = 7
BLOCK = 256
WINDOWS = 2
WATER = 0.3
RESCALE = 2.0

RADIX = 10
PART = SAMPLES // RADIX
HALF = BLOCK // 2
PER = FREQS // RADIX
LANES = 128
WIDE = RADIX * 2 * LANES
HALF_WIDE = WIDE // 2
ORDER = (0, 5, 2, 8, 4, 6, 3, 7, 1, 9)
PAIRS = len(ORDER) // 2 - 1
PLANE = 16
INNER = PLANE - REACH
MINE = HALF // PLANE
CHUNKS = 4


def residue_bins(residue):
    first = (residue - FIRST_BIN) % RADIX
    return FIRST_BIN + first + RADIX * np.arange(PER)


def place_in_band(residue):
    return (residue - FIRST_BIN) % RADIX


def angles(steps, residue):
    phase = steps[:, None] * residue_bins(residue)[None, :] % SAMPLES
    angle = phase * (2.0 * math.pi / SAMPLES)
    fill = ((0, 0), (0, LANES - PER))
    return np.concatenate([np.pad(np.cos(angle), fill), np.pad(-np.sin(angle), fill)], axis=1)


def dft_table():
    columns = [angles(np.arange(PART), residue) for residue in ORDER]
    chunks = [np.concatenate(columns[i : i + 2], axis=1) for i in range(0, RADIX, 2)]
    return np.stack(chunks).astype(np.float32).astype(ml_dtypes.bfloat16)


def lag_tables():
    lag_steps = np.arange(LAGS) - LAGS // 2 + SAMPLES
    factor = RESCALE / math.sqrt(FREQS * WINDOWS)
    table = np.concatenate([angles(lag_steps, residue).T for residue in ORDER]) * factor
    table = table.astype(np.float32)
    high = table.astype(ml_dtypes.bfloat16)
    low = (table - high.astype(np.float32)).astype(ml_dtypes.bfloat16)
    return high, low


def taper_columns(taper):
    parts = jnp.pad((taper * taper).reshape(PER, RADIX).T, ((0, 0), (0, LANES - PER)))
    return jnp.stack([parts[place_in_band(residue)] for residue in ORDER])


def five_point(x):
    cos = [math.cos(2.0 * math.pi * k / 5) for k in (1, 2)]
    sin = [math.sin(2.0 * math.pi * k / 5) for k in (1, 2)]
    near, far = x[1] + x[4], x[2] + x[3]
    near_gap, far_gap = x[1] - x[4], x[2] - x[3]
    return (
        x[0] + near + far,
        x[0] + cos[0] * near + cos[1] * far,
        sin[0] * near_gap + sin[1] * far_gap,
        x[0] + cos[1] * near + cos[0] * far,
        sin[1] * near_gap - sin[0] * far_gap,
    )


def dft_kernel(
    x_hbm, table_hbm, theirs_ref, real_ref, pair_ref, x_ref, table_ref, y_ref, x_sems, t_sems
):
    core = lax.axis_index("tm")
    size = BLOCK // CHUNKS
    x_copies = [
        pltpu.make_async_copy(
            x_hbm.at[pl.ds(c * size, size)], x_ref.at[pl.ds(c * size, size)], x_sems.at[c]
        )
        for c in range(CHUNKS)
    ]
    t_copies = [
        pltpu.make_async_copy(table_hbm.at[c], table_ref.at[c], t_sems.at[c])
        for c in range(PAIRS + 1)
    ]
    for copy in x_copies:
        copy.start()

    def split(i, carry):
        at = pl.ds(pl.multiple_of(i * 16, 16), 16)
        for lane in range(0, PART, LANES):
            x = [
                x_ref[at, n * PART + lane : n * PART + lane + LANES].astype(jnp.float32)
                for n in range(RADIX)
            ]
            even = five_point([x[n] + x[n + 5] for n in range(5)])
            odd = five_point([x[n] - x[n + 5] if n % 2 == 0 else x[n + 5] - x[n] for n in range(5)])
            parts = (even[0], odd[0]) + even[1:] + odd[1:]
            for n, part in enumerate(parts):
                y_ref[
                    pl.ds(pl.multiple_of(n * BLOCK + i * 16, 16), 16), lane : lane + LANES
                ] = part.astype(jnp.bfloat16)
        return carry

    for c in range(CHUNKS):
        x_copies[c].wait()
        if c == CHUNKS - 2:
            for copy in t_copies:
                copy.start()
        lax.fori_loop(c * size // 16, (c + 1) * size // 16, split, 0, unroll=2)

    t_copies[0].wait()
    for n in range(2):
        real_ref[n] = jnp.dot(
            y_ref[n * BLOCK : (n + 1) * BLOCK, :],
            table_ref[0, :, n * 2 * LANES : (n + 1) * 2 * LANES],
            preferred_element_type=jnp.float32,
        )
    for n in range(PAIRS):
        t_copies[n + 1].wait()
        pair_ref[n] = jnp.dot(
            y_ref[(n + 1) * 2 * BLOCK : (n + 2) * 2 * BLOCK, :],
            table_ref[n + 1],
            preferred_element_type=jnp.float32,
        )

    def rows(i, carry):
        row = (1 - core) * HALF + i * 16
        parts = [white_rows(real_ref, pair_ref, row + j * MINE) for j in range(2)]
        for n in range(2 * RADIX):
            theirs_ref[pl.ds(pl.multiple_of(i * 16, 16), 16), n * LANES : (n + 1) * LANES] = (
                jnp.concatenate([parts[0][n], parts[1][n]], axis=0).astype(jnp.bfloat16)
            )
        return carry

    lax.fori_loop(0, HALF // 16, rows, 0, unroll=2)


def spectrum_part(real_ref, pair_ref, row, place):
    at = pl.ds(pl.multiple_of(row, MINE), MINE)
    if place < 2:
        return real_ref[place, at, :LANES], real_ref[place, at, LANES:]
    n, side = (place - 2) // 2, place % 2
    plain = (side == 0) == (n < PAIRS // 2)
    under = pl.ds(pl.multiple_of(row + BLOCK, MINE), MINE)
    first = slice(2 * side * LANES, (2 * side + 1) * LANES)
    second = slice((2 * side + 1) * LANES, (2 * side + 2) * LANES)
    u_cos, u_sin = pair_ref[n, at, first], pair_ref[n, at, second]
    v_cos, v_sin = pair_ref[n, under, first], pair_ref[n, under, second]
    if plain:
        return u_cos + v_sin, u_sin - v_cos
    return u_cos - v_sin, u_sin + v_cos


def white_rows(real_ref, pair_ref, row):
    band = [None] * RADIX
    for place, residue in enumerate(ORDER):
        re, im = spectrum_part(real_ref, pair_ref, row, place)
        square = re * re + im * im
        band[place_in_band(residue)] = square * lax.rsqrt(jnp.maximum(square, 1e-30))
    total = band[0]
    for amplitude in band[1:]:
        total = total + amplitude
    floor = WATER / FREQS * jnp.sum(total, axis=1, keepdims=True) + 1e-05
    line = [pltpu.roll(a, 1, 1) for a in band[RADIX - SMOOTH :]]
    line = line + band + [pltpu.roll(a, LANES - 1, 1) for a in band[:SMOOTH]]
    two = [line[i] + line[i + 1] for i in range(len(line) - 1)]
    four = [two[i] + two[i + 2] for i in range(len(two) - 2)]
    out = []
    for place, residue in enumerate(ORDER):
        i = place_in_band(residue)
        smoothed = (four[i] + four[i + 4] + line[i + 8]) * (1.0 / (2 * SMOOTH + 1))
        level = smoothed + floor
        scale = pl.reciprocal(level, approx=True)
        scale = scale * (2.0 - level * scale)
        re, im = spectrum_part(real_ref, pair_ref, row, place)
        out += [re * scale, im * scale]
    return out


def own_kernel(pairs_ref, real_ref, pair_ref, mine_ref):
    core = lax.axis_index("tm")
    block = lax.axis_index("row") * PLANE + lax.axis_index("col")
    lane = lax.broadcasted_iota(jnp.int32, (MINE, LANES), 1)
    offsets = jnp.zeros((MINE, LANES), jnp.float32)
    for k in range(PARTNERS):
        partner = pairs_ref[0, k]
        offset = jnp.where(partner < 0, 0, partner - block).astype(jnp.float32)
        offsets = jnp.where(lane == PER + k, offset, offsets)

    def rows(j, carry):
        parts = white_rows(real_ref, pair_ref, core * HALF + j * MINE)
        parts[0] = jnp.where(lane >= PER, offsets, parts[0])
        for n, part in enumerate(parts):
            mine_ref[j, :, n * LANES : (n + 1) * LANES] = jnp.concatenate(
                [part, part], axis=0
            ).astype(jnp.bfloat16)
        return carry

    lax.fori_loop(0, PLANE, rows, 0, unroll=4)


def in_vmem(array):
    return pltpu.with_memory_space_constraint(array, pltpu.VMEM)


def spectra(series):
    hbm = pl.BlockSpec(memory_space=pltpu.HBM)
    vmem = pl.BlockSpec(memory_space=pltpu.VMEM)
    return pl.pallas_call(
        dft_kernel,
        in_specs=[hbm, hbm],
        out_specs=[vmem, vmem, vmem],
        out_shape=[
            pltpu.VMEM((HALF, WIDE), jnp.bfloat16),
            pltpu.VMEM((2, BLOCK, 2 * LANES), jnp.float32),
            pltpu.VMEM((PAIRS, 2 * BLOCK, 4 * LANES), jnp.float32),
        ],
        scratch_shapes=[
            pltpu.VMEM((BLOCK, SAMPLES), jnp.bfloat16),
            pltpu.VMEM((PAIRS + 1, PART, 4 * LANES), jnp.bfloat16),
            pltpu.VMEM((RADIX * BLOCK, PART), jnp.bfloat16),
            pltpu.SemaphoreType.DMA((CHUNKS,)),
            pltpu.SemaphoreType.DMA((PAIRS + 1,)),
        ],
        compiler_params=pltpu.CompilerParams(vmem_limit_bytes=20 << 20),
        name="dft_whiten",
    )(*[pltpu.with_memory_space_constraint(a, pltpu.HBM) for a in (series, jnp.asarray(dft_table()))])


def own_half(pairs, real, pair):
    vmem = pl.BlockSpec(memory_space=pltpu.VMEM)
    return pl.pallas_call(
        own_kernel,
        in_specs=[pl.BlockSpec(memory_space=pltpu.SMEM), vmem, vmem],
        out_specs=vmem,
        out_shape=pltpu.VMEM((PLANE, 2 * MINE, WIDE), jnp.bfloat16),
        compiler_params=pltpu.CompilerParams(vmem_limit_bytes=4 << 20),
        cost_estimate=pl.CostEstimate(
            flops=40 * HALF * WIDE, bytes_accessed=5 << 20, transcendentals=0
        ),
        name="whiten_own",
    )(pairs, in_vmem(real), in_vmem(pair))


def head_kernel(plane_ref, *halves):
    for part, half_ref in enumerate(halves):
        for i in range(REACH):
            half_ref[i] = plane_ref[i, :, part * HALF_WIDE : (part + 1) * HALF_WIDE]


def plane_head(plane):
    vmem = pl.BlockSpec(memory_space=pltpu.VMEM)
    return pl.pallas_call(
        head_kernel,
        in_specs=[vmem],
        out_specs=[vmem, vmem],
        out_shape=[pltpu.VMEM((REACH, 2 * MINE, HALF_WIDE), jnp.bfloat16)] * 2,
        compiler_params=pltpu.CompilerParams(vmem_limit_bytes=2 << 20),
        name="plane_head",
    )(in_vmem(plane))


def read_offsets(plane_ref, first_block, count, number_ref, scalar_ref, sem):
    for a in range(count):
        number_ref[a : a + 1, :] = (
            plane_ref[first_block + a, :, :LANES].astype(jnp.float32)[:1].astype(jnp.int32)
        )
    numbers = pltpu.make_async_copy(number_ref, scalar_ref, sem)
    numbers.start()
    return numbers


def cross_and_lag(count, columns, shift, taper_ref, w_ref, high_ref, low_ref, scalar_ref, xh_ref, xl_ref):
    def one_block(a, carry):
        seconds = [a + scalar_ref[a, PER + k] for k in range(PARTNERS)]
        for n in columns:
            here = 2 * n * LANES - shift

            def load(index):
                both = w_ref[index, :, here : here + 2 * LANES].astype(jnp.float32)
                return [
                    (both[w * MINE : (w + 1) * MINE, :LANES], both[w * MINE : (w + 1) * MINE, LANES:])
                    for w in range(WINDOWS)
                ]

            taper = taper_ref[n : n + 1, :]
            first = [(re * taper, im * taper) for re, im in load(a)]
            for slot in range(0, PARTNERS, 2):
                at = pl.ds(pl.multiple_of((a * PARTNERS + slot) * MINE, 16), 2 * MINE)
                re, im = [], []
                for k in (slot, slot + 1):
                    (a_re, a_im), (c_re, c_im) = first
                    (b_re, b_im), (d_re, d_im) = load(seconds[k])
                    re.append((a_re * b_re + a_im * b_im) + (c_re * d_re + c_im * d_im))
                    im.append((a_im * b_re - a_re * b_im) + (c_im * d_re - c_re * d_im))
                for side, both in enumerate((re, im)):
                    cross = jnp.concatenate(both, axis=0)
                    high = cross.astype(jnp.bfloat16)
                    where = slice(here + side * LANES, here + (side + 1) * LANES)
                    xh_ref[at, where] = high
                    xl_ref[at, where] = (cross - high.astype(jnp.float32)).astype(jnp.bfloat16)
        return carry

    lax.fori_loop(0, count, one_block, 0, unroll=True)
    rows = slice(shift, shift + xh_ref.shape[1])
    lagged = jnp.dot(xh_ref[...], high_ref[rows, :], preferred_element_type=jnp.float32)
    lagged += jnp.dot(xh_ref[...], low_ref[rows, :], preferred_element_type=jnp.float32)
    lagged += jnp.dot(xl_ref[...], high_ref[rows, :], preferred_element_type=jnp.float32)
    return lagged.reshape(count * PARTNERS, MINE, LAGS)


def store_lags(out_ref, first_block, count, scalar_ref, lagged):
    for i in range(count * PARTNERS):
        valid = scalar_ref[i // PARTNERS, PER + i % PARTNERS] > 0
        out_ref[first_block * PARTNERS + i] = jnp.where(valid, lagged[i], 0.0)


def inner_kernel(
    taper_ref, plane_ref, high_ref, low_ref, out_ref, number_ref, scalar_ref, sem, xh_ref, xl_ref
):
    read_offsets(plane_ref, 0, INNER, number_ref, scalar_ref, sem).wait()
    lagged = cross_and_lag(
        INNER, range(RADIX), 0, taper_ref, plane_ref, high_ref, low_ref, scalar_ref, xh_ref, xl_ref
    )
    store_lags(out_ref, 0, INNER, scalar_ref, lagged)


def halo_kernel(
    part,
    taper_ref,
    plane_ref,
    halo_ref,
    high_ref,
    low_ref,
    before_ref,
    out_ref,
    number_ref,
    scalar_ref,
    sem,
    xh_ref,
    xl_ref,
    w_ref,
):
    numbers = read_offsets(plane_ref, INNER, REACH, number_ref, scalar_ref, sem)
    shift = part * HALF_WIDE
    for i in range(REACH):
        w_ref[i] = plane_ref[INNER + i, :, shift : shift + HALF_WIDE]
        w_ref[REACH + i] = halo_ref[i]
    numbers.wait()
    columns = range(part * RADIX // 2, (part + 1) * RADIX // 2)
    lagged = cross_and_lag(
        REACH, columns, shift, taper_ref, w_ref, high_ref, low_ref, scalar_ref, xh_ref, xl_ref
    )
    if part == 0:
        out_ref[...] = lagged
    else:
        store_lags(out_ref, INNER, REACH, scalar_ref, lagged + before_ref[...])


def correlated_call(body, name, operands, out_blocks, count, width, aliases, extra):
    rows = count * PARTNERS * MINE
    vmem = pl.BlockSpec(memory_space=pltpu.VMEM)
    return pl.pallas_call(
        body,
        in_specs=[vmem] * len(operands),
        out_specs=vmem,
        out_shape=pltpu.VMEM((out_blocks * PARTNERS, MINE, LAGS), jnp.float32),
        scratch_shapes=[
            pltpu.VMEM((PLANE, LANES), jnp.int32),
            pltpu.SMEM((PLANE, LANES), jnp.int32),
            pltpu.SemaphoreType.DMA(()),
            pltpu.VMEM((rows, width), jnp.bfloat16),
            pltpu.VMEM((rows, width), jnp.bfloat16),
        ]
        + extra,
        input_output_aliases=aliases,
        compiler_params=pltpu.CompilerParams(vmem_limit_bytes=10 << 20),
        cost_estimate=pl.CostEstimate(
            flops=6 * rows * width * LAGS, bytes_accessed=4 << 20, transcendentals=0
        ),
        name=name,
    )(*[in_vmem(operand) for operand in operands])


def per_device(records, taper, pairs):
    theirs, real, pair = spectra(records[0])
    got = lax.ppermute(theirs, "tm", [(0, 1), (1, 0)])
    mine = own_half(pairs, real, pair)
    send = mine.at[:, MINE:].set(got.reshape(PLANE, MINE, WIDE))
    plane = lax.all_to_all(send, "col", 0, 0, tiled=True)
    count = lax.axis_size("row")
    down = [(z, z - 1) for z in range(1, count)]
    halos = [lax.ppermute(half, "row", down) for half in plane_head(plane)]
    plane, taper = lax.optimization_barrier((plane, taper))
    squared = taper_columns(taper)
    high, low = (jnp.asarray(table) for table in lag_tables())
    w = [pltpu.VMEM((2 * REACH, 2 * MINE, HALF_WIDE), jnp.bfloat16)]
    lagged = correlated_call(
        inner_kernel, "correlate_inner", [squared, plane, high, low], PLANE, INNER, WIDE, {}, []
    )

    def first(*refs):
        halo_kernel(0, *refs[:5], None, *refs[5:])

    def second(taper_ref, plane_ref, halo_ref, high_ref, low_ref, before_ref, _, *refs):
        halo_kernel(1, taper_ref, plane_ref, halo_ref, high_ref, low_ref, before_ref, *refs)

    partial = correlated_call(
        first,
        "correlate_halo_first",
        [squared, plane, halos[0], high, low],
        REACH,
        REACH,
        HALF_WIDE,
        {},
        w,
    )
    lagged = correlated_call(
        second,
        "correlate_halo_second",
        [squared, plane, halos[1], high, low, partial, lagged],
        PLANE,
        REACH,
        HALF_WIDE,
        {6: 0},
        w,
    )
    lagged = lagged.reshape(PLANE, PARTNERS, MINE, LAGS)
    back = lax.all_to_all(lagged.astype(jnp.bfloat16), "col", 0, 0, tiled=True).astype(jnp.float32)
    return back.transpose(1, 0, 2, 3).reshape(1, PARTNERS, HALF, LAGS)


def solution(mesh):
    return jax.shard_map(
        per_device,
        mesh=mesh,
        in_specs=(P("tm", ("row", "col"), None), P(), P(("row", "col"), None)),
        out_specs=P(("row", "col"), None, "tm", None),
        check_vma=False,
    )
```

```python
import math

import jax
import jax.numpy as jnp
import ml_dtypes
import numpy as np
from jax import lax
from jax.experimental import pallas as pl
from jax.experimental.pallas import tpu as pltpu
from jax.sharding import PartitionSpec as P

SAMPLES = 7680
FREQS = 1200
FIRST_BIN = 32
LAGS = 256
SMOOTH = 4
PARTNERS = 4
REACH = 7
BLOCK = 256
WINDOWS = 2
WATER = 0.3
RESCALE = 2.0

RADIX = 10
PART = SAMPLES // RADIX
HALF = BLOCK // 2
PER = FREQS // RADIX
LANES = 128
SPARE = LANES - PER
FULL = RADIX - 1
REST = PER - FULL * SPARE
TAIL = 2 * FULL
SIDE = LANES // 2
WIDE = (TAIL + 1) * LANES
HALO_PARTS = ((5, FULL, True), (0, 5, False))
ORDER = (0, 5, 2, 8, 4, 6, 3, 7, 1, 9)
PAIRS = len(ORDER) // 2 - 1
PLANE = 16
INNER = PLANE - REACH
MINE = HALF // PLANE
CHUNKS = 4


def residue_bins(residue):
    first = (residue - FIRST_BIN) % RADIX
    return FIRST_BIN + first + RADIX * np.arange(PER)


def place_in_band(residue):
    return (residue - FIRST_BIN) % RADIX


def angles(steps, residue):
    phase = steps[:, None] * residue_bins(residue)[None, :] % SAMPLES
    angle = phase * (2.0 * math.pi / SAMPLES)
    fill = ((0, 0), (0, LANES - PER))
    return np.concatenate([np.pad(np.cos(angle), fill), np.pad(-np.sin(angle), fill)], axis=1)


def dft_table():
    columns = [angles(np.arange(PART), residue) for residue in ORDER]
    chunks = [np.concatenate(columns[i : i + 2], axis=1) for i in range(0, RADIX, 2)]
    return np.stack(chunks).astype(np.float32).astype(ml_dtypes.bfloat16)


def lag_tables():
    lag_steps = np.arange(LAGS) - LAGS // 2 + SAMPLES
    factor = RESCALE / math.sqrt(FREQS * WINDOWS)
    rows = [angles(lag_steps, residue).T for residue in ORDER]
    last = rows[FULL].reshape(2, LANES, LAGS)
    for place in range(FULL):
        for side in range(2):
            spare = slice(side * LANES + PER, (side + 1) * LANES)
            rows[place][spare] = last[side, place * SPARE : (place + 1) * SPARE]
    tail = np.zeros((2, SIDE, LAGS))
    tail[:, :REST] = last[:, FULL * SPARE : PER]
    table = np.concatenate(rows[:FULL] + [tail.reshape(LANES, LAGS)]) * factor
    table = table.astype(np.float32)
    high = table.astype(ml_dtypes.bfloat16)
    low = (table - high.astype(np.float32)).astype(ml_dtypes.bfloat16)
    return high, low


def taper_columns(taper):
    parts = (taper * taper).reshape(PER, RADIX).T
    parts = [parts[place_in_band(residue)] for residue in ORDER]
    spare = parts[FULL][: FULL * SPARE].reshape(FULL, SPARE)
    full = jnp.concatenate([jnp.stack(parts[:FULL]), spare], axis=1)
    tail = jnp.pad(parts[FULL][FULL * SPARE :], (0, SIDE - REST))
    return jnp.concatenate([full, jnp.concatenate([tail, tail])[None]], axis=0)


def five_point(x):
    cos = [math.cos(2.0 * math.pi * k / 5) for k in (1, 2)]
    sin = [math.sin(2.0 * math.pi * k / 5) for k in (1, 2)]
    near, far = x[1] + x[4], x[2] + x[3]
    near_gap, far_gap = x[1] - x[4], x[2] - x[3]
    return (
        x[0] + near + far,
        x[0] + cos[0] * near + cos[1] * far,
        sin[0] * near_gap + sin[1] * far_gap,
        x[0] + cos[1] * near + cos[0] * far,
        sin[1] * near_gap - sin[0] * far_gap,
    )


def dft_kernel(
    x_hbm, table_hbm, theirs_ref, real_ref, pair_ref, x_ref, table_ref, y_ref, x_sems, t_sems
):
    core = lax.axis_index("tm")
    size = BLOCK // CHUNKS
    x_copies = [
        pltpu.make_async_copy(
            x_hbm.at[pl.ds(c * size, size)], x_ref.at[pl.ds(c * size, size)], x_sems.at[c]
        )
        for c in range(CHUNKS)
    ]
    t_copies = [
        pltpu.make_async_copy(table_hbm.at[c], table_ref.at[c], t_sems.at[c])
        for c in range(PAIRS + 1)
    ]
    for copy in x_copies:
        copy.start()

    def split(i, carry):
        at = pl.ds(pl.multiple_of(i * 16, 16), 16)
        for lane in range(0, PART, LANES):
            x = [
                x_ref[at, n * PART + lane : n * PART + lane + LANES].astype(jnp.float32)
                for n in range(RADIX)
            ]
            even = five_point([x[n] + x[n + 5] for n in range(5)])
            odd = five_point([x[n] - x[n + 5] if n % 2 == 0 else x[n + 5] - x[n] for n in range(5)])
            parts = (even[0], odd[0]) + even[1:] + odd[1:]
            for n, part in enumerate(parts):
                y_ref[
                    pl.ds(pl.multiple_of(n * BLOCK + i * 16, 16), 16), lane : lane + LANES
                ] = part.astype(jnp.bfloat16)
        return carry

    for c in range(CHUNKS):
        x_copies[c].wait()
        if c == CHUNKS - 2:
            for copy in t_copies:
                copy.start()
        lax.fori_loop(c * size // 16, (c + 1) * size // 16, split, 0, unroll=2)

    t_copies[0].wait()
    for n in range(2):
        real_ref[n] = jnp.dot(
            y_ref[n * BLOCK : (n + 1) * BLOCK, :],
            table_ref[0, :, n * 2 * LANES : (n + 1) * 2 * LANES],
            preferred_element_type=jnp.float32,
        )
    for n in range(PAIRS):
        t_copies[n + 1].wait()
        pair_ref[n] = jnp.dot(
            y_ref[(n + 1) * 2 * BLOCK : (n + 2) * 2 * BLOCK, :],
            table_ref[n + 1],
            preferred_element_type=jnp.float32,
        )

    def rows(i, carry):
        row = (1 - core) * HALF + i * 16
        parts = [white_rows(real_ref, pair_ref, row + j * MINE) for j in range(2)]
        for n in range(TAIL + 1):
            theirs_ref[pl.ds(pl.multiple_of(i * 16, 16), 16), n * LANES : (n + 1) * LANES] = (
                jnp.concatenate([parts[0][n], parts[1][n]], axis=0).astype(jnp.bfloat16)
            )
        return carry

    lax.fori_loop(0, HALF // 16, rows, 0, unroll=2)


def spectrum_part(real_ref, pair_ref, row, place):
    at = pl.ds(pl.multiple_of(row, MINE), MINE)
    if place < 2:
        return real_ref[place, at, :LANES], real_ref[place, at, LANES:]
    n, side = (place - 2) // 2, place % 2
    plain = (side == 0) == (n < PAIRS // 2)
    under = pl.ds(pl.multiple_of(row + BLOCK, MINE), MINE)
    first = slice(2 * side * LANES, (2 * side + 1) * LANES)
    second = slice((2 * side + 1) * LANES, (2 * side + 2) * LANES)
    u_cos, u_sin = pair_ref[n, at, first], pair_ref[n, at, second]
    v_cos, v_sin = pair_ref[n, under, first], pair_ref[n, under, second]
    if plain:
        return u_cos + v_sin, u_sin - v_cos
    return u_cos - v_sin, u_sin + v_cos


def white_rows(real_ref, pair_ref, row):
    band = [None] * RADIX
    for place, residue in enumerate(ORDER):
        re, im = spectrum_part(real_ref, pair_ref, row, place)
        square = re * re + im * im
        band[place_in_band(residue)] = square * lax.rsqrt(jnp.maximum(square, 1e-30))
    total = band[0]
    for amplitude in band[1:]:
        total = total + amplitude
    floor = WATER / FREQS * jnp.sum(total, axis=1, keepdims=True) + 1e-05
    line = [pltpu.roll(a, 1, 1) for a in band[RADIX - SMOOTH :]]
    line = line + band + [pltpu.roll(a, LANES - 1, 1) for a in band[:SMOOTH]]
    two = [line[i] + line[i + 1] for i in range(len(line) - 1)]
    four = [two[i] + two[i + 2] for i in range(len(two) - 2)]
    out = []
    for place, residue in enumerate(ORDER):
        i = place_in_band(residue)
        smoothed = (four[i] + four[i + 4] + line[i + 8]) * (1.0 / (2 * SMOOTH + 1))
        level = smoothed + floor
        scale = pl.reciprocal(level, approx=True)
        scale = scale * (2.0 - level * scale)
        re, im = spectrum_part(real_ref, pair_ref, row, place)
        out += [re * scale, im * scale]
    lane = lax.broadcasted_iota(jnp.int32, (MINE, LANES), 1)
    last = out[TAIL:]
    for place in range(FULL):
        for side in range(2):
            moved = pltpu.roll(last[side], PER - place * SPARE, 1)
            here = 2 * place + side
            out[here] = jnp.where(lane >= PER, moved, out[here])
    moved = [pltpu.roll(last[0], LANES - FULL * SPARE, 1), pltpu.roll(last[1], LANES + SIDE - FULL * SPARE, 1)]
    return out[:TAIL] + [jnp.where(lane < SIDE, moved[0], moved[1])]


def own_kernel(pairs_ref, real_ref, pair_ref, mine_ref):
    core = lax.axis_index("tm")
    block = lax.axis_index("row") * PLANE + lax.axis_index("col")
    lane = lax.broadcasted_iota(jnp.int32, (MINE, LANES), 1)
    offsets = jnp.zeros((MINE, LANES), jnp.float32)
    for k in range(PARTNERS):
        partner = pairs_ref[0, k]
        offset = jnp.where(partner < 0, 0, partner - block).astype(jnp.float32)
        offsets = jnp.where(lane == REST + k, offset, offsets)

    def rows(j, carry):
        parts = white_rows(real_ref, pair_ref, core * HALF + j * MINE)
        parts[TAIL] = jnp.where((lane >= REST) & (lane < SIDE), offsets, parts[TAIL])
        for n, part in enumerate(parts):
            mine_ref[j, :, n * LANES : (n + 1) * LANES] = jnp.concatenate(
                [part, part], axis=0
            ).astype(jnp.bfloat16)
        return carry

    lax.fori_loop(0, PLANE, rows, 0, unroll=4)


def in_vmem(array):
    return pltpu.with_memory_space_constraint(array, pltpu.VMEM)


def spectra(series):
    hbm = pl.BlockSpec(memory_space=pltpu.HBM)
    vmem = pl.BlockSpec(memory_space=pltpu.VMEM)
    return pl.pallas_call(
        dft_kernel,
        in_specs=[hbm, hbm],
        out_specs=[vmem, vmem, vmem],
        out_shape=[
            pltpu.VMEM((HALF, WIDE), jnp.bfloat16),
            pltpu.VMEM((2, BLOCK, 2 * LANES), jnp.float32),
            pltpu.VMEM((PAIRS, 2 * BLOCK, 4 * LANES), jnp.float32),
        ],
        scratch_shapes=[
            pltpu.VMEM((BLOCK, SAMPLES), jnp.bfloat16),
            pltpu.VMEM((PAIRS + 1, PART, 4 * LANES), jnp.bfloat16),
            pltpu.VMEM((RADIX * BLOCK, PART), jnp.bfloat16),
            pltpu.SemaphoreType.DMA((CHUNKS,)),
            pltpu.SemaphoreType.DMA((PAIRS + 1,)),
        ],
        compiler_params=pltpu.CompilerParams(vmem_limit_bytes=20 << 20),
        name="dft_whiten",
    )(*[pltpu.with_memory_space_constraint(a, pltpu.HBM) for a in (series, jnp.asarray(dft_table()))])


def own_half(pairs, real, pair):
    vmem = pl.BlockSpec(memory_space=pltpu.VMEM)
    return pl.pallas_call(
        own_kernel,
        in_specs=[pl.BlockSpec(memory_space=pltpu.SMEM), vmem, vmem],
        out_specs=vmem,
        out_shape=pltpu.VMEM((PLANE, 2 * MINE, WIDE), jnp.bfloat16),
        compiler_params=pltpu.CompilerParams(vmem_limit_bytes=4 << 20),
        cost_estimate=pl.CostEstimate(
            flops=40 * HALF * WIDE, bytes_accessed=5 << 20, transcendentals=0
        ),
        name="whiten_own",
    )(pairs, in_vmem(real), in_vmem(pair))


def part_columns(part):
    begin, end, tail = part
    return slice(2 * begin * LANES, (2 * end + tail) * LANES)


def part_width(part):
    columns = part_columns(part)
    return columns.stop - columns.start


def head_kernel(plane_ref, *halves):
    for part, half_ref in zip(HALO_PARTS, halves):
        for i in range(REACH):
            half_ref[i] = plane_ref[i, :, part_columns(part)]


def plane_head(plane):
    vmem = pl.BlockSpec(memory_space=pltpu.VMEM)
    return pl.pallas_call(
        head_kernel,
        in_specs=[vmem],
        out_specs=[vmem, vmem],
        out_shape=[
            pltpu.VMEM((REACH, 2 * MINE, part_width(part)), jnp.bfloat16) for part in HALO_PARTS
        ],
        compiler_params=pltpu.CompilerParams(vmem_limit_bytes=2 << 20),
        name="plane_head",
    )(in_vmem(plane))


def read_offsets(plane_ref, first_block, count, number_ref, scalar_ref, sem):
    for a in range(count):
        number_ref[a : a + 1, :] = (
            plane_ref[first_block + a, :, TAIL * LANES :].astype(jnp.float32)[:1].astype(jnp.int32)
        )
    numbers = pltpu.make_async_copy(number_ref, scalar_ref, sem)
    numbers.start()
    return numbers


def cross_and_lag(count, part, taper_ref, w_ref, high_ref, low_ref, scalar_ref, xh_ref, xl_ref):
    begin, end, with_tail = part
    shift = 2 * begin * LANES
    low_side = lax.broadcasted_iota(jnp.int32, (MINE, LANES), 1) < SIDE

    def one_block(a, carry):
        seconds = [a + scalar_ref[a, REST + k] for k in range(PARTNERS)]

        def load(index, block, blocks):
            here = block * LANES - shift
            both = w_ref[index, :, here : here + blocks * LANES].astype(jnp.float32)
            return [both[w * MINE : (w + 1) * MINE] for w in range(WINDOWS)]

        def store(slot, block, both):
            at = pl.ds(pl.multiple_of((a * PARTNERS + slot) * MINE, 16), 2 * MINE)
            columns = slice(block * LANES - shift, (block + 1) * LANES - shift)
            cross = jnp.concatenate(both, axis=0)
            high = cross.astype(jnp.bfloat16)
            xh_ref[at, columns] = high
            xl_ref[at, columns] = (cross - high.astype(jnp.float32)).astype(jnp.bfloat16)

        for n in range(begin, end):
            taper = taper_ref[n : n + 1, :]
            first = [(x[:, :LANES] * taper, x[:, LANES:] * taper) for x in load(a, 2 * n, 2)]
            for slot in range(0, PARTNERS, 2):
                re, im = [], []
                for k in (slot, slot + 1):
                    (a_re, a_im), (c_re, c_im) = first
                    (b_re, b_im), (d_re, d_im) = [
                        (x[:, :LANES], x[:, LANES:]) for x in load(seconds[k], 2 * n, 2)
                    ]
                    re.append((a_re * b_re + a_im * b_im) + (c_re * d_re + c_im * d_im))
                    im.append((a_im * b_re - a_re * b_im) + (c_im * d_re - c_re * d_im))
                store(slot, 2 * n, re)
                store(slot, 2 * n + 1, im)
        if with_tail:
            taper = taper_ref[FULL : FULL + 1, :]
            first = [x * taper for x in load(a, TAIL, 1)]
            for slot in range(0, PARTNERS, 2):
                both = []
                for k in (slot, slot + 1):
                    second = load(seconds[k], TAIL, 1)
                    straight = first[0] * second[0] + first[1] * second[1]
                    crossed = first[0] * pltpu.roll(second[0], SIDE, 1)
                    crossed = crossed + first[1] * pltpu.roll(second[1], SIDE, 1)
                    both.append(
                        jnp.where(
                            low_side,
                            straight + pltpu.roll(straight, SIDE, 1),
                            crossed - pltpu.roll(crossed, SIDE, 1),
                        )
                    )
                store(slot, TAIL, both)
        return carry

    lax.fori_loop(0, count, one_block, 0, unroll=True)
    rows = part_columns(part)
    lagged = jnp.dot(xh_ref[...], high_ref[rows, :], preferred_element_type=jnp.float32)
    lagged += jnp.dot(xh_ref[...], low_ref[rows, :], preferred_element_type=jnp.float32)
    lagged += jnp.dot(xl_ref[...], high_ref[rows, :], preferred_element_type=jnp.float32)
    return lagged.reshape(count * PARTNERS, MINE, LAGS)


def store_lags(out_ref, first_block, count, scalar_ref, lagged):
    for i in range(count * PARTNERS):
        valid = scalar_ref[i // PARTNERS, REST + i % PARTNERS] > 0
        out_ref[first_block * PARTNERS + i] = jnp.where(valid, lagged[i], 0.0)


def inner_kernel(
    taper_ref, plane_ref, high_ref, low_ref, out_ref, number_ref, scalar_ref, sem, xh_ref, xl_ref
):
    read_offsets(plane_ref, 0, INNER, number_ref, scalar_ref, sem).wait()
    lagged = cross_and_lag(
        INNER, (0, FULL, True), taper_ref, plane_ref, high_ref, low_ref, scalar_ref, xh_ref, xl_ref
    )
    store_lags(out_ref, 0, INNER, scalar_ref, lagged)


def halo_kernel(
    part,
    taper_ref,
    plane_ref,
    halo_ref,
    high_ref,
    low_ref,
    before_ref,
    out_ref,
    number_ref,
    scalar_ref,
    sem,
    xh_ref,
    xl_ref,
    w_ref,
):
    numbers = read_offsets(plane_ref, INNER, REACH, number_ref, scalar_ref, sem)
    for i in range(REACH):
        w_ref[i] = plane_ref[INNER + i, :, part_columns(part)]
        w_ref[REACH + i] = halo_ref[i]
    numbers.wait()
    lagged = cross_and_lag(
        REACH, part, taper_ref, w_ref, high_ref, low_ref, scalar_ref, xh_ref, xl_ref
    )
    if before_ref is None:
        out_ref[...] = lagged
    else:
        store_lags(out_ref, INNER, REACH, scalar_ref, lagged + before_ref[...])


def correlated_call(body, name, operands, out_blocks, count, width, aliases, extra):
    rows = count * PARTNERS * MINE
    vmem = pl.BlockSpec(memory_space=pltpu.VMEM)
    return pl.pallas_call(
        body,
        in_specs=[vmem] * len(operands),
        out_specs=vmem,
        out_shape=pltpu.VMEM((out_blocks * PARTNERS, MINE, LAGS), jnp.float32),
        scratch_shapes=[
            pltpu.VMEM((PLANE, LANES), jnp.int32),
            pltpu.SMEM((PLANE, LANES), jnp.int32),
            pltpu.SemaphoreType.DMA(()),
            pltpu.VMEM((rows, width), jnp.bfloat16),
            pltpu.VMEM((rows, width), jnp.bfloat16),
        ]
        + extra,
        input_output_aliases=aliases,
        compiler_params=pltpu.CompilerParams(vmem_limit_bytes=10 << 20),
        cost_estimate=pl.CostEstimate(
            flops=6 * rows * width * LAGS, bytes_accessed=4 << 20, transcendentals=0
        ),
        name=name,
    )(*[in_vmem(operand) for operand in operands])


def per_device(records, taper, pairs):
    theirs, real, pair = spectra(records[0])
    got = lax.ppermute(theirs, "tm", [(0, 1), (1, 0)])
    mine = own_half(pairs, real, pair)
    send = mine.at[:, MINE:].set(got.reshape(PLANE, MINE, WIDE))
    plane = lax.all_to_all(send, "col", 0, 0, tiled=True)
    count = lax.axis_size("row")
    down = [(z, z - 1) for z in range(1, count)]
    halos = [lax.ppermute(half, "row", down) for half in plane_head(plane)]
    plane, taper = lax.optimization_barrier((plane, taper))
    squared = taper_columns(taper)
    high, low = (jnp.asarray(table) for table in lag_tables())
    widths = [part_width(part) for part in HALO_PARTS]
    w = [[pltpu.VMEM((2 * REACH, 2 * MINE, width), jnp.bfloat16)] for width in widths]
    lagged = correlated_call(
        inner_kernel, "correlate_inner", [squared, plane, high, low], PLANE, INNER, WIDE, {}, []
    )

    def first(*refs):
        halo_kernel(HALO_PARTS[0], *refs[:5], None, *refs[5:])

    def second(taper_ref, plane_ref, halo_ref, high_ref, low_ref, before_ref, _, *refs):
        halo_kernel(
            HALO_PARTS[1], taper_ref, plane_ref, halo_ref, high_ref, low_ref, before_ref, *refs
        )

    partial = correlated_call(
        first,
        "correlate_halo_first",
        [squared, plane, halos[0], high, low],
        REACH,
        REACH,
        widths[0],
        {},
        w[0],
    )
    lagged = correlated_call(
        second,
        "correlate_halo_second",
        [squared, plane, halos[1], high, low, partial, lagged],
        PLANE,
        REACH,
        widths[1],
        {6: 0},
        w[1],
    )
    lagged = lagged.reshape(PLANE, PARTNERS, MINE, LAGS)
    back = lax.all_to_all(lagged.astype(jnp.bfloat16), "col", 0, 0, tiled=True).astype(jnp.float32)
    return back.transpose(1, 0, 2, 3).reshape(1, PARTNERS, HALF, LAGS)


def solution(mesh):
    return jax.shard_map(
        per_device,
        mesh=mesh,
        in_specs=(P("tm", ("row", "col"), None), P(), P(("row", "col"), None)),
        out_specs=P(("row", "col"), None, "tm", None),
        check_vma=False,
    )
```

```python
import math

import jax
import jax.numpy as jnp
import ml_dtypes
import numpy as np
from jax import lax
from jax.experimental import pallas as pl
from jax.experimental.pallas import tpu as pltpu
from jax.sharding import PartitionSpec as P

SAMPLES = 7680
FREQS = 1200
FIRST_BIN = 32
LAGS = 256
SMOOTH = 4
PARTNERS = 4
REACH = 7
BLOCK = 256
WINDOWS = 2
WATER = 0.3
RESCALE = 2.0

RADIX = 10
PART = SAMPLES // RADIX
HALF = BLOCK // 2
PER = FREQS // RADIX
LANES = 128
SPARE = LANES - PER
FULL = RADIX - 1
REST = PER - FULL * SPARE
TAIL = 2 * FULL
SIDE = LANES // 2
WIDE = (TAIL + 1) * LANES
HALO_PARTS = ((3, FULL, True), (0, 3, False))
ORDER = (0, 5, 2, 8, 4, 6, 3, 7, 1, 9)
PAIRS = len(ORDER) // 2 - 1
PLANE = 16
INNER = PLANE - REACH
MINE = HALF // PLANE
CHUNKS = 4


def residue_bins(residue):
    first = (residue - FIRST_BIN) % RADIX
    return FIRST_BIN + first + RADIX * np.arange(PER)


def place_in_band(residue):
    return (residue - FIRST_BIN) % RADIX


def angles(steps, residue):
    phase = steps[:, None] * residue_bins(residue)[None, :] % SAMPLES
    angle = phase * (2.0 * math.pi / SAMPLES)
    fill = ((0, 0), (0, LANES - PER))
    return np.concatenate([np.pad(np.cos(angle), fill), np.pad(-np.sin(angle), fill)], axis=1)


def dft_table():
    columns = [angles(np.arange(PART), residue) for residue in ORDER]
    chunks = [np.concatenate(columns[i : i + 2], axis=1) for i in range(0, RADIX, 2)]
    return np.stack(chunks).astype(np.float32).astype(ml_dtypes.bfloat16)


def lag_tables():
    lag_steps = np.arange(LAGS) - LAGS // 2 + SAMPLES
    factor = RESCALE / math.sqrt(FREQS * WINDOWS)
    rows = [angles(lag_steps, residue).T for residue in ORDER]
    last = rows[FULL].reshape(2, LANES, LAGS)
    for place in range(FULL):
        for side in range(2):
            spare = slice(side * LANES + PER, (side + 1) * LANES)
            rows[place][spare] = last[side, place * SPARE : (place + 1) * SPARE]
    tail = np.zeros((2, SIDE, LAGS))
    tail[:, :REST] = last[:, FULL * SPARE : PER]
    table = np.concatenate(rows[:FULL] + [tail.reshape(LANES, LAGS)]) * factor
    table = table.astype(np.float32)
    high = table.astype(ml_dtypes.bfloat16)
    low = (table - high.astype(np.float32)).astype(ml_dtypes.bfloat16)
    return high, low


def taper_columns(squared):
    parts = squared.reshape(PER, RADIX).T
    parts = [parts[place_in_band(residue)] for residue in ORDER]
    spare = parts[FULL][: FULL * SPARE].reshape(FULL, SPARE)
    full = jnp.concatenate([jnp.stack(parts[:FULL]), spare], axis=1)
    tail = jnp.pad(parts[FULL][FULL * SPARE :], (0, SIDE - REST))
    return jnp.concatenate([full, jnp.concatenate([tail, tail])[None]], axis=0)


def five_point(x):
    cos = [math.cos(2.0 * math.pi * k / 5) for k in (1, 2)]
    sin = [math.sin(2.0 * math.pi * k / 5) for k in (1, 2)]
    near, far = x[1] + x[4], x[2] + x[3]
    near_gap, far_gap = x[1] - x[4], x[2] - x[3]
    return (
        x[0] + near + far,
        x[0] + cos[0] * near + cos[1] * far,
        sin[0] * near_gap + sin[1] * far_gap,
        x[0] + cos[1] * near + cos[0] * far,
        sin[1] * near_gap - sin[0] * far_gap,
    )


def dft_kernel(
    x_hbm, table_hbm, theirs_ref, real_ref, pair_ref, x_ref, table_ref, y_ref, x_sems, t_sems
):
    core = lax.axis_index("tm")
    size = BLOCK // CHUNKS
    x_copies = [
        pltpu.make_async_copy(
            x_hbm.at[pl.ds(c * size, size)], x_ref.at[pl.ds(c * size, size)], x_sems.at[c]
        )
        for c in range(CHUNKS)
    ]
    t_copies = [
        pltpu.make_async_copy(table_hbm.at[c], table_ref.at[c], t_sems.at[c])
        for c in range(PAIRS + 1)
    ]
    for copy in x_copies:
        copy.start()

    def split(i, carry):
        at = pl.ds(pl.multiple_of(i * 16, 16), 16)
        for lane in range(0, PART, LANES):
            x = [
                x_ref[at, n * PART + lane : n * PART + lane + LANES].astype(jnp.float32)
                for n in range(RADIX)
            ]
            even = five_point([x[n] + x[n + 5] for n in range(5)])
            odd = five_point([x[n] - x[n + 5] if n % 2 == 0 else x[n + 5] - x[n] for n in range(5)])
            parts = (even[0], odd[0]) + even[1:] + odd[1:]
            for n, part in enumerate(parts):
                y_ref[
                    pl.ds(pl.multiple_of(n * BLOCK + i * 16, 16), 16), lane : lane + LANES
                ] = part.astype(jnp.bfloat16)
        return carry

    for c in range(CHUNKS):
        x_copies[c].wait()
        if c == CHUNKS - 2:
            for copy in t_copies:
                copy.start()
        lax.fori_loop(c * size // 16, (c + 1) * size // 16, split, 0, unroll=2)

    t_copies[0].wait()
    for n in range(2):
        real_ref[n] = jnp.dot(
            y_ref[n * BLOCK : (n + 1) * BLOCK, :],
            table_ref[0, :, n * 2 * LANES : (n + 1) * 2 * LANES],
            preferred_element_type=jnp.float32,
        )
    for n in range(PAIRS):
        t_copies[n + 1].wait()
        pair_ref[n] = jnp.dot(
            y_ref[(n + 1) * 2 * BLOCK : (n + 2) * 2 * BLOCK, :],
            table_ref[n + 1],
            preferred_element_type=jnp.float32,
        )

    def rows(i, carry):
        row = (1 - core) * HALF + i * 16
        parts = [white_rows(real_ref, pair_ref, row + j * MINE) for j in range(2)]
        for n in range(TAIL + 1):
            theirs_ref[pl.ds(pl.multiple_of(i * 16, 16), 16), n * LANES : (n + 1) * LANES] = (
                jnp.concatenate([parts[0][n], parts[1][n]], axis=0).astype(jnp.bfloat16)
            )
        return carry

    lax.fori_loop(0, HALF // 16, rows, 0, unroll=2)


def spectrum_part(real_ref, pair_ref, row, place):
    at = pl.ds(pl.multiple_of(row, MINE), MINE)
    if place < 2:
        return real_ref[place, at, :LANES], real_ref[place, at, LANES:]
    n, side = (place - 2) // 2, place % 2
    plain = (side == 0) == (n < PAIRS // 2)
    under = pl.ds(pl.multiple_of(row + BLOCK, MINE), MINE)
    first = slice(2 * side * LANES, (2 * side + 1) * LANES)
    second = slice((2 * side + 1) * LANES, (2 * side + 2) * LANES)
    u_cos, u_sin = pair_ref[n, at, first], pair_ref[n, at, second]
    v_cos, v_sin = pair_ref[n, under, first], pair_ref[n, under, second]
    if plain:
        return u_cos + v_sin, u_sin - v_cos
    return u_cos - v_sin, u_sin + v_cos


def white_rows(real_ref, pair_ref, row):
    band = [None] * RADIX
    for place, residue in enumerate(ORDER):
        re, im = spectrum_part(real_ref, pair_ref, row, place)
        square = re * re + im * im
        band[place_in_band(residue)] = square * lax.rsqrt(jnp.maximum(square, 1e-30))
    total = band[0]
    for amplitude in band[1:]:
        total = total + amplitude
    floor = WATER / FREQS * jnp.sum(total, axis=1, keepdims=True) + 1e-05
    line = [pltpu.roll(a, 1, 1) for a in band[RADIX - SMOOTH :]]
    line = line + band + [pltpu.roll(a, LANES - 1, 1) for a in band[:SMOOTH]]
    two = [line[i] + line[i + 1] for i in range(len(line) - 1)]
    four = [two[i] + two[i + 2] for i in range(len(two) - 2)]
    out = []
    for place, residue in enumerate(ORDER):
        i = place_in_band(residue)
        smoothed = (four[i] + four[i + 4] + line[i + 8]) * (1.0 / (2 * SMOOTH + 1))
        level = smoothed + floor
        scale = pl.reciprocal(level, approx=True)
        scale = scale * (2.0 - level * scale)
        re, im = spectrum_part(real_ref, pair_ref, row, place)
        out += [re * scale, im * scale]
    lane = lax.broadcasted_iota(jnp.int32, (MINE, LANES), 1)
    last = out[TAIL:]
    for place in range(FULL):
        for side in range(2):
            moved = pltpu.roll(last[side], PER - place * SPARE, 1)
            here = 2 * place + side
            out[here] = jnp.where(lane >= PER, moved, out[here])
    moved = [pltpu.roll(last[0], LANES - FULL * SPARE, 1), pltpu.roll(last[1], LANES + SIDE - FULL * SPARE, 1)]
    return out[:TAIL] + [jnp.where(lane < SIDE, moved[0], moved[1])]


def own_kernel(pairs_ref, taper_ref, real_ref, pair_ref, mine_ref, squared_ref):
    squared_ref[...] = taper_ref[...] * taper_ref[...]
    core = lax.axis_index("tm")
    block = lax.axis_index("row") * PLANE + lax.axis_index("col")
    lane = lax.broadcasted_iota(jnp.int32, (MINE, LANES), 1)
    offsets = jnp.zeros((MINE, LANES), jnp.float32)
    for k in range(PARTNERS):
        partner = pairs_ref[0, k]
        offset = jnp.where(partner < 0, 0, partner - block).astype(jnp.float32)
        offsets = jnp.where(lane == REST + k, offset, offsets)

    def rows(j, carry):
        parts = white_rows(real_ref, pair_ref, core * HALF + j * MINE)
        parts[TAIL] = jnp.where((lane >= REST) & (lane < SIDE), offsets, parts[TAIL])
        for n, part in enumerate(parts):
            mine_ref[j, :, n * LANES : (n + 1) * LANES] = jnp.concatenate(
                [part, part], axis=0
            ).astype(jnp.bfloat16)
        return carry

    lax.fori_loop(0, PLANE, rows, 0, unroll=4)


def in_vmem(array):
    return pltpu.with_memory_space_constraint(array, pltpu.VMEM)


def spectra(series):
    hbm = pl.BlockSpec(memory_space=pltpu.HBM)
    vmem = pl.BlockSpec(memory_space=pltpu.VMEM)
    return pl.pallas_call(
        dft_kernel,
        in_specs=[hbm, hbm],
        out_specs=[vmem, vmem, vmem],
        out_shape=[
            pltpu.VMEM((HALF, WIDE), jnp.bfloat16),
            pltpu.VMEM((2, BLOCK, 2 * LANES), jnp.float32),
            pltpu.VMEM((PAIRS, 2 * BLOCK, 4 * LANES), jnp.float32),
        ],
        scratch_shapes=[
            pltpu.VMEM((BLOCK, SAMPLES), jnp.bfloat16),
            pltpu.VMEM((PAIRS + 1, PART, 4 * LANES), jnp.bfloat16),
            pltpu.VMEM((RADIX * BLOCK, PART), jnp.bfloat16),
            pltpu.SemaphoreType.DMA((CHUNKS,)),
            pltpu.SemaphoreType.DMA((PAIRS + 1,)),
        ],
        compiler_params=pltpu.CompilerParams(vmem_limit_bytes=20 << 20),
        name="dft_whiten",
    )(*[pltpu.with_memory_space_constraint(a, pltpu.HBM) for a in (series, jnp.asarray(dft_table()))])


def own_half(pairs, taper, real, pair):
    vmem = pl.BlockSpec(memory_space=pltpu.VMEM)
    return pl.pallas_call(
        own_kernel,
        in_specs=[pl.BlockSpec(memory_space=pltpu.SMEM), vmem, vmem, vmem],
        out_specs=[vmem, vmem],
        out_shape=[
            pltpu.VMEM((PLANE, 2 * MINE, WIDE), jnp.bfloat16),
            pltpu.VMEM((FREQS,), jnp.float32),
        ],
        compiler_params=pltpu.CompilerParams(vmem_limit_bytes=4 << 20),
        cost_estimate=pl.CostEstimate(
            flops=40 * HALF * WIDE, bytes_accessed=5 << 20, transcendentals=0
        ),
        name="whiten_own",
    )(pairs, taper, in_vmem(real), in_vmem(pair))


def part_columns(part):
    begin, end, tail = part
    return slice(2 * begin * LANES, (2 * end + tail) * LANES)


def part_width(part):
    columns = part_columns(part)
    return columns.stop - columns.start


def plane_head(plane, part):
    vmem = pl.BlockSpec(memory_space=pltpu.VMEM)

    def body(plane_ref, head_ref):
        for i in range(REACH):
            head_ref[i] = plane_ref[i, :, part_columns(part)]

    return pl.pallas_call(
        body,
        in_specs=[vmem],
        out_specs=vmem,
        out_shape=pltpu.VMEM((REACH, 2 * MINE, part_width(part)), jnp.bfloat16),
        compiler_params=pltpu.CompilerParams(vmem_limit_bytes=2 << 20),
        name="plane_head",
    )(in_vmem(plane))


def cross_and_lag(
    first_block, count, part, taper_ref, w_ref, high_ref, low_ref, scalar_ref, xh_ref, xl_ref
):
    begin, end, with_tail = part
    shift = 2 * begin * LANES
    low_side = lax.broadcasted_iota(jnp.int32, (MINE, LANES), 1) < SIDE

    def one_block(a, carry):
        seconds = [a + scalar_ref[first_block + a, REST + k] for k in range(PARTNERS)]

        def load(index, block, blocks):
            here = block * LANES - shift
            both = w_ref[index, :, here : here + blocks * LANES].astype(jnp.float32)
            return [both[w * MINE : (w + 1) * MINE] for w in range(WINDOWS)]

        def store(slot, block, both):
            at = pl.ds(pl.multiple_of((a * PARTNERS + slot) * MINE, 16), 2 * MINE)
            columns = slice(block * LANES - shift, (block + 1) * LANES - shift)
            cross = jnp.concatenate(both, axis=0)
            high = cross.astype(jnp.bfloat16)
            xh_ref[at, columns] = high
            xl_ref[at, columns] = (cross - high.astype(jnp.float32)).astype(jnp.bfloat16)

        for n in range(begin, end):
            taper = taper_ref[n : n + 1, :]
            first = [(x[:, :LANES] * taper, x[:, LANES:] * taper) for x in load(a, 2 * n, 2)]
            for slot in range(0, PARTNERS, 2):
                re, im = [], []
                for k in (slot, slot + 1):
                    (a_re, a_im), (c_re, c_im) = first
                    (b_re, b_im), (d_re, d_im) = [
                        (x[:, :LANES], x[:, LANES:]) for x in load(seconds[k], 2 * n, 2)
                    ]
                    re.append((a_re * b_re + a_im * b_im) + (c_re * d_re + c_im * d_im))
                    im.append((a_im * b_re - a_re * b_im) + (c_im * d_re - c_re * d_im))
                store(slot, 2 * n, re)
                store(slot, 2 * n + 1, im)
        if with_tail:
            taper = taper_ref[FULL : FULL + 1, :]
            first = [x * taper for x in load(a, TAIL, 1)]
            for slot in range(0, PARTNERS, 2):
                both = []
                for k in (slot, slot + 1):
                    second = load(seconds[k], TAIL, 1)
                    straight = first[0] * second[0] + first[1] * second[1]
                    crossed = first[0] * pltpu.roll(second[0], SIDE, 1)
                    crossed = crossed + first[1] * pltpu.roll(second[1], SIDE, 1)
                    both.append(
                        jnp.where(
                            low_side,
                            straight + pltpu.roll(straight, SIDE, 1),
                            crossed - pltpu.roll(crossed, SIDE, 1),
                        )
                    )
                store(slot, TAIL, both)
        return carry

    lax.fori_loop(0, count, one_block, 0, unroll=True)
    rows = part_columns(part)
    lagged = jnp.dot(xh_ref[...], high_ref[rows, :], preferred_element_type=jnp.float32)
    lagged += jnp.dot(xh_ref[...], low_ref[rows, :], preferred_element_type=jnp.float32)
    lagged += jnp.dot(xl_ref[...], high_ref[rows, :], preferred_element_type=jnp.float32)
    return lagged.reshape(count * PARTNERS, MINE, LAGS)


def store_lags(out_ref, first_block, count, scalar_ref, lagged):
    for i in range(count * PARTNERS):
        valid = scalar_ref[first_block + i // PARTNERS, REST + i % PARTNERS] > 0
        out_ref[first_block * PARTNERS + i] = jnp.where(valid, lagged[i], 0.0)


def inner_kernel(
    taper_ref, plane_ref, high_ref, low_ref, out_ref, scalar_ref, xh_ref, xl_ref, number_ref, sem
):
    for a in range(PLANE):
        number_ref[a : a + 1, :] = (
            plane_ref[a, :, TAIL * LANES :].astype(jnp.float32)[:1].astype(jnp.int32)
        )
    numbers = pltpu.make_async_copy(number_ref, scalar_ref, sem)
    numbers.start()
    numbers.wait()
    lagged = cross_and_lag(
        0, INNER, (0, FULL, True), taper_ref, plane_ref, high_ref, low_ref, scalar_ref, xh_ref, xl_ref
    )
    store_lags(out_ref, 0, INNER, scalar_ref, lagged)


def halo_kernel(
    part,
    scalar_ref,
    taper_ref,
    plane_ref,
    halo_ref,
    high_ref,
    low_ref,
    before_ref,
    out_ref,
    xh_ref,
    xl_ref,
    w_ref,
):
    for i in range(REACH):
        w_ref[i] = plane_ref[INNER + i, :, part_columns(part)]
        w_ref[REACH + i] = halo_ref[i]
    lagged = cross_and_lag(
        INNER, REACH, part, taper_ref, w_ref, high_ref, low_ref, scalar_ref, xh_ref, xl_ref
    )
    if before_ref is None:
        out_ref[...] = lagged
    else:
        store_lags(out_ref, INNER, REACH, scalar_ref, lagged + before_ref[...])


def correlated_call(body, name, scalars, operands, out_blocks, count, width, aliases, extra):
    rows = count * PARTNERS * MINE
    vmem = pl.BlockSpec(memory_space=pltpu.VMEM)
    smem = pl.BlockSpec(memory_space=pltpu.SMEM)
    out_specs = [vmem]
    out_shape = [pltpu.VMEM((out_blocks * PARTNERS, MINE, LAGS), jnp.float32)]
    operands = [in_vmem(operand) for operand in operands]
    in_specs = [vmem] * len(operands)
    if scalars is None:
        out_specs.append(smem)
        out_shape.append(pltpu.SMEM((PLANE, LANES), jnp.int32))
    else:
        in_specs.insert(0, smem)
        operands.insert(0, pltpu.with_memory_space_constraint(scalars, pltpu.SMEM))
    return pl.pallas_call(
        body,
        in_specs=in_specs,
        out_specs=out_specs,
        out_shape=out_shape,
        scratch_shapes=[
            pltpu.VMEM((rows, width), jnp.bfloat16),
            pltpu.VMEM((rows, width), jnp.bfloat16),
        ]
        + extra,
        input_output_aliases=aliases,
        compiler_params=pltpu.CompilerParams(vmem_limit_bytes=10 << 20),
        cost_estimate=pl.CostEstimate(
            flops=6 * rows * width * LAGS, bytes_accessed=4 << 20, transcendentals=0
        ),
        name=name,
    )(*operands)


def per_device(records, taper, pairs):
    theirs, real, pair = spectra(records[0])
    got = lax.ppermute(theirs, "tm", [(0, 1), (1, 0)])
    mine, squared = own_half(pairs, taper, real, pair)
    send = mine.at[:, MINE:].set(got.reshape(PLANE, MINE, WIDE))
    plane = lax.all_to_all(send, "col", 0, 0, tiled=True)
    count = lax.axis_size("row")
    down = [(z, z - 1) for z in range(1, count)]
    head, squared = lax.optimization_barrier((plane_head(plane, HALO_PARTS[0]), squared))
    halos = [lax.ppermute(head, "row", down)]
    squared = taper_columns(squared)
    high, low = (jnp.asarray(table) for table in lag_tables())
    widths = [part_width(part) for part in HALO_PARTS]
    w = [[pltpu.VMEM((2 * REACH, 2 * MINE, width), jnp.bfloat16)] for width in widths]
    lagged, scalars = correlated_call(
        inner_kernel,
        "correlate_inner",
        None,
        [squared, plane, high, low],
        PLANE,
        INNER,
        WIDE,
        {},
        [pltpu.VMEM((PLANE, LANES), jnp.int32), pltpu.SemaphoreType.DMA(())],
    )

    later, scalars = lax.optimization_barrier((plane, scalars))
    halos.append(lax.ppermute(plane_head(later, HALO_PARTS[1]), "row", down))

    def first(*refs):
        halo_kernel(HALO_PARTS[0], *refs[:6], None, *refs[6:])

    def second(*refs):
        halo_kernel(HALO_PARTS[1], *refs[:7], *refs[8:])

    (partial,) = correlated_call(
        first,
        "correlate_halo_first",
        scalars,
        [squared, plane, halos[0], high, low],
        REACH,
        REACH,
        widths[0],
        {},
        w[0],
    )
    (lagged,) = correlated_call(
        second,
        "correlate_halo_second",
        scalars,
        [squared, plane, halos[1], high, low, partial, lagged],
        PLANE,
        REACH,
        widths[1],
        {7: 0},
        w[1],
    )
    lagged = lagged.reshape(PLANE, PARTNERS, MINE, LAGS)
    back = lax.all_to_all(lagged.astype(jnp.bfloat16), "col", 0, 0, tiled=True).astype(jnp.float32)
    return back.transpose(1, 0, 2, 3).reshape(1, PARTNERS, HALF, LAGS)


def solution(mesh):
    return jax.shard_map(
        per_device,
        mesh=mesh,
        in_specs=(P("tm", ("row", "col"), None), P(), P(("row", "col"), None)),
        out_specs=P(("row", "col"), None, "tm", None),
        check_vma=False,
    )
```

```python
import math

import jax
import jax.numpy as jnp
import ml_dtypes
import numpy as np
from jax import lax
from jax.experimental import pallas as pl
from jax.experimental.pallas import tpu as pltpu
from jax.sharding import PartitionSpec as P

SAMPLES = 7680
FREQS = 1200
FIRST_BIN = 32
LAGS = 256
SMOOTH = 4
PARTNERS = 4
REACH = 7
BLOCK = 256
WINDOWS = 2
WATER = 0.3
RESCALE = 2.0

RADIX = 10
PART = SAMPLES // RADIX
HALF = BLOCK // 2
PER = FREQS // RADIX
LANES = 128
SPARE = LANES - PER
FULL = RADIX - 1
REST = PER - FULL * SPARE
TAIL = 2 * FULL
SIDE = LANES // 2
WIDE = (TAIL + 1) * LANES
HALO_PARTS = ((3, FULL, True), (0, 3, False))
BASE = 3
TURNS = 4
ORDER = (0, 1, -1, 2, -2, 3, -3, 4, -4, 5)
ROWS = (1 + 2 * (TURNS + 1)) * BLOCK
PLANE = 16
INNER = PLANE - REACH
MINE = HALF // PLANE
CHUNKS = 4


def lowest_lane(residue):
    return 0 if residue + RADIX * BASE >= FIRST_BIN else 1


def place_in_band(residue):
    return residue + SMOOTH


def turn(phase):
    angle = phase % SAMPLES * (2.0 * math.pi / SAMPLES)
    return np.cos(angle), -np.sin(angle)


def base_table():
    steps = np.arange(PART)[:, None] * (RADIX * (BASE + np.arange(LANES)))[None, :]
    return np.concatenate(turn(steps), axis=1).astype(np.float32).astype(ml_dtypes.bfloat16)


def twiddles():
    steps = np.arange(1, TURNS + 2)[:, None] * np.arange(PART)[None, :]
    return np.stack(turn(steps), axis=1).reshape(-1, PART).astype(np.float32)


def lag_tables():
    lag_steps = np.arange(LAGS) - LAGS // 2 + SAMPLES
    factor = RESCALE / math.sqrt(FREQS * WINDOWS)
    rows = []
    for residue in ORDER:
        bins = residue + RADIX * (BASE + lowest_lane(residue) + np.arange(PER))
        rows.append(np.stack(turn(bins[:, None] * lag_steps[None, :])))
    blocks = []
    for place, residue in enumerate(ORDER[:FULL]):
        spare = rows[FULL][:, place * SPARE : (place + 1) * SPARE]
        block = np.concatenate([rows[place], spare], axis=1)
        blocks.append(np.roll(block, lowest_lane(residue), axis=1).reshape(-1, LAGS))
    tail = np.zeros((2, SIDE, LAGS))
    tail[:, :REST] = rows[FULL][:, FULL * SPARE :]
    table = np.concatenate(blocks + [tail.reshape(LANES, LAGS)]) * factor
    table = table.astype(np.float32)
    high = table.astype(ml_dtypes.bfloat16)
    low = (table - high.astype(np.float32)).astype(ml_dtypes.bfloat16)
    return high, low


def taper_columns(square_ref, taper_ref):
    rows = jnp.transpose(square_ref[...])
    lane = lax.broadcasted_iota(jnp.int32, (1, LANES), 1)
    spare = [lane >= PER, (lane > PER) | (lane < 1)]

    def row(residue):
        index = residue + RADIX * (BASE + lowest_lane(residue)) - FIRST_BIN
        return rows[index : index + 1, :]

    last = row(ORDER[FULL])
    for place, residue in enumerate(ORDER[:FULL]):
        low = lowest_lane(residue)
        own = pltpu.roll(row(residue), 1, 1) if low else row(residue)
        moved = pltpu.roll(last, PER + low - place * SPARE, 1)
        taper_ref[place : place + 1, :] = jnp.where(spare[low], moved, own)
    moved = [pltpu.roll(last, LANES + side * SIDE - FULL * SPARE, 1) for side in range(2)]
    taper_ref[FULL : FULL + 1, :] = jnp.where(lane < SIDE, moved[0], moved[1])


def five_point(x):
    cos = [math.cos(2.0 * math.pi * k / 5) for k in (1, 2)]
    sin = [math.sin(2.0 * math.pi * k / 5) for k in (1, 2)]
    near, far = x[1] + x[4], x[2] + x[3]
    near_gap, far_gap = x[1] - x[4], x[2] - x[3]
    return (
        x[0] + near + far,
        x[0] + cos[0] * near + cos[1] * far,
        sin[0] * near_gap + sin[1] * far_gap,
        x[0] + cos[1] * near + cos[0] * far,
        sin[1] * near_gap - sin[0] * far_gap,
    )


def dft_kernel(
    x_hbm,
    table_hbm,
    turn_hbm,
    theirs_ref,
    sums_ref,
    x_ref,
    table_ref,
    turn_ref,
    y_ref,
    x_sems,
    t_sems,
):
    core = lax.axis_index("tm")
    size = BLOCK // CHUNKS
    x_copies = [
        pltpu.make_async_copy(
            x_hbm.at[pl.ds(c * size, size)], x_ref.at[pl.ds(c * size, size)], x_sems.at[c]
        )
        for c in range(CHUNKS)
    ]
    turn_copy = pltpu.make_async_copy(turn_hbm, turn_ref, t_sems.at[0])
    table_copy = pltpu.make_async_copy(table_hbm, table_ref, t_sems.at[1])
    for copy in [turn_copy] + x_copies + [table_copy]:
        copy.start()

    def split(i, carry):
        at = pl.ds(pl.multiple_of(i * 16, 16), 16)
        for lane in range(0, PART, LANES):
            x = [
                x_ref[at, n * PART + lane : n * PART + lane + LANES].astype(jnp.float32)
                for n in range(RADIX)
            ]
            even = five_point([x[n] + x[n + 5] for n in range(5)])
            odd = five_point([x[n] - x[n + 5] if n % 2 == 0 else x[n + 5] - x[n] for n in range(5)])
            sums = [(odd[3], -odd[4]), even[1:3], (odd[1], -odd[2]), even[3:5]]
            parts = [even[0]]
            for r in range(TURNS + 1):
                cos = turn_ref[2 * r : 2 * r + 1, lane : lane + LANES]
                sin = turn_ref[2 * r + 1 : 2 * r + 2, lane : lane + LANES]
                if r < TURNS:
                    real, imag = sums[r]
                    parts += [real * cos + imag * sin, real * sin - imag * cos]
                else:
                    parts += [odd[0] * cos, odd[0] * sin]
            for n, part in enumerate(parts):
                y_ref[
                    pl.ds(pl.multiple_of(n * BLOCK + i * 16, 16), 16), lane : lane + LANES
                ] = part.astype(jnp.bfloat16)
        return carry

    turn_copy.wait()
    for c in range(CHUNKS):
        x_copies[c].wait()
        lax.fori_loop(c * size // 16, (c + 1) * size // 16, split, 0, unroll=2)

    table_copy.wait()
    for begin in range(0, ROWS, 2 * BLOCK):
        at = slice(begin, min(begin + 2 * BLOCK, ROWS))
        sums_ref[at] = jnp.dot(y_ref[at], table_ref[...], preferred_element_type=jnp.float32)

    def rows(i, carry):
        row = (1 - core) * HALF + i * 16
        parts = [white_rows(sums_ref, row + j * MINE) for j in range(2)]
        for n in range(TAIL + 1):
            theirs_ref[pl.ds(pl.multiple_of(i * 16, 16), 16), n * LANES : (n + 1) * LANES] = (
                jnp.concatenate([parts[0][n], parts[1][n]], axis=0).astype(jnp.bfloat16)
            )
        return carry

    lax.fori_loop(0, HALF // 16, rows, 0, unroll=2)


def spectrum_parts(sums_ref, row):
    def load(index):
        at = pl.ds(pl.multiple_of(index * BLOCK + row, MINE), MINE)
        return sums_ref[at, :LANES], sums_ref[at, LANES:]

    parts = [load(0)]
    for r in range(TURNS + 1):
        (real_cos, real_sin), (imag_cos, imag_sin) = load(1 + 2 * r), load(2 + 2 * r)
        parts.append((real_cos - imag_sin, real_sin + imag_cos))
        if r < TURNS:
            parts.append((real_cos + imag_sin, real_sin - imag_cos))
    return parts


def white_rows(sums_ref, row):
    lane = lax.broadcasted_iota(jnp.int32, (MINE, LANES), 1)
    spare = [lane >= PER, (lane > PER) | (lane < 1)]
    band = [None] * RADIX
    for residue, (re, im) in zip(ORDER, spectrum_parts(sums_ref, row)):
        square = re * re + im * im
        amplitude = square * lax.rsqrt(jnp.maximum(square, 1e-30))
        band[place_in_band(residue)] = jnp.where(spare[lowest_lane(residue)], 0.0, amplitude)
    total = band[0]
    for amplitude in band[1:]:
        total = total + amplitude
    floor = WATER / FREQS * jnp.sum(total, axis=1, keepdims=True) + 1e-05
    line = [pltpu.roll(a, 1, 1) for a in band[RADIX - SMOOTH :]]
    line = line + band + [pltpu.roll(a, LANES - 1, 1) for a in band[:SMOOTH]]
    two = [line[i] + line[i + 1] for i in range(len(line) - 1)]
    four = [two[i] + two[i + 2] for i in range(len(two) - 2)]
    out = []
    for residue, (re, im) in zip(ORDER, spectrum_parts(sums_ref, row)):
        i = place_in_band(residue)
        smoothed = (four[i] + four[i + 4] + line[i + 8]) * (1.0 / (2 * SMOOTH + 1))
        level = smoothed + floor
        scale = pl.reciprocal(level, approx=True)
        scale = scale * (2.0 - level * scale)
        out += [re * scale, im * scale]
    last = out[TAIL:]
    for place, residue in enumerate(ORDER[:FULL]):
        low = lowest_lane(residue)
        for side in range(2):
            moved = pltpu.roll(last[side], PER + low - place * SPARE, 1)
            here = 2 * place + side
            out[here] = jnp.where(spare[low], moved, out[here])
    moved = [
        pltpu.roll(last[side], LANES + side * SIDE - FULL * SPARE, 1) for side in range(2)
    ]
    return out[:TAIL] + [jnp.where(lane < SIDE, moved[0], moved[1])]


def own_kernel(pairs_ref, taper_ref, sums_ref, mine_ref, squared_ref):
    squared_ref[...] = taper_ref[...] * taper_ref[...]
    core = lax.axis_index("tm")
    block = lax.axis_index("row") * PLANE + lax.axis_index("col")
    lane = lax.broadcasted_iota(jnp.int32, (MINE, LANES), 1)
    offsets = jnp.zeros((MINE, LANES), jnp.float32)
    for k in range(PARTNERS):
        partner = pairs_ref[0, k]
        offset = jnp.where(partner < 0, 0, partner - block).astype(jnp.float32)
        offsets = jnp.where(lane == REST + k, offset, offsets)

    def rows(j, carry):
        parts = white_rows(sums_ref, core * HALF + j * MINE)
        parts[TAIL] = jnp.where((lane >= REST) & (lane < SIDE), offsets, parts[TAIL])
        for n, part in enumerate(parts):
            mine_ref[j, :, n * LANES : (n + 1) * LANES] = jnp.concatenate(
                [part, part], axis=0
            ).astype(jnp.bfloat16)
        return carry

    lax.fori_loop(0, PLANE, rows, 0, unroll=4)


def in_vmem(array):
    return pltpu.with_memory_space_constraint(array, pltpu.VMEM)


def spectra(series):
    hbm = pl.BlockSpec(memory_space=pltpu.HBM)
    vmem = pl.BlockSpec(memory_space=pltpu.VMEM)
    operands = [
        pltpu.with_memory_space_constraint(a, pltpu.HBM)
        for a in (series, jnp.asarray(base_table()), jnp.asarray(twiddles()))
    ]
    return pl.pallas_call(
        dft_kernel,
        in_specs=[hbm, hbm, hbm],
        out_specs=[vmem, vmem],
        out_shape=[
            pltpu.VMEM((HALF, WIDE), jnp.bfloat16),
            pltpu.VMEM((ROWS, 2 * LANES), jnp.float32),
        ],
        scratch_shapes=[
            pltpu.VMEM((BLOCK, SAMPLES), jnp.bfloat16),
            pltpu.VMEM((PART, 2 * LANES), jnp.bfloat16),
            pltpu.VMEM((2 * (TURNS + 1), PART), jnp.float32),
            pltpu.VMEM((ROWS, PART), jnp.bfloat16),
            pltpu.SemaphoreType.DMA((CHUNKS,)),
            pltpu.SemaphoreType.DMA((2,)),
        ],
        compiler_params=pltpu.CompilerParams(vmem_limit_bytes=16 << 20),
        name="dft_whiten",
    )(*operands)


def own_half(pairs, taper, sums):
    vmem = pl.BlockSpec(memory_space=pltpu.VMEM)
    return pl.pallas_call(
        own_kernel,
        in_specs=[pl.BlockSpec(memory_space=pltpu.SMEM), vmem, vmem],
        out_specs=[vmem, vmem],
        out_shape=[
            pltpu.VMEM((PLANE, 2 * MINE, WIDE), jnp.bfloat16),
            pltpu.VMEM((FREQS,), jnp.float32),
        ],
        compiler_params=pltpu.CompilerParams(vmem_limit_bytes=4 << 20),
        cost_estimate=pl.CostEstimate(
            flops=40 * HALF * WIDE, bytes_accessed=5 << 20, transcendentals=0
        ),
        name="whiten_own",
    )(pairs, taper, in_vmem(sums))


def part_columns(part):
    begin, end, tail = part
    return slice(2 * begin * LANES, (2 * end + tail) * LANES)


def part_width(part):
    columns = part_columns(part)
    return columns.stop - columns.start


def plane_head(plane, part):
    vmem = pl.BlockSpec(memory_space=pltpu.VMEM)

    def body(plane_ref, head_ref):
        for i in range(REACH):
            head_ref[i] = plane_ref[i, :, part_columns(part)]

    return pl.pallas_call(
        body,
        in_specs=[vmem],
        out_specs=vmem,
        out_shape=pltpu.VMEM((REACH, 2 * MINE, part_width(part)), jnp.bfloat16),
        compiler_params=pltpu.CompilerParams(vmem_limit_bytes=2 << 20),
        name="plane_head",
    )(in_vmem(plane))


def cross_and_lag(
    first_block, count, part, taper_ref, w_ref, high_ref, low_ref, scalar_ref, xh_ref, xl_ref
):
    begin, end, with_tail = part
    shift = 2 * begin * LANES
    low_side = lax.broadcasted_iota(jnp.int32, (MINE, LANES), 1) < SIDE

    def one_block(a, carry):
        seconds = [a + scalar_ref[first_block + a, REST + k] for k in range(PARTNERS)]

        def load(index, block, blocks):
            here = block * LANES - shift
            both = w_ref[index, :, here : here + blocks * LANES].astype(jnp.float32)
            return [both[w * MINE : (w + 1) * MINE] for w in range(WINDOWS)]

        def store(slot, block, both):
            at = pl.ds(pl.multiple_of((a * PARTNERS + slot) * MINE, 16), 2 * MINE)
            columns = slice(block * LANES - shift, (block + 1) * LANES - shift)
            cross = jnp.concatenate(both, axis=0)
            high = cross.astype(jnp.bfloat16)
            xh_ref[at, columns] = high
            xl_ref[at, columns] = (cross - high.astype(jnp.float32)).astype(jnp.bfloat16)

        for n in range(begin, end):
            taper = taper_ref[n : n + 1, :]
            first = [(x[:, :LANES] * taper, x[:, LANES:] * taper) for x in load(a, 2 * n, 2)]
            for slot in range(0, PARTNERS, 2):
                re, im = [], []
                for k in (slot, slot + 1):
                    (a_re, a_im), (c_re, c_im) = first
                    (b_re, b_im), (d_re, d_im) = [
                        (x[:, :LANES], x[:, LANES:]) for x in load(seconds[k], 2 * n, 2)
                    ]
                    re.append((a_re * b_re + a_im * b_im) + (c_re * d_re + c_im * d_im))
                    im.append((a_im * b_re - a_re * b_im) + (c_im * d_re - c_re * d_im))
                store(slot, 2 * n, re)
                store(slot, 2 * n + 1, im)
        if with_tail:
            taper = taper_ref[FULL : FULL + 1, :]
            first = [x * taper for x in load(a, TAIL, 1)]
            for slot in range(0, PARTNERS, 2):
                both = []
                for k in (slot, slot + 1):
                    second = load(seconds[k], TAIL, 1)
                    straight = first[0] * second[0] + first[1] * second[1]
                    crossed = first[0] * pltpu.roll(second[0], SIDE, 1)
                    crossed = crossed + first[1] * pltpu.roll(second[1], SIDE, 1)
                    both.append(
                        jnp.where(
                            low_side,
                            straight + pltpu.roll(straight, SIDE, 1),
                            crossed - pltpu.roll(crossed, SIDE, 1),
                        )
                    )
                store(slot, TAIL, both)
        return carry

    lax.fori_loop(0, count, one_block, 0, unroll=True)
    rows = part_columns(part)
    lagged = jnp.dot(xh_ref[...], high_ref[rows, :], preferred_element_type=jnp.float32)
    lagged += jnp.dot(xh_ref[...], low_ref[rows, :], preferred_element_type=jnp.float32)
    lagged += jnp.dot(xl_ref[...], high_ref[rows, :], preferred_element_type=jnp.float32)
    return lagged.reshape(count * PARTNERS, MINE, LAGS)


def store_lags(out_ref, first_block, count, scalar_ref, lagged):
    for i in range(count * PARTNERS):
        valid = scalar_ref[first_block + i // PARTNERS, REST + i % PARTNERS] > 0
        out_ref[first_block * PARTNERS + i] = jnp.where(valid, lagged[i], 0.0)


def inner_kernel(
    squared_ref,
    plane_ref,
    high_ref,
    low_ref,
    out_ref,
    scalar_ref,
    taper_ref,
    xh_ref,
    xl_ref,
    number_ref,
    sem,
    square_ref,
):
    for a in range(PLANE):
        number_ref[a : a + 1, :] = (
            plane_ref[a, :, TAIL * LANES :].astype(jnp.float32)[:1].astype(jnp.int32)
        )
    numbers = pltpu.make_async_copy(number_ref, scalar_ref, sem)
    numbers.start()
    square_ref[...] = jnp.zeros_like(square_ref)
    square_ref[:PER, :RADIX] = squared_ref[...]
    taper_columns(square_ref, taper_ref)
    numbers.wait()
    lagged = cross_and_lag(
        0, INNER, (0, FULL, True), taper_ref, plane_ref, high_ref, low_ref, scalar_ref, xh_ref, xl_ref
    )
    store_lags(out_ref, 0, INNER, scalar_ref, lagged)


def halo_kernel(
    part,
    scalar_ref,
    taper_ref,
    plane_ref,
    halo_ref,
    high_ref,
    low_ref,
    before_ref,
    out_ref,
    xh_ref,
    xl_ref,
    w_ref,
):
    for i in range(REACH):
        w_ref[i] = plane_ref[INNER + i, :, part_columns(part)]
        w_ref[REACH + i] = halo_ref[i]
    lagged = cross_and_lag(
        INNER, REACH, part, taper_ref, w_ref, high_ref, low_ref, scalar_ref, xh_ref, xl_ref
    )
    if before_ref is None:
        out_ref[...] = lagged
    else:
        store_lags(out_ref, INNER, REACH, scalar_ref, lagged + before_ref[...])


def correlated_call(body, name, scalars, operands, out_blocks, count, width, aliases, extra):
    rows = count * PARTNERS * MINE
    vmem = pl.BlockSpec(memory_space=pltpu.VMEM)
    smem = pl.BlockSpec(memory_space=pltpu.SMEM)
    out_specs = [vmem]
    out_shape = [pltpu.VMEM((out_blocks * PARTNERS, MINE, LAGS), jnp.float32)]
    operands = [in_vmem(operand) for operand in operands]
    in_specs = [vmem] * len(operands)
    if scalars is None:
        out_specs += [smem, vmem]
        out_shape.append(pltpu.SMEM((PLANE, LANES), jnp.int32))
        out_shape.append(pltpu.VMEM((RADIX, LANES), jnp.float32))
    else:
        in_specs.insert(0, smem)
        operands.insert(0, pltpu.with_memory_space_constraint(scalars, pltpu.SMEM))
    return pl.pallas_call(
        body,
        in_specs=in_specs,
        out_specs=out_specs,
        out_shape=out_shape,
        scratch_shapes=[
            pltpu.VMEM((rows, width), jnp.bfloat16),
            pltpu.VMEM((rows, width), jnp.bfloat16),
        ]
        + extra,
        input_output_aliases=aliases,
        compiler_params=pltpu.CompilerParams(vmem_limit_bytes=10 << 20),
        cost_estimate=pl.CostEstimate(
            flops=6 * rows * width * LAGS, bytes_accessed=4 << 20, transcendentals=0
        ),
        name=name,
    )(*operands)


def per_device(records, taper, pairs):
    theirs, sums = spectra(records[0])
    got = lax.ppermute(theirs, "tm", [(0, 1), (1, 0)])
    mine, squared = own_half(pairs, taper, sums)
    send = mine.at[:, MINE:].set(got.reshape(PLANE, MINE, WIDE))
    plane = lax.all_to_all(send, "col", 0, 0, tiled=True)
    count = lax.axis_size("row")
    down = [(z, z - 1) for z in range(1, count)]
    head, squared = lax.optimization_barrier((plane_head(plane, HALO_PARTS[0]), squared))
    halos = [lax.ppermute(head, "row", down)]
    squared = squared.reshape(PER, RADIX)
    high, low = (jnp.asarray(table) for table in lag_tables())
    widths = [part_width(part) for part in HALO_PARTS]
    w = [[pltpu.VMEM((2 * REACH, 2 * MINE, width), jnp.bfloat16)] for width in widths]
    lagged, scalars, columns = correlated_call(
        inner_kernel,
        "correlate_inner",
        None,
        [squared, plane, high, low],
        PLANE,
        INNER,
        WIDE,
        {},
        [
            pltpu.VMEM((PLANE, LANES), jnp.int32),
            pltpu.SemaphoreType.DMA(()),
            pltpu.VMEM((LANES, LANES), jnp.float32),
        ],
    )

    later, scalars = lax.optimization_barrier((plane, scalars))
    halos.append(lax.ppermute(plane_head(later, HALO_PARTS[1]), "row", down))

    def first(*refs):
        halo_kernel(HALO_PARTS[0], *refs[:6], None, *refs[6:])

    def second(*refs):
        halo_kernel(HALO_PARTS[1], *refs[:7], *refs[8:])

    (partial,) = correlated_call(
        first,
        "correlate_halo_first",
        scalars,
        [columns, plane, halos[0], high, low],
        REACH,
        REACH,
        widths[0],
        {},
        w[0],
    )
    (lagged,) = correlated_call(
        second,
        "correlate_halo_second",
        scalars,
        [columns, plane, halos[1], high, low, partial, lagged],
        PLANE,
        REACH,
        widths[1],
        {7: 0},
        w[1],
    )
    lagged = lagged.reshape(PLANE, PARTNERS, MINE, LAGS)
    back = lax.all_to_all(lagged.astype(jnp.bfloat16), "col", 0, 0, tiled=True).astype(jnp.float32)
    return back.transpose(1, 0, 2, 3).reshape(1, PARTNERS, HALF, LAGS)


def solution(mesh):
    return jax.shard_map(
        per_device,
        mesh=mesh,
        in_specs=(P("tm", ("row", "col"), None), P(), P(("row", "col"), None)),
        out_specs=P(("row", "col"), None, "tm", None),
        check_vma=False,
    )
```

```python
import math

import jax
import jax.numpy as jnp
import ml_dtypes
import numpy as np
from jax import lax
from jax.experimental import pallas as pl
from jax.experimental.pallas import tpu as pltpu
from jax.sharding import PartitionSpec as P

SAMPLES = 7680
FREQS = 1200
FIRST_BIN = 32
LAGS = 256
SMOOTH = 4
PARTNERS = 4
REACH = 7
BLOCK = 256
WINDOWS = 2
WATER = 0.3
RESCALE = 2.0

RADIX = 10
PART = SAMPLES // RADIX
HALF = BLOCK // 2
PER = FREQS // RADIX
LANES = 128
SPARE = LANES - PER
FULL = RADIX - 1
REST = PER - FULL * SPARE
TAIL = 2 * FULL
SIDE = LANES // 2
WIDE = (TAIL + 1) * LANES
HALO_PARTS = ((3, FULL, True), (0, 3, False))
BASE = 3
TURNS = 4
ORDER = (0, 1, -1, 2, -2, 3, -3, 4, -4, 5)
PRODUCTS = 1 + 2 * TURNS
FINE = 256
PLANE = 16
INNER = PLANE - REACH
MINE = HALF // PLANE
CHUNKS = 4


def lowest_lane(residue):
    return 0 if residue + RADIX * BASE >= FIRST_BIN else 1


def place_in_band(residue):
    return residue + SMOOTH


def turn(phase):
    angle = phase % SAMPLES * (2.0 * math.pi / SAMPLES)
    return np.cos(angle), -np.sin(angle)


def dft_tables():
    def table(residue):
        steps = np.arange(PART)[:, None] * (residue + RADIX * (BASE + np.arange(LANES)))[None, :]
        return np.concatenate(turn(steps), axis=1).astype(np.float32)

    base, last = table(0), table(ORDER[-1])
    high = base.astype(ml_dtypes.bfloat16)
    low = (base - high.astype(np.float32))[:FINE].astype(ml_dtypes.bfloat16)
    return np.concatenate([high, last.astype(ml_dtypes.bfloat16), low])


def twiddles():
    steps = np.arange(1, TURNS + 1)[:, None] * np.arange(PART)[None, :]
    return np.stack(turn(steps), axis=1).reshape(-1, PART).astype(np.float32)


def lag_tables():
    lag_steps = np.arange(LAGS) - LAGS // 2 + SAMPLES
    factor = RESCALE / math.sqrt(FREQS * WINDOWS)
    rows = []
    for residue in ORDER:
        bins = residue + RADIX * (BASE + lowest_lane(residue) + np.arange(PER))
        rows.append(np.stack(turn(bins[:, None] * lag_steps[None, :])))
    blocks = []
    for place, residue in enumerate(ORDER[:FULL]):
        spare = rows[FULL][:, place * SPARE : (place + 1) * SPARE]
        block = np.concatenate([rows[place], spare], axis=1)
        blocks.append(np.roll(block, lowest_lane(residue), axis=1).reshape(-1, LAGS))
    tail = np.zeros((2, SIDE, LAGS))
    tail[:, :REST] = rows[FULL][:, FULL * SPARE :]
    table = np.concatenate(blocks + [tail.reshape(LANES, LAGS)]) * factor
    table = table.astype(np.float32)
    high = table.astype(ml_dtypes.bfloat16)
    low = (table - high.astype(np.float32)).astype(ml_dtypes.bfloat16)
    return high, low


def taper_columns(square_ref, taper_ref):
    rows = jnp.transpose(square_ref[...])
    lane = lax.broadcasted_iota(jnp.int32, (1, LANES), 1)
    spare = [lane >= PER, (lane > PER) | (lane < 1)]

    def row(residue):
        index = residue + RADIX * (BASE + lowest_lane(residue)) - FIRST_BIN
        return rows[index : index + 1, :]

    last = row(ORDER[FULL])
    for place, residue in enumerate(ORDER[:FULL]):
        low = lowest_lane(residue)
        own = pltpu.roll(row(residue), 1, 1) if low else row(residue)
        moved = pltpu.roll(last, PER + low - place * SPARE, 1)
        taper_ref[place : place + 1, :] = jnp.where(spare[low], moved, own)
    moved = [pltpu.roll(last, LANES + side * SIDE - FULL * SPARE, 1) for side in range(2)]
    taper_ref[FULL : FULL + 1, :] = jnp.where(lane < SIDE, moved[0], moved[1])


def five_point(x):
    cos = [math.cos(2.0 * math.pi * k / 5) for k in (1, 2)]
    sin = [math.sin(2.0 * math.pi * k / 5) for k in (1, 2)]
    near, far = x[1] + x[4], x[2] + x[3]
    near_gap, far_gap = x[1] - x[4], x[2] - x[3]
    return (
        x[0] + near + far,
        x[0] + cos[0] * near + cos[1] * far,
        sin[0] * near_gap + sin[1] * far_gap,
        x[0] + cos[1] * near + cos[0] * far,
        sin[1] * near_gap - sin[0] * far_gap,
    )


def dft_kernel(
    x_hbm,
    table_hbm,
    turn_hbm,
    theirs_ref,
    sums_ref,
    x_ref,
    table_ref,
    turn_ref,
    even_ref,
    odd_ref,
    last_ref,
    x_sems,
    t_sems,
):
    core = lax.axis_index("tm")
    size = BLOCK // CHUNKS
    y_refs = (even_ref, odd_ref)
    x_copies = [
        pltpu.make_async_copy(
            x_hbm.at[pl.ds(c * size, size)], x_ref.at[pl.ds(c * size, size)], x_sems.at[c]
        )
        for c in range(CHUNKS)
    ]
    turn_copy = pltpu.make_async_copy(turn_hbm, turn_ref, t_sems.at[0])
    table_copy = pltpu.make_async_copy(table_hbm, table_ref, t_sems.at[1])
    for copy in [turn_copy] + x_copies + [table_copy]:
        copy.start()

    def split(c, i):
        y_ref = y_refs[c % 2]
        at = slice(c * size + i * 16, c * size + (i + 1) * 16)
        for lane in range(0, PART, LANES):
            x = [
                x_ref[at, n * PART + lane : n * PART + lane + LANES].astype(jnp.float32)
                for n in range(RADIX)
            ]
            even = five_point([x[n] + x[n + 5] for n in range(5)])
            odd = five_point([x[n] - x[n + 5] if n % 2 == 0 else x[n + 5] - x[n] for n in range(5)])
            sums = [(odd[3], -odd[4]), even[1:3], (odd[1], -odd[2]), even[3:5]]
            parts = [even[0]]
            for r, (real, imag) in enumerate(sums):
                cos = turn_ref[2 * r : 2 * r + 1, lane : lane + LANES]
                sin = turn_ref[2 * r + 1 : 2 * r + 2, lane : lane + LANES]
                parts += [real * cos + imag * sin, real * sin - imag * cos]
            last_ref[at, lane : lane + LANES] = odd[0].astype(jnp.bfloat16)
            for n, part in enumerate(parts):
                y_ref[n * size + i * 16 : n * size + (i + 1) * 16, lane : lane + LANES] = part.astype(
                    jnp.bfloat16
                )

    def multiply(c):
        y_ref = y_refs[c % 2]
        product = jnp.dot(y_ref[...], table_ref[:PART], preferred_element_type=jnp.float32)
        for n in range(PRODUCTS):
            sums_ref[n * BLOCK + c * size : n * BLOCK + (c + 1) * size] = product[
                n * size : (n + 1) * size
            ]
        product = jnp.dot(
            y_ref[size:, :FINE], table_ref[2 * PART :], preferred_element_type=jnp.float32
        )
        for n in range(1, PRODUCTS):
            at = slice(n * BLOCK + c * size, n * BLOCK + (c + 1) * size)
            sums_ref[at] = sums_ref[at] + product[(n - 1) * size : n * size]

    turn_copy.wait()
    for c in range(CHUNKS):
        x_copies[c].wait()
        if c == 1:
            table_copy.wait()
        if c > 0:
            multiply(c - 1)
        for i in range(size // 16):
            split(c, i)
    multiply(CHUNKS - 1)
    sums_ref[PRODUCTS * BLOCK :] = jnp.dot(
        last_ref[...], table_ref[PART : 2 * PART], preferred_element_type=jnp.float32
    )

    def rows(i, carry):
        row = (1 - core) * HALF + i * 16
        parts = [white_rows(sums_ref, row + j * MINE) for j in range(2)]
        for n in range(TAIL + 1):
            theirs_ref[pl.ds(pl.multiple_of(i * 16, 16), 16), n * LANES : (n + 1) * LANES] = (
                jnp.concatenate([parts[0][n], parts[1][n]], axis=0).astype(jnp.bfloat16)
            )
        return carry

    lax.fori_loop(0, HALF // 16, rows, 0, unroll=2)


def spectrum_parts(sums_ref, row):
    def load(index):
        at = pl.ds(pl.multiple_of(index * BLOCK + row, MINE), MINE)
        return sums_ref[at, :LANES], sums_ref[at, LANES:]

    parts = [load(0)]
    for r in range(TURNS):
        (real_cos, real_sin), (imag_cos, imag_sin) = load(1 + 2 * r), load(2 + 2 * r)
        parts.append((real_cos - imag_sin, real_sin + imag_cos))
        parts.append((real_cos + imag_sin, real_sin - imag_cos))
    return parts + [load(PRODUCTS)]


def white_rows(sums_ref, row):
    lane = lax.broadcasted_iota(jnp.int32, (MINE, LANES), 1)
    spare = [lane >= PER, (lane > PER) | (lane < 1)]
    band = [None] * RADIX
    for residue, (re, im) in zip(ORDER, spectrum_parts(sums_ref, row)):
        square = re * re + im * im
        amplitude = square * lax.rsqrt(jnp.maximum(square, 1e-30))
        band[place_in_band(residue)] = jnp.where(spare[lowest_lane(residue)], 0.0, amplitude)
    total = band[0]
    for amplitude in band[1:]:
        total = total + amplitude
    floor = WATER / FREQS * jnp.sum(total, axis=1, keepdims=True) + 1e-05
    line = [pltpu.roll(a, 1, 1) for a in band[RADIX - SMOOTH :]]
    line = line + band + [pltpu.roll(a, LANES - 1, 1) for a in band[:SMOOTH]]
    two = [line[i] + line[i + 1] for i in range(len(line) - 1)]
    four = [two[i] + two[i + 2] for i in range(len(two) - 2)]
    out = []
    for residue, (re, im) in zip(ORDER, spectrum_parts(sums_ref, row)):
        i = place_in_band(residue)
        smoothed = (four[i] + four[i + 4] + line[i + 8]) * (1.0 / (2 * SMOOTH + 1))
        level = smoothed + floor
        scale = pl.reciprocal(level, approx=True)
        scale = scale * (2.0 - level * scale)
        out += [re * scale, im * scale]
    last = out[TAIL:]
    for place, residue in enumerate(ORDER[:FULL]):
        low = lowest_lane(residue)
        for side in range(2):
            moved = pltpu.roll(last[side], PER + low - place * SPARE, 1)
            here = 2 * place + side
            out[here] = jnp.where(spare[low], moved, out[here])
    moved = [
        pltpu.roll(last[side], LANES + side * SIDE - FULL * SPARE, 1) for side in range(2)
    ]
    return out[:TAIL] + [jnp.where(lane < SIDE, moved[0], moved[1])]


def own_kernel(pairs_ref, taper_ref, sums_ref, mine_ref, squared_ref):
    squared_ref[...] = taper_ref[...] * taper_ref[...]
    core = lax.axis_index("tm")
    block = lax.axis_index("row") * PLANE + lax.axis_index("col")
    lane = lax.broadcasted_iota(jnp.int32, (MINE, LANES), 1)
    offsets = jnp.zeros((MINE, LANES), jnp.float32)
    for k in range(PARTNERS):
        partner = pairs_ref[0, k]
        offset = jnp.where(partner < 0, 0, partner - block).astype(jnp.float32)
        offsets = jnp.where(lane == REST + k, offset, offsets)

    def rows(j, carry):
        parts = white_rows(sums_ref, core * HALF + j * MINE)
        parts[TAIL] = jnp.where((lane >= REST) & (lane < SIDE), offsets, parts[TAIL])
        for n, part in enumerate(parts):
            mine_ref[j, :, n * LANES : (n + 1) * LANES] = jnp.concatenate(
                [part, part], axis=0
            ).astype(jnp.bfloat16)
        return carry

    lax.fori_loop(0, PLANE, rows, 0, unroll=4)


def in_vmem(array):
    return pltpu.with_memory_space_constraint(array, pltpu.VMEM)


def spectra(series):
    hbm = pl.BlockSpec(memory_space=pltpu.HBM)
    vmem = pl.BlockSpec(memory_space=pltpu.VMEM)
    operands = [
        pltpu.with_memory_space_constraint(a, pltpu.HBM)
        for a in (series, jnp.asarray(dft_tables()), jnp.asarray(twiddles()))
    ]
    return pl.pallas_call(
        dft_kernel,
        in_specs=[hbm, hbm, hbm],
        out_specs=[vmem, vmem],
        out_shape=[
            pltpu.VMEM((HALF, WIDE), jnp.bfloat16),
            pltpu.VMEM(((PRODUCTS + 1) * BLOCK, 2 * LANES), jnp.float32),
        ],
        scratch_shapes=[
            pltpu.VMEM((BLOCK, SAMPLES), jnp.bfloat16),
            pltpu.VMEM((2 * PART + FINE, 2 * LANES), jnp.bfloat16),
            pltpu.VMEM((2 * TURNS, PART), jnp.float32),
            pltpu.VMEM((PRODUCTS * BLOCK // CHUNKS, PART), jnp.bfloat16),
            pltpu.VMEM((PRODUCTS * BLOCK // CHUNKS, PART), jnp.bfloat16),
            pltpu.VMEM((BLOCK, PART), jnp.bfloat16),
            pltpu.SemaphoreType.DMA((CHUNKS,)),
            pltpu.SemaphoreType.DMA((2,)),
        ],
        compiler_params=pltpu.CompilerParams(vmem_limit_bytes=16 << 20),
        name="dft_whiten",
    )(*operands)


def own_half(pairs, taper, sums):
    vmem = pl.BlockSpec(memory_space=pltpu.VMEM)
    return pl.pallas_call(
        own_kernel,
        in_specs=[pl.BlockSpec(memory_space=pltpu.SMEM), vmem, vmem],
        out_specs=[vmem, vmem],
        out_shape=[
            pltpu.VMEM((PLANE, 2 * MINE, WIDE), jnp.bfloat16),
            pltpu.VMEM((FREQS,), jnp.float32),
        ],
        compiler_params=pltpu.CompilerParams(vmem_limit_bytes=4 << 20),
        cost_estimate=pl.CostEstimate(
            flops=40 * HALF * WIDE, bytes_accessed=5 << 20, transcendentals=0
        ),
        name="whiten_own",
    )(pairs, taper, in_vmem(sums))


def part_columns(part):
    begin, end, tail = part
    return slice(2 * begin * LANES, (2 * end + tail) * LANES)


def part_width(part):
    columns = part_columns(part)
    return columns.stop - columns.start


def plane_head(plane, part):
    vmem = pl.BlockSpec(memory_space=pltpu.VMEM)

    def body(plane_ref, head_ref):
        for i in range(REACH):
            head_ref[i] = plane_ref[i, :, part_columns(part)]

    return pl.pallas_call(
        body,
        in_specs=[vmem],
        out_specs=vmem,
        out_shape=pltpu.VMEM((REACH, 2 * MINE, part_width(part)), jnp.bfloat16),
        compiler_params=pltpu.CompilerParams(vmem_limit_bytes=2 << 20),
        name="plane_head",
    )(in_vmem(plane))


def cross_and_lag(
    first_block, count, part, taper_ref, w_ref, high_ref, low_ref, scalar_ref, xh_ref, xl_ref
):
    begin, end, with_tail = part
    shift = 2 * begin * LANES
    low_side = lax.broadcasted_iota(jnp.int32, (MINE, LANES), 1) < SIDE

    def one_block(a, carry):
        seconds = [a + scalar_ref[first_block + a, REST + k] for k in range(PARTNERS)]

        def load(index, block, blocks):
            here = block * LANES - shift
            both = w_ref[index, :, here : here + blocks * LANES].astype(jnp.float32)
            return [both[w * MINE : (w + 1) * MINE] for w in range(WINDOWS)]

        def store(slot, block, both):
            at = pl.ds(pl.multiple_of((a * PARTNERS + slot) * MINE, 16), 2 * MINE)
            columns = slice(block * LANES - shift, (block + 1) * LANES - shift)
            cross = jnp.concatenate(both, axis=0)
            high = cross.astype(jnp.bfloat16)
            xh_ref[at, columns] = high
            xl_ref[at, columns] = (cross - high.astype(jnp.float32)).astype(jnp.bfloat16)

        for n in range(begin, end):
            taper = taper_ref[n : n + 1, :]
            first = [(x[:, :LANES] * taper, x[:, LANES:] * taper) for x in load(a, 2 * n, 2)]
            for slot in range(0, PARTNERS, 2):
                re, im = [], []
                for k in (slot, slot + 1):
                    (a_re, a_im), (c_re, c_im) = first
                    (b_re, b_im), (d_re, d_im) = [
                        (x[:, :LANES], x[:, LANES:]) for x in load(seconds[k], 2 * n, 2)
                    ]
                    re.append((a_re * b_re + a_im * b_im) + (c_re * d_re + c_im * d_im))
                    im.append((a_im * b_re - a_re * b_im) + (c_im * d_re - c_re * d_im))
                store(slot, 2 * n, re)
                store(slot, 2 * n + 1, im)
        if with_tail:
            taper = taper_ref[FULL : FULL + 1, :]
            first = [x * taper for x in load(a, TAIL, 1)]
            for slot in range(0, PARTNERS, 2):
                both = []
                for k in (slot, slot + 1):
                    second = load(seconds[k], TAIL, 1)
                    straight = first[0] * second[0] + first[1] * second[1]
                    crossed = first[0] * pltpu.roll(second[0], SIDE, 1)
                    crossed = crossed + first[1] * pltpu.roll(second[1], SIDE, 1)
                    both.append(
                        jnp.where(
                            low_side,
                            straight + pltpu.roll(straight, SIDE, 1),
                            crossed - pltpu.roll(crossed, SIDE, 1),
                        )
                    )
                store(slot, TAIL, both)
        return carry

    lax.fori_loop(0, count, one_block, 0, unroll=True)
    rows = part_columns(part)
    lagged = jnp.dot(xh_ref[...], high_ref[rows, :], preferred_element_type=jnp.float32)
    lagged += jnp.dot(xh_ref[...], low_ref[rows, :], preferred_element_type=jnp.float32)
    lagged += jnp.dot(xl_ref[...], high_ref[rows, :], preferred_element_type=jnp.float32)
    return lagged.reshape(count * PARTNERS, MINE, LAGS)


def store_lags(out_ref, first_block, count, scalar_ref, lagged):
    for i in range(count * PARTNERS):
        valid = scalar_ref[first_block + i // PARTNERS, REST + i % PARTNERS] > 0
        out_ref[first_block * PARTNERS + i] = jnp.where(valid, lagged[i], 0.0)


def inner_kernel(
    squared_ref,
    plane_ref,
    high_ref,
    low_ref,
    out_ref,
    scalar_ref,
    taper_ref,
    xh_ref,
    xl_ref,
    number_ref,
    sem,
    square_ref,
):
    for a in range(PLANE):
        number_ref[a : a + 1, :] = (
            plane_ref[a, :, TAIL * LANES :].astype(jnp.float32)[:1].astype(jnp.int32)
        )
    numbers = pltpu.make_async_copy(number_ref, scalar_ref, sem)
    numbers.start()
    square_ref[...] = jnp.zeros_like(square_ref)
    square_ref[:PER, :RADIX] = squared_ref[...]
    taper_columns(square_ref, taper_ref)
    numbers.wait()
    lagged = cross_and_lag(
        0, INNER, (0, FULL, True), taper_ref, plane_ref, high_ref, low_ref, scalar_ref, xh_ref, xl_ref
    )
    store_lags(out_ref, 0, INNER, scalar_ref, lagged)


def halo_kernel(
    part,
    scalar_ref,
    taper_ref,
    plane_ref,
    halo_ref,
    high_ref,
    low_ref,
    before_ref,
    out_ref,
    xh_ref,
    xl_ref,
    w_ref,
):
    for i in range(REACH):
        w_ref[i] = plane_ref[INNER + i, :, part_columns(part)]
        w_ref[REACH + i] = halo_ref[i]
    lagged = cross_and_lag(
        INNER, REACH, part, taper_ref, w_ref, high_ref, low_ref, scalar_ref, xh_ref, xl_ref
    )
    if before_ref is None:
        out_ref[...] = lagged
    else:
        store_lags(out_ref, INNER, REACH, scalar_ref, lagged + before_ref[...])


def correlated_call(body, name, scalars, operands, out_blocks, count, width, aliases, extra):
    rows = count * PARTNERS * MINE
    vmem = pl.BlockSpec(memory_space=pltpu.VMEM)
    smem = pl.BlockSpec(memory_space=pltpu.SMEM)
    out_specs = [vmem]
    out_shape = [pltpu.VMEM((out_blocks * PARTNERS, MINE, LAGS), jnp.float32)]
    operands = [in_vmem(operand) for operand in operands]
    in_specs = [vmem] * len(operands)
    if scalars is None:
        out_specs += [smem, vmem]
        out_shape.append(pltpu.SMEM((PLANE, LANES), jnp.int32))
        out_shape.append(pltpu.VMEM((RADIX, LANES), jnp.float32))
    else:
        in_specs.insert(0, smem)
        operands.insert(0, pltpu.with_memory_space_constraint(scalars, pltpu.SMEM))
    return pl.pallas_call(
        body,
        in_specs=in_specs,
        out_specs=out_specs,
        out_shape=out_shape,
        scratch_shapes=[
            pltpu.VMEM((rows, width), jnp.bfloat16),
            pltpu.VMEM((rows, width), jnp.bfloat16),
        ]
        + extra,
        input_output_aliases=aliases,
        compiler_params=pltpu.CompilerParams(vmem_limit_bytes=10 << 20),
        cost_estimate=pl.CostEstimate(
            flops=6 * rows * width * LAGS, bytes_accessed=4 << 20, transcendentals=0
        ),
        name=name,
    )(*operands)


def per_device(records, taper, pairs):
    theirs, sums = spectra(records[0])
    got = lax.ppermute(theirs, "tm", [(0, 1), (1, 0)])
    mine, squared = own_half(pairs, taper, sums)
    send = mine.at[:, MINE:].set(got.reshape(PLANE, MINE, WIDE))
    plane = lax.all_to_all(send, "col", 0, 0, tiled=True)
    count = lax.axis_size("row")
    down = [(z, z - 1) for z in range(1, count)]
    head, squared = lax.optimization_barrier((plane_head(plane, HALO_PARTS[0]), squared))
    halos = [lax.ppermute(head, "row", down)]
    squared = squared.reshape(PER, RADIX)
    high, low = (jnp.asarray(table) for table in lag_tables())
    widths = [part_width(part) for part in HALO_PARTS]
    w = [[pltpu.VMEM((2 * REACH, 2 * MINE, width), jnp.bfloat16)] for width in widths]
    lagged, scalars, columns = correlated_call(
        inner_kernel,
        "correlate_inner",
        None,
        [squared, plane, high, low],
        PLANE,
        INNER,
        WIDE,
        {},
        [
            pltpu.VMEM((PLANE, LANES), jnp.int32),
            pltpu.SemaphoreType.DMA(()),
            pltpu.VMEM((LANES, LANES), jnp.float32),
        ],
    )

    later, scalars = lax.optimization_barrier((plane, scalars))
    halos.append(lax.ppermute(plane_head(later, HALO_PARTS[1]), "row", down))

    def first(*refs):
        halo_kernel(HALO_PARTS[0], *refs[:6], None, *refs[6:])

    def second(*refs):
        halo_kernel(HALO_PARTS[1], *refs[:7], *refs[8:])

    (partial,) = correlated_call(
        first,
        "correlate_halo_first",
        scalars,
        [columns, plane, halos[0], high, low],
        REACH,
        REACH,
        widths[0],
        {},
        w[0],
    )
    (lagged,) = correlated_call(
        second,
        "correlate_halo_second",
        scalars,
        [columns, plane, halos[1], high, low, partial, lagged],
        PLANE,
        REACH,
        widths[1],
        {7: 0},
        w[1],
    )
    lagged = lagged.reshape(PLANE, PARTNERS, MINE, LAGS)
    back = lax.all_to_all(lagged.astype(jnp.bfloat16), "col", 0, 0, tiled=True).astype(jnp.float32)
    return back.transpose(1, 0, 2, 3).reshape(1, PARTNERS, HALF, LAGS)


def solution(mesh):
    return jax.shard_map(
        per_device,
        mesh=mesh,
        in_specs=(P("tm", ("row", "col"), None), P(), P(("row", "col"), None)),
        out_specs=P(("row", "col"), None, "tm", None),
        check_vma=False,
    )
```

```python
import math

import jax
import jax.numpy as jnp
import ml_dtypes
import numpy as np
from jax import lax
from jax.experimental import pallas as pl
from jax.experimental.pallas import tpu as pltpu
from jax.sharding import PartitionSpec as P

SAMPLES = 7680
FREQS = 1200
FIRST_BIN = 32
LAGS = 256
SMOOTH = 4
PARTNERS = 4
REACH = 7
BLOCK = 256
WINDOWS = 2
WATER = 0.3
RESCALE = 2.0

RADIX = 10
PART = SAMPLES // RADIX
HALF = BLOCK // 2
PER = FREQS // RADIX
LANES = 128
SPARE = LANES - PER
FULL = RADIX - 1
REST = PER - FULL * SPARE
TAIL = 2 * FULL
SIDE = LANES // 2
WIDE = (TAIL + 1) * LANES
HALO_PARTS = ((3, FULL, True), (0, 3, False))
BASE = 3
TURNS = 4
ORDER = (0, 1, -1, 2, -2, 3, -3, 4, -4, 5)
PRODUCTS = 1 + 2 * TURNS
FINE = 256
PLANE = 16
INNER = PLANE - REACH
MINE = HALF // PLANE
CHUNKS = 4


def lowest_lane(residue):
    return 0 if residue + RADIX * BASE >= FIRST_BIN else 1


def place_in_band(residue):
    return residue + SMOOTH


def turn(phase):
    angle = phase % SAMPLES * (2.0 * math.pi / SAMPLES)
    return np.cos(angle), -np.sin(angle)


def dft_tables():
    def table(residue):
        steps = np.arange(PART)[:, None] * (residue + RADIX * (BASE + np.arange(LANES)))[None, :]
        return np.concatenate(turn(steps), axis=1).astype(np.float32)

    base, last = table(0), table(ORDER[-1])
    high = base.astype(ml_dtypes.bfloat16)
    low = (base - high.astype(np.float32))[:FINE].astype(ml_dtypes.bfloat16)
    return np.concatenate([high, last.astype(ml_dtypes.bfloat16), low])


def twiddles():
    steps = np.arange(1, TURNS + 1)[:, None] * np.arange(PART)[None, :]
    return np.stack(turn(steps), axis=1).reshape(-1, PART).astype(np.float32)


def lag_tables():
    lag_steps = np.arange(LAGS) - LAGS // 2 + SAMPLES
    factor = RESCALE / math.sqrt(FREQS * WINDOWS)
    rows = []
    for residue in ORDER:
        bins = residue + RADIX * (BASE + lowest_lane(residue) + np.arange(PER))
        rows.append(np.stack(turn(bins[:, None] * lag_steps[None, :])))
    blocks = []
    for place, residue in enumerate(ORDER[:FULL]):
        spare = rows[FULL][:, place * SPARE : (place + 1) * SPARE]
        block = np.concatenate([rows[place], spare], axis=1)
        blocks.append(np.roll(block, lowest_lane(residue), axis=1).reshape(-1, LAGS))
    tail = np.zeros((2, SIDE, LAGS))
    tail[:, :REST] = rows[FULL][:, FULL * SPARE :]
    table = np.concatenate(blocks + [tail.reshape(LANES, LAGS)]) * factor
    table = table.astype(np.float32)
    high = table.astype(ml_dtypes.bfloat16)
    low = (table - high.astype(np.float32)).astype(ml_dtypes.bfloat16)
    return high, low


def taper_columns(square_ref, taper_ref):
    rows = jnp.transpose(square_ref[...])
    lane = lax.broadcasted_iota(jnp.int32, (1, LANES), 1)
    spare = [lane >= PER, (lane > PER) | (lane < 1)]

    def row(residue):
        index = residue + RADIX * (BASE + lowest_lane(residue)) - FIRST_BIN
        return rows[index : index + 1, :]

    last = row(ORDER[FULL])
    for place, residue in enumerate(ORDER[:FULL]):
        low = lowest_lane(residue)
        own = pltpu.roll(row(residue), 1, 1) if low else row(residue)
        moved = pltpu.roll(last, PER + low - place * SPARE, 1)
        taper_ref[place : place + 1, :] = jnp.where(spare[low], moved, own)
    moved = [pltpu.roll(last, LANES + side * SIDE - FULL * SPARE, 1) for side in range(2)]
    taper_ref[FULL : FULL + 1, :] = jnp.where(lane < SIDE, moved[0], moved[1])


def five_point(x):
    cos = [math.cos(2.0 * math.pi * k / 5) for k in (1, 2)]
    sin = [math.sin(2.0 * math.pi * k / 5) for k in (1, 2)]
    near, far = x[1] + x[4], x[2] + x[3]
    near_gap, far_gap = x[1] - x[4], x[2] - x[3]
    return (
        x[0] + near + far,
        x[0] + cos[0] * near + cos[1] * far,
        sin[0] * near_gap + sin[1] * far_gap,
        x[0] + cos[1] * near + cos[0] * far,
        sin[1] * near_gap - sin[0] * far_gap,
    )


def dft_kernel(
    x_hbm,
    table_hbm,
    turn_hbm,
    theirs_ref,
    sums_ref,
    x_ref,
    table_ref,
    turn_ref,
    even_ref,
    odd_ref,
    last_ref,
    x_sems,
    t_sems,
):
    core = lax.axis_index("tm")
    size = BLOCK // CHUNKS
    y_refs = (even_ref, odd_ref)

    def rows_of(c):
        half, rest = c * size // HALF, c * size % HALF
        side = 1 - core if half == 0 else core
        return pl.ds(pl.multiple_of(side * HALF + rest, size), size)

    x_copies = [
        pltpu.make_async_copy(
            x_hbm.at[rows_of(c)], x_ref.at[pl.ds(c * size, size)], x_sems.at[c]
        )
        for c in range(CHUNKS)
    ]
    turn_copy = pltpu.make_async_copy(turn_hbm, turn_ref, t_sems.at[0])
    table_copy = pltpu.make_async_copy(table_hbm, table_ref, t_sems.at[1])
    for copy in [turn_copy] + x_copies + [table_copy]:
        copy.start()

    def split(c, i):
        y_ref = y_refs[c % 2]
        at = slice(c * size + i * 16, c * size + (i + 1) * 16)
        for lane in range(0, PART, LANES):
            x = [
                x_ref[at, n * PART + lane : n * PART + lane + LANES].astype(jnp.float32)
                for n in range(RADIX)
            ]
            even = five_point([x[n] + x[n + 5] for n in range(5)])
            odd = five_point([x[n] - x[n + 5] if n % 2 == 0 else x[n + 5] - x[n] for n in range(5)])
            sums = [(odd[3], -odd[4]), even[1:3], (odd[1], -odd[2]), even[3:5]]
            parts = [even[0]]
            for r, (real, imag) in enumerate(sums):
                cos = turn_ref[2 * r : 2 * r + 1, lane : lane + LANES]
                sin = turn_ref[2 * r + 1 : 2 * r + 2, lane : lane + LANES]
                parts += [real * cos + imag * sin, real * sin - imag * cos]
            last_ref[at, lane : lane + LANES] = odd[0].astype(jnp.bfloat16)
            for n, part in enumerate(parts):
                y_ref[n * size + i * 16 : n * size + (i + 1) * 16, lane : lane + LANES] = part.astype(
                    jnp.bfloat16
                )

    def multiply(c):
        y_ref = y_refs[c % 2]
        product = jnp.dot(y_ref[...], table_ref[:PART], preferred_element_type=jnp.float32)
        for n in range(PRODUCTS):
            sums_ref[n * BLOCK + c * size : n * BLOCK + (c + 1) * size] = product[
                n * size : (n + 1) * size
            ]
        product = jnp.dot(
            y_ref[size:, :FINE], table_ref[2 * PART :], preferred_element_type=jnp.float32
        )
        for n in range(1, PRODUCTS):
            at = slice(n * BLOCK + c * size, n * BLOCK + (c + 1) * size)
            sums_ref[at] = sums_ref[at] + product[(n - 1) * size : n * size]

    def multiply_last(half):
        at = slice(half * HALF, (half + 1) * HALF)
        sums_ref[PRODUCTS * BLOCK + half * HALF : PRODUCTS * BLOCK + (half + 1) * HALF] = jnp.dot(
            last_ref[at], table_ref[PART : 2 * PART], preferred_element_type=jnp.float32
        )

    turn_copy.wait()
    for c in range(CHUNKS):
        x_copies[c].wait()
        if c == 1:
            table_copy.wait()
        for i in range(size // 16):
            split(c, i)
        if c > 0:
            multiply(c - 1)
        if c == CHUNKS // 2:
            multiply_last(0)
    for i in range(HALF // 16):
        parts = [white_rows(sums_ref, i * 16 + j * MINE) for j in range(2)]
        for n in range(TAIL + 1):
            theirs_ref[i * 16 : (i + 1) * 16, n * LANES : (n + 1) * LANES] = jnp.concatenate(
                [parts[0][n], parts[1][n]], axis=0
            ).astype(jnp.bfloat16)
    multiply(CHUNKS - 1)
    multiply_last(1)


def spectrum_parts(sums_ref, row):
    def load(index):
        first = index * BLOCK + row
        at = pl.ds(first if isinstance(first, int) else pl.multiple_of(first, MINE), MINE)
        return sums_ref[at, :LANES], sums_ref[at, LANES:]

    parts = [load(0)]
    for r in range(TURNS):
        (real_cos, real_sin), (imag_cos, imag_sin) = load(1 + 2 * r), load(2 + 2 * r)
        parts.append((real_cos - imag_sin, real_sin + imag_cos))
        parts.append((real_cos + imag_sin, real_sin - imag_cos))
    return parts + [load(PRODUCTS)]


def white_rows(sums_ref, row):
    lane = lax.broadcasted_iota(jnp.int32, (MINE, LANES), 1)
    spare = [lane >= PER, (lane > PER) | (lane < 1)]
    band = [None] * RADIX
    for residue, (re, im) in zip(ORDER, spectrum_parts(sums_ref, row)):
        square = re * re + im * im
        amplitude = square * lax.rsqrt(jnp.maximum(square, 1e-30))
        band[place_in_band(residue)] = jnp.where(spare[lowest_lane(residue)], 0.0, amplitude)
    total = band[0]
    for amplitude in band[1:]:
        total = total + amplitude
    floor = WATER / FREQS * jnp.sum(total, axis=1, keepdims=True) + 1e-05
    line = [pltpu.roll(a, 1, 1) for a in band[RADIX - SMOOTH :]]
    line = line + band + [pltpu.roll(a, LANES - 1, 1) for a in band[:SMOOTH]]
    two = [line[i] + line[i + 1] for i in range(len(line) - 1)]
    four = [two[i] + two[i + 2] for i in range(len(two) - 2)]
    out = []
    for residue, (re, im) in zip(ORDER, spectrum_parts(sums_ref, row)):
        i = place_in_band(residue)
        smoothed = (four[i] + four[i + 4] + line[i + 8]) * (1.0 / (2 * SMOOTH + 1))
        level = smoothed + floor
        scale = pl.reciprocal(level, approx=True)
        scale = scale * (2.0 - level * scale)
        out += [re * scale, im * scale]
    last = out[TAIL:]
    for place, residue in enumerate(ORDER[:FULL]):
        low = lowest_lane(residue)
        for side in range(2):
            moved = pltpu.roll(last[side], PER + low - place * SPARE, 1)
            here = 2 * place + side
            out[here] = jnp.where(spare[low], moved, out[here])
    moved = [
        pltpu.roll(last[side], LANES + side * SIDE - FULL * SPARE, 1) for side in range(2)
    ]
    return out[:TAIL] + [jnp.where(lane < SIDE, moved[0], moved[1])]


def own_kernel(pairs_ref, taper_ref, sums_ref, mine_ref, squared_ref):
    squared_ref[...] = taper_ref[...] * taper_ref[...]
    block = lax.axis_index("row") * PLANE + lax.axis_index("col")
    lane = lax.broadcasted_iota(jnp.int32, (MINE, LANES), 1)
    offsets = jnp.zeros((MINE, LANES), jnp.float32)
    for k in range(PARTNERS):
        partner = pairs_ref[0, k]
        offset = jnp.where(partner < 0, 0, partner - block).astype(jnp.float32)
        offsets = jnp.where(lane == REST + k, offset, offsets)

    def rows(j, carry):
        parts = white_rows(sums_ref, HALF + j * MINE)
        parts[TAIL] = jnp.where((lane >= REST) & (lane < SIDE), offsets, parts[TAIL])
        for n, part in enumerate(parts):
            mine_ref[j, :, n * LANES : (n + 1) * LANES] = jnp.concatenate(
                [part, part], axis=0
            ).astype(jnp.bfloat16)
        return carry

    lax.fori_loop(0, PLANE, rows, 0, unroll=4)


def in_vmem(array):
    return pltpu.with_memory_space_constraint(array, pltpu.VMEM)


def spectra(series):
    hbm = pl.BlockSpec(memory_space=pltpu.HBM)
    vmem = pl.BlockSpec(memory_space=pltpu.VMEM)
    operands = [
        pltpu.with_memory_space_constraint(a, pltpu.HBM)
        for a in (series, jnp.asarray(dft_tables()), jnp.asarray(twiddles()))
    ]
    return pl.pallas_call(
        dft_kernel,
        in_specs=[hbm, hbm, hbm],
        out_specs=[vmem, vmem],
        out_shape=[
            pltpu.VMEM((HALF, WIDE), jnp.bfloat16),
            pltpu.VMEM(((PRODUCTS + 1) * BLOCK, 2 * LANES), jnp.float32),
        ],
        scratch_shapes=[
            pltpu.VMEM((BLOCK, SAMPLES), jnp.bfloat16),
            pltpu.VMEM((2 * PART + FINE, 2 * LANES), jnp.bfloat16),
            pltpu.VMEM((2 * TURNS, PART), jnp.float32),
            pltpu.VMEM((PRODUCTS * BLOCK // CHUNKS, PART), jnp.bfloat16),
            pltpu.VMEM((PRODUCTS * BLOCK // CHUNKS, PART), jnp.bfloat16),
            pltpu.VMEM((BLOCK, PART), jnp.bfloat16),
            pltpu.SemaphoreType.DMA((CHUNKS,)),
            pltpu.SemaphoreType.DMA((2,)),
        ],
        compiler_params=pltpu.CompilerParams(vmem_limit_bytes=16 << 20),
        name="dft_whiten",
    )(*operands)


def own_half(pairs, taper, sums):
    vmem = pl.BlockSpec(memory_space=pltpu.VMEM)
    return pl.pallas_call(
        own_kernel,
        in_specs=[pl.BlockSpec(memory_space=pltpu.SMEM), vmem, vmem],
        out_specs=[vmem, vmem],
        out_shape=[
            pltpu.VMEM((PLANE, 2 * MINE, WIDE), jnp.bfloat16),
            pltpu.VMEM((FREQS,), jnp.float32),
        ],
        compiler_params=pltpu.CompilerParams(vmem_limit_bytes=4 << 20),
        cost_estimate=pl.CostEstimate(
            flops=40 * HALF * WIDE, bytes_accessed=5 << 20, transcendentals=0
        ),
        name="whiten_own",
    )(pairs, taper, in_vmem(sums))


def part_columns(part):
    begin, end, tail = part
    return slice(2 * begin * LANES, (2 * end + tail) * LANES)


def part_width(part):
    columns = part_columns(part)
    return columns.stop - columns.start


def plane_head(plane, part):
    vmem = pl.BlockSpec(memory_space=pltpu.VMEM)

    def body(plane_ref, head_ref):
        for i in range(REACH):
            head_ref[i] = plane_ref[i, :, part_columns(part)]

    return pl.pallas_call(
        body,
        in_specs=[vmem],
        out_specs=vmem,
        out_shape=pltpu.VMEM((REACH, 2 * MINE, part_width(part)), jnp.bfloat16),
        compiler_params=pltpu.CompilerParams(vmem_limit_bytes=2 << 20),
        name="plane_head",
    )(in_vmem(plane))


def cross_and_lag(
    first_block, count, part, taper_ref, w_ref, high_ref, low_ref, scalar_ref, xh_ref, xl_ref
):
    begin, end, with_tail = part
    shift = 2 * begin * LANES
    low_side = lax.broadcasted_iota(jnp.int32, (MINE, LANES), 1) < SIDE

    def one_block(a, carry):
        seconds = [a + scalar_ref[first_block + a, REST + k] for k in range(PARTNERS)]

        def load(index, block, blocks):
            here = block * LANES - shift
            both = w_ref[index, :, here : here + blocks * LANES].astype(jnp.float32)
            return [both[w * MINE : (w + 1) * MINE] for w in range(WINDOWS)]

        def store(slot, block, both):
            at = pl.ds(pl.multiple_of((a * PARTNERS + slot) * MINE, 16), 2 * MINE)
            columns = slice(block * LANES - shift, (block + 1) * LANES - shift)
            cross = jnp.concatenate(both, axis=0)
            high = cross.astype(jnp.bfloat16)
            xh_ref[at, columns] = high
            xl_ref[at, columns] = (cross - high.astype(jnp.float32)).astype(jnp.bfloat16)

        for n in range(begin, end):
            taper = taper_ref[n : n + 1, :]
            first = [(x[:, :LANES] * taper, x[:, LANES:] * taper) for x in load(a, 2 * n, 2)]
            for slot in range(0, PARTNERS, 2):
                re, im = [], []
                for k in (slot, slot + 1):
                    (a_re, a_im), (c_re, c_im) = first
                    (b_re, b_im), (d_re, d_im) = [
                        (x[:, :LANES], x[:, LANES:]) for x in load(seconds[k], 2 * n, 2)
                    ]
                    re.append((a_re * b_re + a_im * b_im) + (c_re * d_re + c_im * d_im))
                    im.append((a_im * b_re - a_re * b_im) + (c_im * d_re - c_re * d_im))
                store(slot, 2 * n, re)
                store(slot, 2 * n + 1, im)
        if with_tail:
            taper = taper_ref[FULL : FULL + 1, :]
            first = [x * taper for x in load(a, TAIL, 1)]
            for slot in range(0, PARTNERS, 2):
                both = []
                for k in (slot, slot + 1):
                    second = load(seconds[k], TAIL, 1)
                    straight = first[0] * second[0] + first[1] * second[1]
                    crossed = first[0] * pltpu.roll(second[0], SIDE, 1)
                    crossed = crossed + first[1] * pltpu.roll(second[1], SIDE, 1)
                    both.append(
                        jnp.where(
                            low_side,
                            straight + pltpu.roll(straight, SIDE, 1),
                            crossed - pltpu.roll(crossed, SIDE, 1),
                        )
                    )
                store(slot, TAIL, both)
        return carry

    lax.fori_loop(0, count, one_block, 0, unroll=True)
    rows = part_columns(part)
    lagged = jnp.dot(xh_ref[...], high_ref[rows, :], preferred_element_type=jnp.float32)
    lagged += jnp.dot(xh_ref[...], low_ref[rows, :], preferred_element_type=jnp.float32)
    lagged += jnp.dot(xl_ref[...], high_ref[rows, :], preferred_element_type=jnp.float32)
    return lagged.reshape(count * PARTNERS, MINE, LAGS)


def store_lags(out_ref, first_block, count, scalar_ref, lagged):
    for i in range(count * PARTNERS):
        valid = scalar_ref[first_block + i // PARTNERS, REST + i % PARTNERS] > 0
        out_ref[first_block * PARTNERS + i] = jnp.where(valid, lagged[i], 0.0)


def inner_kernel(
    squared_ref,
    plane_ref,
    high_ref,
    low_ref,
    out_ref,
    scalar_ref,
    taper_ref,
    xh_ref,
    xl_ref,
    number_ref,
    sem,
    square_ref,
):
    for a in range(PLANE):
        number_ref[a : a + 1, :] = (
            plane_ref[a, :, TAIL * LANES :].astype(jnp.float32)[:1].astype(jnp.int32)
        )
    numbers = pltpu.make_async_copy(number_ref, scalar_ref, sem)
    numbers.start()
    square_ref[...] = jnp.zeros_like(square_ref)
    square_ref[:PER, :RADIX] = squared_ref[...]
    taper_columns(square_ref, taper_ref)
    numbers.wait()
    lagged = cross_and_lag(
        0, INNER, (0, FULL, True), taper_ref, plane_ref, high_ref, low_ref, scalar_ref, xh_ref, xl_ref
    )
    store_lags(out_ref, 0, INNER, scalar_ref, lagged)


def halo_kernel(
    part,
    scalar_ref,
    taper_ref,
    plane_ref,
    halo_ref,
    high_ref,
    low_ref,
    before_ref,
    out_ref,
    xh_ref,
    xl_ref,
    w_ref,
):
    for i in range(REACH):
        w_ref[i] = plane_ref[INNER + i, :, part_columns(part)]
        w_ref[REACH + i] = halo_ref[i]
    lagged = cross_and_lag(
        INNER, REACH, part, taper_ref, w_ref, high_ref, low_ref, scalar_ref, xh_ref, xl_ref
    )
    if before_ref is None:
        out_ref[...] = lagged
    else:
        store_lags(out_ref, INNER, REACH, scalar_ref, lagged + before_ref[...])


def correlated_call(body, name, scalars, operands, out_blocks, count, width, aliases, extra):
    rows = count * PARTNERS * MINE
    vmem = pl.BlockSpec(memory_space=pltpu.VMEM)
    smem = pl.BlockSpec(memory_space=pltpu.SMEM)
    out_specs = [vmem]
    out_shape = [pltpu.VMEM((out_blocks * PARTNERS, MINE, LAGS), jnp.float32)]
    operands = [in_vmem(operand) for operand in operands]
    in_specs = [vmem] * len(operands)
    if scalars is None:
        out_specs += [smem, vmem]
        out_shape.append(pltpu.SMEM((PLANE, LANES), jnp.int32))
        out_shape.append(pltpu.VMEM((RADIX, LANES), jnp.float32))
    else:
        in_specs.insert(0, smem)
        operands.insert(0, pltpu.with_memory_space_constraint(scalars, pltpu.SMEM))
    return pl.pallas_call(
        body,
        in_specs=in_specs,
        out_specs=out_specs,
        out_shape=out_shape,
        scratch_shapes=[
            pltpu.VMEM((rows, width), jnp.bfloat16),
            pltpu.VMEM((rows, width), jnp.bfloat16),
        ]
        + extra,
        input_output_aliases=aliases,
        compiler_params=pltpu.CompilerParams(vmem_limit_bytes=10 << 20),
        cost_estimate=pl.CostEstimate(
            flops=6 * rows * width * LAGS, bytes_accessed=4 << 20, transcendentals=0
        ),
        name=name,
    )(*operands)


def per_device(records, taper, pairs):
    theirs, sums = spectra(records[0])
    got = lax.ppermute(theirs, "tm", [(0, 1), (1, 0)])
    mine, squared = own_half(pairs, taper, sums)
    send = mine.at[:, MINE:].set(got.reshape(PLANE, MINE, WIDE))
    plane = lax.all_to_all(send, "col", 0, 0, tiled=True)
    count = lax.axis_size("row")
    down = [(z, z - 1) for z in range(1, count)]
    head, squared = lax.optimization_barrier((plane_head(plane, HALO_PARTS[0]), squared))
    halos = [lax.ppermute(head, "row", down)]
    squared = squared.reshape(PER, RADIX)
    high, low = (jnp.asarray(table) for table in lag_tables())
    widths = [part_width(part) for part in HALO_PARTS]
    w = [[pltpu.VMEM((2 * REACH, 2 * MINE, width), jnp.bfloat16)] for width in widths]
    lagged, scalars, columns = correlated_call(
        inner_kernel,
        "correlate_inner",
        None,
        [squared, plane, high, low],
        PLANE,
        INNER,
        WIDE,
        {},
        [
            pltpu.VMEM((PLANE, LANES), jnp.int32),
            pltpu.SemaphoreType.DMA(()),
            pltpu.VMEM((LANES, LANES), jnp.float32),
        ],
    )

    later, scalars = lax.optimization_barrier((plane, scalars))
    halos.append(lax.ppermute(plane_head(later, HALO_PARTS[1]), "row", down))

    def first(*refs):
        halo_kernel(HALO_PARTS[0], *refs[:6], None, *refs[6:])

    def second(*refs):
        halo_kernel(HALO_PARTS[1], *refs[:7], *refs[8:])

    (partial,) = correlated_call(
        first,
        "correlate_halo_first",
        scalars,
        [columns, plane, halos[0], high, low],
        REACH,
        REACH,
        widths[0],
        {},
        w[0],
    )
    (lagged,) = correlated_call(
        second,
        "correlate_halo_second",
        scalars,
        [columns, plane, halos[1], high, low, partial, lagged],
        PLANE,
        REACH,
        widths[1],
        {7: 0},
        w[1],
    )
    lagged = lagged.reshape(PLANE, PARTNERS, MINE, LAGS)
    back = lax.all_to_all(lagged.astype(jnp.bfloat16), "col", 0, 0, tiled=True).astype(jnp.float32)
    return back.transpose(1, 0, 2, 3).reshape(1, PARTNERS, HALF, LAGS)


def solution(mesh):
    return jax.shard_map(
        per_device,
        mesh=mesh,
        in_specs=(P("tm", ("row", "col"), None), P(), P(("row", "col"), None)),
        out_specs=P(("row", "col"), None, "tm", None),
        check_vma=False,
    )
```

```python
import math

import jax
import jax.numpy as jnp
import ml_dtypes
import numpy as np
from jax import lax
from jax.experimental import pallas as pl
from jax.experimental.pallas import tpu as pltpu
from jax.sharding import PartitionSpec as P

SAMPLES = 7680
FREQS = 1200
FIRST_BIN = 32
LAGS = 256
SMOOTH = 4
PARTNERS = 4
REACH = 7
BLOCK = 256
WINDOWS = 2
WATER = 0.3
RESCALE = 2.0

RADIX = 10
PART = SAMPLES // RADIX
HALF = BLOCK // 2
PER = FREQS // RADIX
LANES = 128
SPARE = LANES - PER
FULL = RADIX - 1
REST = PER - FULL * SPARE
TAIL = 2 * FULL
SIDE = LANES // 2
WIDE = (TAIL + 1) * LANES
HALO_PARTS = ((3, FULL, True), (0, 3, False))
BASE = 3
TURNS = 4
ORDER = (0, 1, -1, 2, -2, 3, -3, 4, -4, 5)
PRODUCTS = 1 + 2 * TURNS
FINE = 512
PLANE = 16
INNER = PLANE - REACH
MINE = HALF // PLANE
CHUNKS = 4


def lowest_lane(residue):
    return 0 if residue + RADIX * BASE >= FIRST_BIN else 1


def place_in_band(residue):
    return residue + SMOOTH


def turn(phase):
    angle = phase % SAMPLES * (2.0 * math.pi / SAMPLES)
    return np.cos(angle), -np.sin(angle)


def dft_tables():
    def table(residue):
        steps = np.arange(PART)[:, None] * (residue + RADIX * (BASE + np.arange(LANES)))[None, :]
        return np.concatenate(turn(steps), axis=1).astype(np.float32)

    base, last = table(0), table(ORDER[-1])
    high = base.astype(ml_dtypes.bfloat16)
    low = (base - high.astype(np.float32))[:FINE].astype(ml_dtypes.bfloat16)
    return np.concatenate([high, last.astype(ml_dtypes.bfloat16), low])


def twiddles():
    steps = np.arange(1, TURNS + 1)[:, None] * np.arange(PART)[None, :]
    return np.stack(turn(steps), axis=1).reshape(-1, PART).astype(np.float32)


def lag_tables():
    lag_steps = np.arange(LAGS) - LAGS // 2 + SAMPLES
    factor = RESCALE / math.sqrt(FREQS * WINDOWS)
    rows = []
    for residue in ORDER:
        bins = residue + RADIX * (BASE + lowest_lane(residue) + np.arange(PER))
        rows.append(np.stack(turn(bins[:, None] * lag_steps[None, :])))
    blocks = []
    for place, residue in enumerate(ORDER[:FULL]):
        spare = rows[FULL][:, place * SPARE : (place + 1) * SPARE]
        block = np.concatenate([rows[place], spare], axis=1)
        blocks.append(np.roll(block, lowest_lane(residue), axis=1).reshape(-1, LAGS))
    tail = np.zeros((2, SIDE, LAGS))
    tail[:, :REST] = rows[FULL][:, FULL * SPARE :]
    table = np.concatenate(blocks + [tail.reshape(LANES, LAGS)]) * factor
    table = table.astype(np.float32)
    high = table.astype(ml_dtypes.bfloat16)
    low = (table - high.astype(np.float32)).astype(ml_dtypes.bfloat16)
    return high, low


def taper_columns(square_ref, taper_ref):
    rows = jnp.transpose(square_ref[...])
    lane = lax.broadcasted_iota(jnp.int32, (1, LANES), 1)
    spare = [lane >= PER, (lane > PER) | (lane < 1)]

    def row(residue):
        index = residue + RADIX * (BASE + lowest_lane(residue)) - FIRST_BIN
        return rows[index : index + 1, :]

    last = row(ORDER[FULL])
    for place, residue in enumerate(ORDER[:FULL]):
        low = lowest_lane(residue)
        own = pltpu.roll(row(residue), 1, 1) if low else row(residue)
        moved = pltpu.roll(last, PER + low - place * SPARE, 1)
        taper_ref[place : place + 1, :] = jnp.where(spare[low], moved, own)
    moved = [pltpu.roll(last, LANES + side * SIDE - FULL * SPARE, 1) for side in range(2)]
    taper_ref[FULL : FULL + 1, :] = jnp.where(lane < SIDE, moved[0], moved[1])


def five_point(x):
    cos = [math.cos(2.0 * math.pi * k / 5) for k in (1, 2)]
    sin = [math.sin(2.0 * math.pi * k / 5) for k in (1, 2)]
    near, far = x[1] + x[4], x[2] + x[3]
    near_gap, far_gap = x[1] - x[4], x[2] - x[3]
    return (
        x[0] + near + far,
        x[0] + cos[0] * near + cos[1] * far,
        sin[0] * near_gap + sin[1] * far_gap,
        x[0] + cos[1] * near + cos[0] * far,
        sin[1] * near_gap - sin[0] * far_gap,
    )


def dft_kernel(
    x_hbm,
    table_hbm,
    turn_hbm,
    theirs_ref,
    sums_ref,
    x_ref,
    table_ref,
    turn_ref,
    even_ref,
    odd_ref,
    last_ref,
    x_sems,
    t_sems,
):
    core = lax.axis_index("tm")
    size = BLOCK // CHUNKS
    y_refs = (even_ref, odd_ref)

    def rows_of(c):
        half, rest = c * size // HALF, c * size % HALF
        side = 1 - core if half == 0 else core
        return pl.ds(pl.multiple_of(side * HALF + rest, size), size)

    x_copies = [
        pltpu.make_async_copy(
            x_hbm.at[rows_of(c)], x_ref.at[pl.ds(c * size, size)], x_sems.at[c]
        )
        for c in range(CHUNKS)
    ]
    turn_copy = pltpu.make_async_copy(turn_hbm, turn_ref, t_sems.at[0])
    table_copy = pltpu.make_async_copy(table_hbm, table_ref, t_sems.at[1])
    for copy in [turn_copy] + x_copies + [table_copy]:
        copy.start()

    def split(c, i):
        y_ref = y_refs[c % 2]
        at = slice(c * size + i * 16, c * size + (i + 1) * 16)
        for lane in range(0, PART, LANES):
            x = [
                x_ref[at, n * PART + lane : n * PART + lane + LANES].astype(jnp.float32)
                for n in range(RADIX)
            ]
            even = five_point([x[n] + x[n + 5] for n in range(5)])
            odd = five_point([x[n] - x[n + 5] if n % 2 == 0 else x[n + 5] - x[n] for n in range(5)])
            sums = [(odd[3], -odd[4]), even[1:3], (odd[1], -odd[2]), even[3:5]]
            parts = [even[0]]
            for r, (real, imag) in enumerate(sums):
                cos = turn_ref[2 * r : 2 * r + 1, lane : lane + LANES]
                sin = turn_ref[2 * r + 1 : 2 * r + 2, lane : lane + LANES]
                parts += [real * cos + imag * sin, real * sin - imag * cos]
            last_ref[at, lane : lane + LANES] = odd[0].astype(jnp.bfloat16)
            for n, part in enumerate(parts):
                y_ref[n * size + i * 16 : n * size + (i + 1) * 16, lane : lane + LANES] = part.astype(
                    jnp.bfloat16
                )

    def multiply(c):
        y_ref = y_refs[c % 2]
        product = jnp.dot(y_ref[...], table_ref[:PART], preferred_element_type=jnp.float32)
        for n in range(PRODUCTS):
            sums_ref[n * BLOCK + c * size : n * BLOCK + (c + 1) * size] = product[
                n * size : (n + 1) * size
            ]
        product = jnp.dot(
            y_ref[size:, :FINE], table_ref[2 * PART :], preferred_element_type=jnp.float32
        )
        for n in range(1, PRODUCTS):
            at = slice(n * BLOCK + c * size, n * BLOCK + (c + 1) * size)
            sums_ref[at] = sums_ref[at] + product[(n - 1) * size : n * size]

    def multiply_last(half):
        at = slice(half * HALF, (half + 1) * HALF)
        sums_ref[PRODUCTS * BLOCK + half * HALF : PRODUCTS * BLOCK + (half + 1) * HALF] = jnp.dot(
            last_ref[at], table_ref[PART : 2 * PART], preferred_element_type=jnp.float32
        )

    turn_copy.wait()
    for c in range(CHUNKS):
        x_copies[c].wait()
        if c == 1:
            table_copy.wait()
        for i in range(size // 16):
            split(c, i)
        if c > 0:
            multiply(c - 1)
        if c == CHUNKS // 2:
            multiply_last(0)
    for i in range(HALF // 16):
        parts = [white_rows(sums_ref, i * 16 + j * MINE) for j in range(2)]
        for n in range(TAIL + 1):
            theirs_ref[i * 16 : (i + 1) * 16, n * LANES : (n + 1) * LANES] = jnp.concatenate(
                [parts[0][n], parts[1][n]], axis=0
            ).astype(jnp.bfloat16)
    multiply(CHUNKS - 1)
    multiply_last(1)


def spectrum_parts(sums_ref, row):
    def load(index):
        first = index * BLOCK + row
        at = pl.ds(first if isinstance(first, int) else pl.multiple_of(first, MINE), MINE)
        return sums_ref[at, :LANES], sums_ref[at, LANES:]

    parts = [load(0)]
    for r in range(TURNS):
        (real_cos, real_sin), (imag_cos, imag_sin) = load(1 + 2 * r), load(2 + 2 * r)
        parts.append((real_cos - imag_sin, real_sin + imag_cos))
        parts.append((real_cos + imag_sin, real_sin - imag_cos))
    return parts + [load(PRODUCTS)]


def white_rows(sums_ref, row):
    lane = lax.broadcasted_iota(jnp.int32, (MINE, LANES), 1)
    spare = [lane >= PER, (lane > PER) | (lane < 1)]
    band = [None] * RADIX
    for residue, (re, im) in zip(ORDER, spectrum_parts(sums_ref, row)):
        square = re * re + im * im
        amplitude = square * lax.rsqrt(jnp.maximum(square, 1e-30))
        band[place_in_band(residue)] = jnp.where(spare[lowest_lane(residue)], 0.0, amplitude)
    total = band[0]
    for amplitude in band[1:]:
        total = total + amplitude
    floor = WATER / FREQS * jnp.sum(total, axis=1, keepdims=True) + 1e-05
    line = [pltpu.roll(a, 1, 1) for a in band[RADIX - SMOOTH :]]
    line = line + band + [pltpu.roll(a, LANES - 1, 1) for a in band[:SMOOTH]]
    two = [line[i] + line[i + 1] for i in range(len(line) - 1)]
    four = [two[i] + two[i + 2] for i in range(len(two) - 2)]
    out = []
    for residue, (re, im) in zip(ORDER, spectrum_parts(sums_ref, row)):
        i = place_in_band(residue)
        smoothed = (four[i] + four[i + 4] + line[i + 8]) * (1.0 / (2 * SMOOTH + 1))
        level = smoothed + floor
        scale = pl.reciprocal(level, approx=True)
        scale = scale * (2.0 - level * scale)
        out += [re * scale, im * scale]
    last = out[TAIL:]
    for place, residue in enumerate(ORDER[:FULL]):
        low = lowest_lane(residue)
        for side in range(2):
            moved = pltpu.roll(last[side], PER + low - place * SPARE, 1)
            here = 2 * place + side
            out[here] = jnp.where(spare[low], moved, out[here])
    moved = [
        pltpu.roll(last[side], LANES + side * SIDE - FULL * SPARE, 1) for side in range(2)
    ]
    return out[:TAIL] + [jnp.where(lane < SIDE, moved[0], moved[1])]


def own_kernel(pairs_ref, taper_ref, sums_ref, mine_ref, squared_ref):
    squared_ref[...] = taper_ref[...] * taper_ref[...]
    block = lax.axis_index("row") * PLANE + lax.axis_index("col")
    lane = lax.broadcasted_iota(jnp.int32, (MINE, LANES), 1)
    offsets = jnp.zeros((MINE, LANES), jnp.float32)
    for k in range(PARTNERS):
        partner = pairs_ref[0, k]
        offset = jnp.where(partner < 0, 0, partner - block).astype(jnp.float32)
        offsets = jnp.where(lane == REST + k, offset, offsets)

    def rows(j, carry):
        parts = white_rows(sums_ref, HALF + j * MINE)
        parts[TAIL] = jnp.where((lane >= REST) & (lane < SIDE), offsets, parts[TAIL])
        for n, part in enumerate(parts):
            mine_ref[j, :, n * LANES : (n + 1) * LANES] = jnp.concatenate(
                [part, part], axis=0
            ).astype(jnp.bfloat16)
        return carry

    lax.fori_loop(0, PLANE, rows, 0, unroll=4)


def in_vmem(array):
    return pltpu.with_memory_space_constraint(array, pltpu.VMEM)


def spectra(series):
    hbm = pl.BlockSpec(memory_space=pltpu.HBM)
    vmem = pl.BlockSpec(memory_space=pltpu.VMEM)
    operands = [
        pltpu.with_memory_space_constraint(a, pltpu.HBM)
        for a in (series, jnp.asarray(dft_tables()), jnp.asarray(twiddles()))
    ]
    return pl.pallas_call(
        dft_kernel,
        in_specs=[hbm, hbm, hbm],
        out_specs=[vmem, vmem],
        out_shape=[
            pltpu.VMEM((HALF, WIDE), jnp.bfloat16),
            pltpu.VMEM(((PRODUCTS + 1) * BLOCK, 2 * LANES), jnp.float32),
        ],
        scratch_shapes=[
            pltpu.VMEM((BLOCK, SAMPLES), jnp.bfloat16),
            pltpu.VMEM((2 * PART + FINE, 2 * LANES), jnp.bfloat16),
            pltpu.VMEM((2 * TURNS, PART), jnp.float32),
            pltpu.VMEM((PRODUCTS * BLOCK // CHUNKS, PART), jnp.bfloat16),
            pltpu.VMEM((PRODUCTS * BLOCK // CHUNKS, PART), jnp.bfloat16),
            pltpu.VMEM((BLOCK, PART), jnp.bfloat16),
            pltpu.SemaphoreType.DMA((CHUNKS,)),
            pltpu.SemaphoreType.DMA((2,)),
        ],
        compiler_params=pltpu.CompilerParams(vmem_limit_bytes=16 << 20),
        name="dft_whiten",
    )(*operands)


def own_half(pairs, taper, sums):
    vmem = pl.BlockSpec(memory_space=pltpu.VMEM)
    return pl.pallas_call(
        own_kernel,
        in_specs=[pl.BlockSpec(memory_space=pltpu.SMEM), vmem, vmem],
        out_specs=[vmem, vmem],
        out_shape=[
            pltpu.VMEM((PLANE, 2 * MINE, WIDE), jnp.bfloat16),
            pltpu.VMEM((FREQS,), jnp.float32),
        ],
        compiler_params=pltpu.CompilerParams(vmem_limit_bytes=4 << 20),
        cost_estimate=pl.CostEstimate(
            flops=40 * HALF * WIDE, bytes_accessed=5 << 20, transcendentals=0
        ),
        name="whiten_own",
    )(pairs, taper, in_vmem(sums))


def part_columns(part):
    begin, end, tail = part
    return slice(2 * begin * LANES, (2 * end + tail) * LANES)


def part_width(part):
    columns = part_columns(part)
    return columns.stop - columns.start


def plane_head(plane, part):
    vmem = pl.BlockSpec(memory_space=pltpu.VMEM)

    def body(plane_ref, head_ref):
        for i in range(REACH):
            head_ref[i] = plane_ref[i, :, part_columns(part)]

    return pl.pallas_call(
        body,
        in_specs=[vmem],
        out_specs=vmem,
        out_shape=pltpu.VMEM((REACH, 2 * MINE, part_width(part)), jnp.bfloat16),
        compiler_params=pltpu.CompilerParams(vmem_limit_bytes=2 << 20),
        name="plane_head",
    )(in_vmem(plane))


def cross_and_lag(
    first_block, count, part, taper_ref, w_ref, high_ref, low_ref, scalar_ref, xh_ref, xl_ref
):
    begin, end, with_tail = part
    shift = 2 * begin * LANES
    low_side = lax.broadcasted_iota(jnp.int32, (MINE, LANES), 1) < SIDE

    def one_block(a, carry):
        seconds = [a + scalar_ref[first_block + a, REST + k] for k in range(PARTNERS)]

        def load(index, block, blocks):
            here = block * LANES - shift
            both = w_ref[index, :, here : here + blocks * LANES].astype(jnp.float32)
            return [both[w * MINE : (w + 1) * MINE] for w in range(WINDOWS)]

        def store(slot, block, both):
            at = pl.ds(pl.multiple_of((a * PARTNERS + slot) * MINE, 16), 2 * MINE)
            columns = slice(block * LANES - shift, (block + 1) * LANES - shift)
            cross = jnp.concatenate(both, axis=0)
            high = cross.astype(jnp.bfloat16)
            xh_ref[at, columns] = high
            xl_ref[at, columns] = (cross - high.astype(jnp.float32)).astype(jnp.bfloat16)

        for n in range(begin, end):
            taper = taper_ref[n : n + 1, :]
            first = [(x[:, :LANES] * taper, x[:, LANES:] * taper) for x in load(a, 2 * n, 2)]
            for slot in range(0, PARTNERS, 2):
                re, im = [], []
                for k in (slot, slot + 1):
                    (a_re, a_im), (c_re, c_im) = first
                    (b_re, b_im), (d_re, d_im) = [
                        (x[:, :LANES], x[:, LANES:]) for x in load(seconds[k], 2 * n, 2)
                    ]
                    re.append((a_re * b_re + a_im * b_im) + (c_re * d_re + c_im * d_im))
                    im.append((a_im * b_re - a_re * b_im) + (c_im * d_re - c_re * d_im))
                store(slot, 2 * n, re)
                store(slot, 2 * n + 1, im)
        if with_tail:
            taper = taper_ref[FULL : FULL + 1, :]
            first = [x * taper for x in load(a, TAIL, 1)]
            for slot in range(0, PARTNERS, 2):
                both = []
                for k in (slot, slot + 1):
                    second = load(seconds[k], TAIL, 1)
                    straight = first[0] * second[0] + first[1] * second[1]
                    crossed = first[0] * pltpu.roll(second[0], SIDE, 1)
                    crossed = crossed + first[1] * pltpu.roll(second[1], SIDE, 1)
                    both.append(
                        jnp.where(
                            low_side,
                            straight + pltpu.roll(straight, SIDE, 1),
                            crossed - pltpu.roll(crossed, SIDE, 1),
                        )
                    )
                store(slot, TAIL, both)
        return carry

    lax.fori_loop(0, count, one_block, 0, unroll=True)
    rows = part_columns(part)
    lagged = jnp.dot(xh_ref[...], high_ref[rows, :], preferred_element_type=jnp.float32)
    lagged += jnp.dot(xh_ref[...], low_ref[rows, :], preferred_element_type=jnp.float32)
    lagged += jnp.dot(xl_ref[...], high_ref[rows, :], preferred_element_type=jnp.float32)
    return lagged.reshape(count * PARTNERS, MINE, LAGS)


def store_lags(out_ref, first_block, count, scalar_ref, lagged):
    for i in range(count * PARTNERS):
        valid = scalar_ref[first_block + i // PARTNERS, REST + i % PARTNERS] > 0
        out_ref[first_block * PARTNERS + i] = jnp.where(valid, lagged[i], 0.0)


def inner_kernel(
    squared_ref,
    plane_ref,
    high_ref,
    low_ref,
    out_ref,
    scalar_ref,
    taper_ref,
    xh_ref,
    xl_ref,
    number_ref,
    sem,
    square_ref,
):
    for a in range(PLANE):
        number_ref[a : a + 1, :] = (
            plane_ref[a, :, TAIL * LANES :].astype(jnp.float32)[:1].astype(jnp.int32)
        )
    numbers = pltpu.make_async_copy(number_ref, scalar_ref, sem)
    numbers.start()
    square_ref[...] = jnp.zeros_like(square_ref)
    square_ref[:PER, :RADIX] = squared_ref[...]
    taper_columns(square_ref, taper_ref)
    numbers.wait()
    lagged = cross_and_lag(
        0, INNER, (0, FULL, True), taper_ref, plane_ref, high_ref, low_ref, scalar_ref, xh_ref, xl_ref
    )
    store_lags(out_ref, 0, INNER, scalar_ref, lagged)


def halo_kernel(
    part,
    scalar_ref,
    taper_ref,
    plane_ref,
    halo_ref,
    high_ref,
    low_ref,
    before_ref,
    out_ref,
    xh_ref,
    xl_ref,
    w_ref,
):
    for i in range(REACH):
        w_ref[i] = plane_ref[INNER + i, :, part_columns(part)]
        w_ref[REACH + i] = halo_ref[i]
    lagged = cross_and_lag(
        INNER, REACH, part, taper_ref, w_ref, high_ref, low_ref, scalar_ref, xh_ref, xl_ref
    )
    if before_ref is None:
        out_ref[...] = lagged
    else:
        store_lags(out_ref, INNER, REACH, scalar_ref, lagged + before_ref[...])


def correlated_call(body, name, scalars, operands, out_blocks, count, width, aliases, extra):
    rows = count * PARTNERS * MINE
    vmem = pl.BlockSpec(memory_space=pltpu.VMEM)
    smem = pl.BlockSpec(memory_space=pltpu.SMEM)
    out_specs = [vmem]
    out_shape = [pltpu.VMEM((out_blocks * PARTNERS, MINE, LAGS), jnp.float32)]
    operands = [in_vmem(operand) for operand in operands]
    in_specs = [vmem] * len(operands)
    if scalars is None:
        out_specs += [smem, vmem]
        out_shape.append(pltpu.SMEM((PLANE, LANES), jnp.int32))
        out_shape.append(pltpu.VMEM((RADIX, LANES), jnp.float32))
    else:
        in_specs.insert(0, smem)
        operands.insert(0, pltpu.with_memory_space_constraint(scalars, pltpu.SMEM))
    return pl.pallas_call(
        body,
        in_specs=in_specs,
        out_specs=out_specs,
        out_shape=out_shape,
        scratch_shapes=[
            pltpu.VMEM((rows, width), jnp.bfloat16),
            pltpu.VMEM((rows, width), jnp.bfloat16),
        ]
        + extra,
        input_output_aliases=aliases,
        compiler_params=pltpu.CompilerParams(vmem_limit_bytes=10 << 20),
        cost_estimate=pl.CostEstimate(
            flops=6 * rows * width * LAGS, bytes_accessed=4 << 20, transcendentals=0
        ),
        name=name,
    )(*operands)


def per_device(records, taper, pairs):
    theirs, sums = spectra(records[0])
    got = lax.ppermute(theirs, "tm", [(0, 1), (1, 0)])
    mine, squared = own_half(pairs, taper, sums)
    send = mine.at[:, MINE:].set(got.reshape(PLANE, MINE, WIDE))
    plane = lax.all_to_all(send, "col", 0, 0, tiled=True)
    count = lax.axis_size("row")
    down = [(z, z - 1) for z in range(1, count)]
    head, squared = lax.optimization_barrier((plane_head(plane, HALO_PARTS[0]), squared))
    halos = [lax.ppermute(head, "row", down)]
    squared = squared.reshape(PER, RADIX)
    high, low = (jnp.asarray(table) for table in lag_tables())
    widths = [part_width(part) for part in HALO_PARTS]
    w = [[pltpu.VMEM((2 * REACH, 2 * MINE, width), jnp.bfloat16)] for width in widths]
    lagged, scalars, columns = correlated_call(
        inner_kernel,
        "correlate_inner",
        None,
        [squared, plane, high, low],
        PLANE,
        INNER,
        WIDE,
        {},
        [
            pltpu.VMEM((PLANE, LANES), jnp.int32),
            pltpu.SemaphoreType.DMA(()),
            pltpu.VMEM((LANES, LANES), jnp.float32),
        ],
    )

    later, scalars = lax.optimization_barrier((plane, scalars))
    halos.append(lax.ppermute(plane_head(later, HALO_PARTS[1]), "row", down))

    def first(*refs):
        halo_kernel(HALO_PARTS[0], *refs[:6], None, *refs[6:])

    def second(*refs):
        halo_kernel(HALO_PARTS[1], *refs[:7], *refs[8:])

    (partial,) = correlated_call(
        first,
        "correlate_halo_first",
        scalars,
        [columns, plane, halos[0], high, low],
        REACH,
        REACH,
        widths[0],
        {},
        w[0],
    )
    (lagged,) = correlated_call(
        second,
        "correlate_halo_second",
        scalars,
        [columns, plane, halos[1], high, low, partial, lagged],
        PLANE,
        REACH,
        widths[1],
        {7: 0},
        w[1],
    )
    lagged = lagged.reshape(PLANE, PARTNERS, MINE, LAGS)
    back = lax.all_to_all(lagged.astype(jnp.bfloat16), "col", 0, 0, tiled=True).astype(jnp.float32)
    return back.transpose(1, 0, 2, 3).reshape(1, PARTNERS, HALF, LAGS)


def solution(mesh):
    return jax.shard_map(
        per_device,
        mesh=mesh,
        in_specs=(P("tm", ("row", "col"), None), P(), P(("row", "col"), None)),
        out_specs=P(("row", "col"), None, "tm", None),
        check_vma=False,
    )
```
